512 devices in a mesh: row: 32 (over y, x, core), col: 16 (over z).
Axes of the slice: x: 4, y: 4, z: 16, core: 2. Of those that a mesh axis runs over, the one named last changes fastest.
Arguments:
- hidden_in: bfloat16 [512, 8192], P('col', 'row'), may hold values from -6 to 6
- norm_mixer: float32 [8192], P('row'), may hold values from 0.5 to 1.5
- mixer_in: bfloat16 [8192, 4, 32, 128], P('row', None, 'col'), may hold values from -0.0625 to 0.0625
- bc_proj: bfloat16 [8192, 4, 512], P('row', None, 'col'), may hold values from -0.0625 to 0.0625
- dt_proj: bfloat16 [8192, 4, 32], P('row', None, 'col'), may hold values from -0.0625 to 0.0625
- dt_bias: float32 [4, 32], P(None, 'col'), may hold values from -5 to -1
- a_log: float32 [4, 32], P(None, 'col'), may hold values from -4 to 1
- skip_d: float32 [4, 32], P(None, 'col'), may hold values from 0.5 to 1.5
- conv_x: bfloat16 [4, 4, 2048], P(None, None, 'col'), may hold values from -3 to 3
- conv_bc: bfloat16 [4, 4, 512], replicated, may hold values from -3 to 3
- x_cache: bfloat16 [32, 4, 3, 2048], P('row', None, None, 'col'), may hold values from -6 to 6
- bc_cache: bfloat16 [32, 4, 3, 512], P('row'), may hold values from -6 to 6
- ssm_cache: float32 [32, 4, 32, 64, 256], P('row', None, 'col'), may hold values from -2 to 2
- slot_ids: int32 [8], replicated, may hold values from 0 to 3, as said below
- parents: int32 [8, 64], replicated, may hold values from -1 to 62, as said below
- ancestors: int32 [8, 64, 64], replicated, may hold values from 0 to 1, as said below
- norm_gated: float32 [4, 2048], P(None, 'col'), may hold values from 0.5 to 1.5
- out_proj: bfloat16 [4, 2048, 8192], P(None, 'col', 'row'), may hold values from -0.0625 to 0.0625
- norm_ffn: float32 [8192], P('row'), may hold values from 0.5 to 1.5
- ffn_up: bfloat16 [8192, 32768], P('row', 'col'), may hold values from -0.0625 to 0.0625
- ffn_down: bfloat16 [32768, 8192], P('col', 'row'), may hold values from -0.03125 to 0.03125
Outputs:
- hidden_out: bfloat16 [512, 8192], P('col', 'row')
The draws below stay inside these ranges and needn't reach their ends.
Inputs may be any that keep to these rules, and one draw needn't show every extreme that they name: `parents`: node 0 of every tree is its root, with parent -1; every other node i has its parent among nodes max(i - 4, 0) to i - 1. ancestors[q, i, j] is 1 exactly when node j is node i or an ancestor of node i in request q's tree under parents, else 0. `slot_ids`: the first 4 requests hold 4 different slots (so one of them holds slot 3); the other requests may hold any slot.
All inputs are finite; a program needn't handle non-finite values.
Results may differ from the reference program's by a relative error of at most 0.04.
Values may be sent and summed in bfloat16 or wider, within the bound.
No kernel may reach another device: no remote copies, remote signals or barrier semaphores. Data moves between devices by JAX's collectives and lax.ppermute only.
A program may use at most 64 MiB of HBM per device.

```python
import jax
import jax.numpy as jnp
from jax import lax

D = 8192
H = 128
P_SIZE = 64
N = 256
G = 4
FF = 32768
KC = 4
NODES = 64
SLOTS = 4
REQ = 8
TOKENS = 512
N_ROW = 32
N_COL = 16


def linked_parents(key):
    jumps = jax.random.randint(key, (REQ, NODES), 1, 5)
    positions = jnp.arange(NODES, dtype=jnp.int32)
    linked = jnp.maximum(positions[None, :] - jumps, 0)
    return jnp.where(positions[None, :] == 0, -1, linked).astype(jnp.int32)


def draw_parents(key, part):
    return linked_parents(key)


def draw_ancestors(key, part):
    linked = linked_parents(key)
    positions = jnp.arange(NODES, dtype=jnp.int32)

    def add_node(node, table):
        parent_ids = lax.dynamic_index_in_dim(linked, node, 1, keepdims=False)
        parent_pick = (positions[None, :] == parent_ids[:, None]).astype(jnp.int32)
        inherited = jnp.sum(parent_pick[:, :, None] * table, axis=1)
        new_row = inherited + (positions[None, :] == node).astype(jnp.int32)
        return lax.dynamic_update_index_in_dim(table, new_row, node, 1)
    table = jnp.zeros((REQ, NODES, NODES), jnp.int32)
    return lax.fori_loop(0, NODES, add_node, table)


def draw_slot_ids(key, part):
    key = jax.random.fold_in(key, 7)
    order_key, rest_key, place_key = jax.random.split(key, 3)
    early = min(REQ, SLOTS)
    others = jax.random.permutation(order_key, SLOTS - 1).astype(jnp.int32)
    top_place = jax.random.randint(place_key, (), 0, early).astype(jnp.int32)
    rest = jax.random.randint(rest_key, (REQ,), 0, SLOTS).astype(jnp.int32)
    positions = jnp.arange(REQ, dtype=jnp.int32)
    source = jnp.where(positions < top_place, positions, positions - 1)
    other_pick = (source[:, None] == jnp.arange(SLOTS - 1, dtype=jnp.int32)[None, :]).astype(jnp.int32)
    from_order = jnp.sum(other_pick * others[None, :], axis=1)
    first_part = jnp.where(positions == top_place, SLOTS - 1, from_order)
    return jnp.where(positions < early, first_part, rest).astype(jnp.int32)


def block_scale(own_key, extent, cuts, low, largest):
    gain, own = 1.0, jax.random.fold_in(own_key, 6)
    for position, shards_of in cuts:
        steps = jnp.exp(jax.random.uniform(jax.random.fold_in(own, position), (shards_of,), jnp.float32, low / len(cuts), largest / len(cuts)))
        gain = gain * jnp.repeat(steps, extent[position] // shards_of).reshape([-1 if axis == position else 1 for axis in range(len(extent))])
    return gain


def scatter_about(key, dims, scale, limit, shards=(), kind=jnp.bfloat16):
    factor_of = block_scale(key, dims, shards, -0.22, 0.18) if shards else 1.0
    array = jax.random.normal(key, dims, jnp.float32) * scale * factor_of
    return jnp.minimum(jnp.maximum(array, -limit), limit).astype(kind)


def setup_inputs(seed: int = 0) -> dict:
    key_list = jax.random.split(jax.random.key(seed), 22)
    return {
        "hidden_in": scatter_about(key_list[0], (TOKENS, D), 1.0, 6.0, ((0, 16), (1, 32))),
        "norm_mixer": jnp.clip(1.0 + 0.1 * jax.random.normal(key_list[1], (D,), jnp.float32), 0.5, 1.5),
        "mixer_in": scatter_about(key_list[2], (D, G, H // G, 2 * P_SIZE), D ** -0.5, 0.0625, ((0, 32), (2, 16))),
        "bc_proj": scatter_about(key_list[3], (D, G, 2 * N), D ** -0.5, 0.0625, ((0, 32), (2, 16))),
        "dt_proj": scatter_about(key_list[4], (D, G, H // G), D ** -0.5, 0.0625, ((0, 32), (2, 16))),
        "dt_bias": jnp.clip(-5.0 + 4.0 * jax.random.uniform(key_list[5], (G, H // G), jnp.float32) ** block_scale(key_list[5], (G, H // G), ((1, 16),), -0.2, 0.2), -5.0, -1.0),
        "a_log": jnp.clip(-4.0 + 5.0 * jax.random.uniform(key_list[6], (G, H // G), jnp.float32) ** block_scale(key_list[6], (G, H // G), ((1, 16),), -0.2, 0.2), -4.0, 1.0),
        "skip_d": jnp.clip(0.5 + 1.0 * jax.random.uniform(key_list[7], (G, H // G), jnp.float32) ** block_scale(key_list[7], (G, H // G), ((1, 16),), -0.2, 0.2), 0.5, 1.5),
        "conv_x": scatter_about(key_list[8], (KC, G, H // G * P_SIZE), KC ** -0.5, 3.0, ((2, 16),)),
        "conv_bc": scatter_about(key_list[9], (KC, G, 2 * N), KC ** -0.5, 3.0),
        "x_cache": scatter_about(key_list[10], (REQ * G, SLOTS, KC - 1, H // G * P_SIZE), 1.0, 6.0, ((0, 32), (3, 16))),
        "bc_cache": scatter_about(key_list[11], (REQ * G, SLOTS, KC - 1, 2 * N), 1.0, 6.0, ((0, 32),)),
        "ssm_cache": scatter_about(key_list[12], (REQ * G, SLOTS, H // G, P_SIZE, N), 0.3, 2.0, ((0, 32), (2, 16)), jnp.float32),
        "slot_ids": draw_slot_ids(jax.random.fold_in(key_list[21], 71), 0),
        "parents": draw_parents(jax.random.fold_in(key_list[21], 71), 0),
        "ancestors": draw_ancestors(jax.random.fold_in(key_list[21], 71), 0),
        "norm_gated": jnp.clip(1.0 + 0.1 * jax.random.normal(key_list[16], (G, H // G * P_SIZE), jnp.float32), 0.5, 1.5),
        "out_proj": scatter_about(key_list[17], (G, H // G * P_SIZE, D), (H * P_SIZE) ** -0.5, 0.0625, ((1, 16), (2, 32))),
        "norm_ffn": jnp.clip(1.0 + 0.1 * jax.random.normal(key_list[18], (D,), jnp.float32), 0.5, 1.5),
        "ffn_up": scatter_about(key_list[19], (D, FF), D ** -0.5, 0.0625, ((0, 32), (1, 16))),
        "ffn_down": scatter_about(key_list[20], (FF, D), FF ** -0.5, 0.03125, ((0, 16), (1, 32))),
    }


EPSILON = 1e-05
HIGHEST = lax.Precision.HIGHEST

def blockwise(left_rows, right_cols, blocks):
    inner_size = left_rows.shape[1] // blocks
    left_blocks = left_rows.reshape(left_rows.shape[0], blocks, inner_size).transpose(1, 0, 2)
    right_blocks = right_cols.reshape(blocks, inner_size, right_cols.shape[1])

    def add_block(running, block_pair):
        partial_value = jnp.dot(block_pair[0], block_pair[1], preferred_element_type=jnp.float32)
        partial_value = lax.optimization_barrier(partial_value.astype(jnp.bfloat16))
        return (running + partial_value.astype(jnp.float32), None)
    start_sum = jnp.zeros((left_rows.shape[0], right_cols.shape[1]), jnp.float32)
    running, _ = lax.scan(add_block, start_sum, (left_blocks, right_blocks))
    return running

def rms_normed(row_values, gain_row):
    values = row_values.astype(jnp.float32)
    square_sum = lax.optimization_barrier(jnp.sum(values * values, axis=1, keepdims=True))
    return (values * lax.rsqrt(square_sum / D + EPSILON) * gain_row[None, :]).astype(jnp.bfloat16)

def tree_conv(values, history, kernel, tree_parents, tree_anc):
    node_count = values.shape[0]
    tap_count = kernel.shape[0]
    positions = jnp.arange(node_count, dtype=jnp.int32)
    parent_hop = (tree_parents[:, None] == positions[None, :]).astype(jnp.float32)
    node_depth = lax.optimization_barrier(jnp.sum(tree_anc, axis=1)) - 1
    history_pos = jnp.arange(tap_count - 1, dtype=jnp.int32)
    running = kernel[tap_count - 1][None, :] * values
    ancestor_hop = parent_hop
    for distance in range(1, tap_count):
        from_tree = jnp.dot(ancestor_hop, values, precision=HIGHEST)
        cache_pick = ((distance > node_depth)[:, None] & (history_pos[None, :] == (tap_count - 1 - distance + node_depth)[:, None])).astype(jnp.float32)
        from_cache = jnp.dot(cache_pick, history, precision=HIGHEST)
        running = running + kernel[tap_count - 1 - distance][None, :] * (from_tree + from_cache)
        ancestor_hop = jnp.dot(ancestor_hop, parent_hop, precision=HIGHEST)
    return jax.nn.silu(running)

def mixer_group(values, history, kernel, dt_raw, dt_offset, rate_log, skip_gain, start_state, gate_in, tree_parents, tree_anc):
    head_count = dt_raw.shape[1]
    head_width = head_count * P_SIZE
    conv_out = tree_conv(values, history, kernel, tree_parents, tree_anc)
    x_conv = conv_out[:, :head_width].reshape(-1, head_count, P_SIZE)
    b_matrix = conv_out[:, head_width:head_width + N]
    c_matrix = conv_out[:, head_width + N:]
    dt_step = jax.nn.softplus(dt_raw + dt_offset[None, :])
    log_decay = dt_step * (-jnp.exp(rate_log))[None, :]
    anc_float = tree_anc.astype(jnp.float32)
    cum_decay = jnp.dot(anc_float, log_decay, precision=HIGHEST)
    scores = jnp.dot(c_matrix, b_matrix.T, precision=HIGHEST)
    is_ancestor = tree_anc[:, :, None] > 0
    gaps_log = jnp.where(is_ancestor, cum_decay[:, None, :] - cum_decay[None, :, :], 0.0)
    weights = jnp.where(is_ancestor, jnp.exp(gaps_log), 0.0) * scores[:, :, None]
    inner_sum = jnp.einsum('ijh,jhp->ihp', weights, dt_step[:, :, None] * x_conv, precision=HIGHEST)
    carried = jnp.exp(cum_decay)[:, :, None] * jnp.einsum('in,hpn->ihp', c_matrix, start_state, precision=HIGHEST)
    mixed_out = inner_sum + carried + skip_gain[None, :, None] * x_conv
    return mixed_out * jax.nn.silu(gate_in)

def reference(hidden_in, norm_mixer, mixer_in, bc_proj, dt_proj, dt_bias, a_log, skip_d, conv_x, conv_bc, x_cache, bc_cache, ssm_cache, slot_ids, parents, ancestors, norm_gated, out_proj, norm_ffn, ffn_up, ffn_down):
    head_count = H // G
    head_width = head_count * P_SIZE
    mixer_normed = rms_normed(hidden_in, norm_mixer)
    projected = blockwise(mixer_normed, mixer_in.reshape(D, G * head_count * 2 * P_SIZE), N_ROW).reshape(REQ, NODES, G, head_count, 2 * P_SIZE)
    dt_raw = blockwise(mixer_normed, dt_proj.reshape(D, G * head_count), N_ROW).reshape(REQ, NODES, G, head_count)
    bc_raw = blockwise(mixer_normed, bc_proj.reshape(D, G * 2 * N), N_ROW).reshape(REQ, NODES, G, 2 * N)
    x_new = projected[..., :P_SIZE].reshape(REQ, NODES, G, head_width)
    gate_in = projected[..., P_SIZE:]
    conv_in = jnp.concatenate([x_new, bc_raw], axis=3)
    x_hist = x_cache.reshape(REQ, G, SLOTS, KC - 1, head_width)
    bc_hist = bc_cache.reshape(REQ, G, SLOTS, KC - 1, 2 * N)
    states = ssm_cache.reshape(REQ, G, SLOTS, head_count, P_SIZE, N)
    kernels = jnp.concatenate([conv_x, conv_bc], axis=2).astype(jnp.float32)
    run_group = jax.vmap(mixer_group, in_axes=(1, 0, 1, 1, 0, 0, 0, 0, 1, None, None))

    def one_request(request):
        slot_index = slot_ids[request]
        history = jnp.concatenate([x_hist[request][:, slot_index], bc_hist[request][:, slot_index]], axis=2).astype(jnp.float32)
        start_states = states[request][:, slot_index]
        return run_group(conv_in[request], history, kernels, dt_raw[request], dt_bias, a_log, skip_d, start_states, gate_in[request], parents[request], ancestors[request])
    gated = lax.map(one_request, jnp.arange(REQ, dtype=jnp.int32)).reshape(REQ, G, NODES, head_width)
    group_stat = lax.optimization_barrier(jnp.sum(gated * gated, axis=3, keepdims=True))
    mixed_heads = (gated * lax.rsqrt(group_stat / head_width + EPSILON) * norm_gated[None, :, None, :]).astype(jnp.bfloat16)
    col_width = head_width // N_COL
    left_rows = mixed_heads.reshape(REQ, G, NODES, N_COL, col_width).transpose(0, 2, 3, 1, 4).reshape(TOKENS, N_COL * G * col_width)
    right_cols = out_proj.reshape(G, N_COL, col_width, D).transpose(1, 0, 2, 3).reshape(N_COL * G * col_width, D)
    mixer_out = blockwise(left_rows, right_cols, N_COL)
    after = (hidden_in.astype(jnp.float32) + mixer_out).astype(jnp.bfloat16)
    ffn_normed = rms_normed(after, norm_ffn)
    up_sum = blockwise(ffn_normed, ffn_up, N_ROW)
    act = jnp.square(jax.nn.relu(up_sum)).astype(jnp.bfloat16)
    ffn_out = blockwise(act, ffn_down, N_COL)
    return (after.astype(jnp.float32) + ffn_out).astype(jnp.bfloat16)
```

```python
import jax
import jax.numpy as jnp
from jax import lax
from jax.sharding import PartitionSpec as P

D = 8192
H = 128
P_SIZE = 64
N = 256
G = 4


EPSILON = 1e-05
HIGHEST = lax.Precision.HIGHEST


def tree_conv(values, history, kernel, tree_parents, tree_anc):
    node_count = values.shape[0]
    tap_count = kernel.shape[0]
    positions = jnp.arange(node_count, dtype=jnp.int32)
    parent_hop = (tree_parents[:, None] == positions[None, :]).astype(jnp.float32)
    node_depth = jnp.sum(tree_anc, axis=1) - 1
    history_pos = jnp.arange(tap_count - 1, dtype=jnp.int32)
    running = kernel[tap_count - 1][None, :] * values
    ancestor_hop = parent_hop
    for distance in range(1, tap_count):
        from_tree = jnp.dot(ancestor_hop, values, precision=HIGHEST)
        cache_pick = (
            (distance > node_depth)[:, None]
            & (history_pos[None, :] == (tap_count - 1 - distance + node_depth)[:, None])
        ).astype(jnp.float32)
        from_cache = jnp.dot(cache_pick, history, precision=HIGHEST)
        running = running + kernel[tap_count - 1 - distance][None, :] * (from_tree + from_cache)
        ancestor_hop = jnp.dot(ancestor_hop, parent_hop, precision=HIGHEST)
    return jax.nn.silu(running)


def mixer_group(
    values,
    history,
    kernel,
    dt_raw,
    dt_offset,
    rate_log,
    skip_gain,
    start_state,
    gate_in,
    tree_parents,
    tree_anc,
):
    head_count = dt_raw.shape[1]
    head_width = head_count * P_SIZE
    conv_out = tree_conv(values, history, kernel, tree_parents, tree_anc)
    x_conv = conv_out[:, :head_width].reshape(-1, head_count, P_SIZE)
    b_matrix = conv_out[:, head_width : head_width + N]
    c_matrix = conv_out[:, head_width + N :]
    dt_step = jax.nn.softplus(dt_raw + dt_offset[None, :])
    log_decay = dt_step * (-jnp.exp(rate_log))[None, :]
    anc_float = tree_anc.astype(jnp.float32)
    cum_decay = jnp.dot(anc_float, log_decay, precision=HIGHEST)
    scores = jnp.dot(c_matrix, b_matrix.T, precision=HIGHEST)
    is_ancestor = tree_anc[:, :, None] > 0
    gaps_log = jnp.where(is_ancestor, cum_decay[:, None, :] - cum_decay[None, :, :], 0.0)
    weights = jnp.where(is_ancestor, jnp.exp(gaps_log), 0.0) * scores[:, :, None]
    inner_sum = jnp.einsum("ijh,jhp->ihp", weights, dt_step[:, :, None] * x_conv, precision=HIGHEST)
    carried = jnp.exp(cum_decay)[:, :, None] * jnp.einsum(
        "in,hpn->ihp", c_matrix, start_state, precision=HIGHEST
    )
    mixed_out = inner_sum + carried + skip_gain[None, :, None] * x_conv
    return mixed_out * jax.nn.silu(gate_in)


def sum_parts(parts, axis):
    received = lax.all_to_all(parts, axis, 0, 0, tiled=True)
    return jnp.sum(received.astype(jnp.float32), axis=0)


def local(
    hidden_in,
    norm_mixer,
    mixer_in,
    bc_proj,
    dt_proj,
    dt_bias,
    a_log,
    skip_d,
    conv_x,
    conv_bc,
    x_cache,
    bc_cache,
    ssm_cache,
    slot_ids,
    parents,
    ancestors,
    norm_gated,
    out_proj,
    norm_ffn,
    ffn_up,
    ffn_down,
):
    groups = mixer_in.shape[1]
    requests = slot_ids.shape[0]
    node_count = parents.shape[1]
    row_index = lax.axis_index("row")
    request = row_index // groups
    group_index = row_index % groups
    rows = lax.axis_size("row")
    cols = lax.axis_size("col")
    residual = hidden_in.astype(jnp.float32)
    all_hidden = lax.all_gather(hidden_in, "col", axis=0, tiled=True).astype(jnp.float32)
    mixer_part = jnp.sum(all_hidden * all_hidden, axis=1)
    tokens = (all_hidden * norm_mixer[None, :]).astype(jnp.bfloat16)
    tokens = tokens.reshape(requests, node_count, tokens.shape[1])
    xz_term = jnp.einsum("qtd,dghe->qgthe", tokens, mixer_in, preferred_element_type=jnp.float32)
    xz_term = xz_term.reshape(rows, node_count, -1)
    dt_term = jnp.einsum("qtd,dgh->qgth", tokens, dt_proj, preferred_element_type=jnp.float32)
    dt_term = dt_term.reshape(rows, node_count, -1)
    bc_term = jnp.einsum("qtd,dge->qgte", tokens, bc_proj, preferred_element_type=jnp.float32)
    bc_term = bc_term.reshape(rows, node_count, -1)
    sq_term = jnp.broadcast_to(
        mixer_part.reshape(requests, 1, node_count, 1), (requests, groups, node_count, 1)
    ).reshape(rows, node_count, 1)
    widths = [xz_term.shape[2], bc_term.shape[2], dt_term.shape[2]]
    in_term = jnp.concatenate([xz_term, bc_term, dt_term, sq_term], axis=2).astype(jnp.bfloat16)
    in_sum = sum_parts(in_term, "row")
    scale = lax.rsqrt(in_sum[:, -1:] / D + EPSILON)
    in_sum = in_sum[:, :-1] * scale
    xz_sum = in_sum[None, :, : widths[0]]
    bc_sum = in_sum[None, :, widths[0] : widths[0] + widths[1]]
    dt_sum = in_sum[None, :, widths[0] + widths[1] :]
    head_count = dt_sum.shape[2]
    xz_local = xz_sum[0].reshape(node_count, head_count, 2 * P_SIZE)
    x_new = xz_local[:, :, :P_SIZE].reshape(node_count, head_count * P_SIZE)
    gate_in = xz_local[:, :, P_SIZE:]
    bc_new = lax.all_gather(bc_sum[0], "col", axis=1, tiled=True)
    slot_index = lax.dynamic_index_in_dim(slot_ids, request, 0, keepdims=False)
    tree_parents = lax.dynamic_index_in_dim(parents, request, 0, keepdims=False)
    tree_anc = lax.dynamic_index_in_dim(ancestors, request, 0, keepdims=False)
    x_hist = lax.dynamic_index_in_dim(x_cache[0], slot_index, 0, keepdims=False)
    bc_hist = lax.dynamic_index_in_dim(bc_cache[0], slot_index, 0, keepdims=False)
    start_state = lax.dynamic_index_in_dim(ssm_cache[0], slot_index, 0, keepdims=False)
    history = jnp.concatenate([x_hist, bc_hist], axis=1).astype(jnp.float32)
    kernel = jnp.concatenate(
        [
            lax.dynamic_index_in_dim(conv_x, group_index, 1, keepdims=False),
            lax.dynamic_index_in_dim(conv_bc, group_index, 1, keepdims=False),
        ],
        axis=1,
    ).astype(jnp.float32)
    values = jnp.concatenate([x_new, bc_new], axis=1)

    def pick_group(table):
        return lax.dynamic_index_in_dim(table, group_index, 0, keepdims=False)

    gated = mixer_group(
        values,
        history,
        kernel,
        dt_sum[0],
        pick_group(dt_bias),
        pick_group(a_log),
        pick_group(skip_d),
        start_state,
        gate_in,
        tree_parents,
        tree_anc,
    )
    group_sq = lax.psum(jnp.sum(gated * gated, axis=(1, 2)), "col")
    gated_flat = gated.reshape(node_count, -1)
    mixed_heads = (
        gated_flat
        * lax.rsqrt(group_sq[:, None] / (H // G * P_SIZE) + EPSILON)
        * pick_group(norm_gated)[None, :]
    ).astype(jnp.bfloat16)
    all_heads = lax.all_gather(mixed_heads[None], "row", axis=0, tiled=True)
    all_heads = all_heads.reshape(requests, groups, node_count, -1)
    mixer_term = jnp.einsum(
        "qgtc,gcd->qtd", all_heads, out_proj, preferred_element_type=jnp.float32
    )
    mixer_out = sum_parts(
        mixer_term.reshape(cols, -1, mixer_term.shape[-1]).astype(jnp.bfloat16), "col"
    )
    after = (residual + mixer_out).astype(jnp.bfloat16)
    all_after = lax.all_gather(after, "col", axis=0, tiled=True).astype(jnp.float32)
    ffn_part = jnp.sum(all_after * all_after, axis=1)
    up_term = jnp.dot(
        (all_after * norm_ffn[None, :]).astype(jnp.bfloat16),
        ffn_up,
        preferred_element_type=jnp.float32,
    )
    up_term = jnp.concatenate([up_term, ffn_part[:, None]], axis=1).astype(jnp.bfloat16)
    up_sum = sum_parts(up_term.reshape(rows, -1, up_term.shape[1]), "row")
    up_share = up_sum[:, :-1] * lax.rsqrt(up_sum[:, -1:] / D + EPSILON)
    act_share = jnp.square(jax.nn.relu(up_share)).astype(jnp.bfloat16)
    act_all = lax.all_to_all(
        jnp.broadcast_to(act_share[None], (rows,) + act_share.shape), "row", 0, 0, tiled=True
    )
    act_all = act_all.reshape(-1, act_all.shape[-1])
    ffn_term = jnp.dot(act_all, ffn_down, preferred_element_type=jnp.float32).astype(jnp.bfloat16)
    ffn_out = sum_parts(ffn_term.reshape(cols, -1, ffn_term.shape[1]), "col")
    return (after.astype(jnp.float32) + ffn_out).astype(jnp.bfloat16)


def solution(mesh):
    return jax.shard_map(
        local,
        mesh=mesh,
        in_specs=(
            P("col", "row"),
            P("row"),
            P("row", None, "col", None),
            P("row", None, "col"),
            P("row", None, "col"),
            P(None, "col"),
            P(None, "col"),
            P(None, "col"),
            P(None, None, "col"),
            P(),
            P("row", None, None, "col"),
            P("row", None, None, None),
            P("row", None, "col", None, None),
            P(),
            P(),
            P(),
            P(None, "col"),
            P(None, "col", "row"),
            P("row"),
            P("row", "col"),
            P("col", "row"),
        ),
        out_specs=P("col", "row"),
        check_vma=False,
    )
```

```python
import jax
import jax.numpy as jnp
from jax import lax
from jax.experimental import pallas as pl
from jax.experimental.pallas import tpu as pltpu
from jax.sharding import PartitionSpec as P

D = 8192
H = 128
P_SIZE = 64
N = 256
G = 4

EPSILON = 1e-05
F32 = jnp.float32
BF16 = jnp.bfloat16
NT = (((1,), (1,)), ((), ()))
VMEM_LIMIT = 48 * 1024 * 1024


def spread(block, axis):
    size = lax.axis_size(axis)
    return lax.all_to_all(
        jnp.broadcast_to(block[None], (size,) + block.shape), axis, 0, 0, tiled=True
    )


def sum_parts(parts, axis):
    received = lax.all_to_all(parts, axis, 0, 0, tiled=True)
    return jnp.sum(received.astype(F32), axis=0)


def call(kernel, out_shape, *operands):
    return pl.pallas_call(
        kernel,
        out_shape=out_shape,
        compiler_params=pltpu.CompilerParams(vmem_limit_bytes=VMEM_LIMIT),
    )(*operands)


def two_halves(values):
    high = lax.reduce_precision(values, 8, 7)
    return high.astype(BF16), (values - high).astype(BF16)


def project_kernel(hidden_ref, gain_ref, main_ref, side_ref, out_ref):
    hidden = hidden_ref[...].astype(F32)
    normed = (hidden * gain_ref[...]).astype(BF16)
    squares = (hidden * hidden).astype(BF16)
    ones = jnp.ones((16, hidden.shape[1]), BF16)
    stat = lax.dot_general(ones, squares, NT, preferred_element_type=F32)
    for group in range(G):
        main = jnp.dot(
            normed, main_ref[:, group * 256 : (group + 1) * 256], preferred_element_type=F32
        ).astype(BF16)
        side = lax.dot_general(
            side_ref[group * 64 : (group + 1) * 64, :], normed, NT, preferred_element_type=F32
        )
        for request in range(8):
            nodes = slice(request * 64, (request + 1) * 64)
            out_ref[request, group, 0:64, :] = main[nodes, :]
            pieces = [side[0:16, nodes], side[16:32, nodes], side[32:48, nodes], stat[:, nodes]]
            out_ref[request, group, 64:80, :] = jnp.concatenate(pieces, axis=1).astype(BF16)


def combine_kernel(parts_ref, out_ref):
    total = parts_ref[0].astype(F32)
    for part in range(1, parts_ref.shape[0]):
        total = total + parts_ref[part].astype(F32)
    scale_row = lax.rsqrt(total[64:65, 192:256] / D + EPSILON)
    eye = lax.broadcasted_iota(jnp.int32, (64, 64), 0) == lax.broadcasted_iota(
        jnp.int32, (64, 64), 1
    )
    scale_col = jnp.sum(
        jnp.where(eye, jnp.broadcast_to(scale_row, (64, 64)), 0.0), axis=1, keepdims=True
    )
    main = total[0:64, :]
    main = jnp.concatenate(
        [main[:, 0:64], main[:, 128:192], main[:, 64:128], main[:, 192:256]], axis=1
    )
    out_ref[0:64, :] = (main * scale_col).astype(BF16)
    scale_all = jnp.concatenate([scale_row] * 4, axis=1)
    out_ref[64:80, :] = (total[64:80, :] * scale_all).astype(BF16)


def mixer_kernel(
    place_ref,
    new_ref,
    x_hist_ref,
    x_taps_ref,
    bc_hist_ref,
    bc_taps_ref,
    head_ref,
    gain_ref,
    state_ref,
    parents_ref,
    anc_ref,
    out_ref,
    x_ref,
    gate_ref,
    bc_ref,
    step_ref,
):
    cols = new_ref.shape[0]
    first = place_ref[0] * 4
    for col in range(cols):
        lanes = slice(col * 128, (col + 1) * 128)
        x_ref[0:64, lanes] = new_ref[col, 0:64, 0:128]
        gate_ref[:, lanes] = new_ref[col, 0:64, 128:256]
        tail = new_ref[col, 64:80, :].astype(F32)
        bc_ref[col * 32 : col * 32 + 16, 0:64] = tail[:, 0:64].astype(BF16)
        bc_ref[col * 32 + 16 : col * 32 + 32, 0:64] = tail[:, 64:128].astype(BF16)
        step_ref[col * 2 : col * 2 + 2, :] = tail[0:2, 128:192]
    x_ref[64:80, :] = x_hist_ref[...]
    bc_ref[:, 64:128] = bc_hist_ref[...]

    node_row = lax.broadcasted_iota(jnp.int32, (64, 64), 1)
    node_col = lax.broadcasted_iota(jnp.int32, (64, 64), 0)
    anc = anc_ref[...]
    anc_float = anc.astype(F32)
    depth = jnp.sum(anc, axis=1, keepdims=True) - 1
    hop = (parents_ref[...] == node_row).astype(BF16)
    hops = [None, hop]
    for _ in range(2):
        hops.append(jnp.dot(hops[-1], hop, preferred_element_type=F32).astype(BF16))

    def picks(distance, width):
        lane = lax.broadcasted_iota(jnp.int32, (64, width), 1)
        return ((distance > depth) & (lane == 3 - distance + depth)).astype(BF16)

    x_run = x_ref[0:64, :].astype(F32) * x_taps_ref[3:4, :]
    for distance in range(1, 4):
        mover = jnp.concatenate([hops[distance], picks(distance, 16)], axis=1)
        moved = jnp.dot(mover, x_ref[...], preferred_element_type=F32)
        x_run = x_run + moved * x_taps_ref[3 - distance : 4 - distance, :]
    x_conv = (x_run * jax.nn.sigmoid(x_run)).astype(BF16)
    bc_run = bc_ref[:, 0:64].astype(F32) * bc_taps_ref[:, 3:4]
    for distance in range(1, 4):
        mover = jnp.concatenate([hops[distance], picks(distance, 64)], axis=1)
        moved = lax.dot_general(bc_ref[...], mover, NT, preferred_element_type=F32)
        bc_run = bc_run + moved * bc_taps_ref[:, 3 - distance : 4 - distance]
    bc_conv = (bc_run * jax.nn.sigmoid(bc_run)).astype(BF16)

    raw = step_ref[...] + head_ref[:, 0:1]
    step = jnp.maximum(raw, 0.0) + jnp.log1p(jnp.exp(-jnp.abs(raw)))
    log_decay = -jnp.exp(head_ref[:, 1:2]) * step
    cum = lax.dot_general(
        log_decay,
        anc_float,
        NT,
        precision=lax.Precision.HIGHEST,
        preferred_element_type=F32,
    )

    own = (
        lax.broadcasted_iota(jnp.int32, (16, 64), 0) + first
        == lax.broadcasted_iota(jnp.int32, (16, 64), 1)
    ).astype(BF16)
    c_own = lax.dot_general(own, bc_conv[256:512, :], NT, preferred_element_type=F32).astype(BF16)
    scores = jnp.dot(c_own, bc_conv[0:256, :], preferred_element_type=F32)
    state = state_ref[...].reshape(-1, N)
    carried = lax.dot_general(c_own, state, NT, preferred_element_type=F32)
    x_own = jnp.dot(own, x_conv, preferred_element_type=F32)
    gate_own = jnp.dot(own, gate_ref[...], preferred_element_type=F32)

    weights = []
    starts = []
    for node in range(4):
        here = first + node
        mask = jnp.sum(jnp.where(node_col == here, anc, 0), axis=0, keepdims=True) > 0
        lane = lax.broadcasted_iota(jnp.int32, cum.shape, 1)
        cum_here = jnp.sum(jnp.where(lane == here, cum, 0.0), axis=1, keepdims=True)
        gap = jnp.where(mask, cum_here - cum, 0.0)
        weight = jnp.where(mask, jnp.exp(gap), 0.0) * scores[node : node + 1, :] * step
        weights.append(weight.astype(BF16))
        starts.append(jnp.exp(cum_here))
    mixed = jnp.dot(jnp.concatenate(weights, axis=0), x_conv, preferred_element_type=F32)
    heads = 2 * cols
    wide = (heads, heads * P_SIZE)
    own_head = (
        lax.broadcasted_iota(jnp.int32, wide, 1) // P_SIZE
        == lax.broadcasted_iota(jnp.int32, wide, 0)
    )
    skip = head_ref[:, 2:3]
    rows = []
    for node in range(4):
        term = (
            mixed[node * heads : (node + 1) * heads, :]
            + starts[node] * carried[node : node + 1, :]
            + skip * x_own[node : node + 1, :]
        )
        rows.append(jnp.sum(jnp.where(own_head, term, 0.0), axis=0, keepdims=True))
    mixed_own = jnp.concatenate(rows, axis=0)
    gate = gate_own[0:4, :]
    gated = mixed_own * (gate * jax.nn.sigmoid(gate))
    group_sq = jnp.sum(gated * gated, axis=1, keepdims=True)
    out = gated * lax.rsqrt(group_sq / (H // G * P_SIZE) + EPSILON) * gain_ref[...]
    out_ref[...] = out.astype(BF16)


def local(
    hidden_in,
    norm_mixer,
    mixer_in,
    bc_proj,
    dt_proj,
    dt_bias,
    a_log,
    skip_d,
    conv_x,
    conv_bc,
    x_cache,
    bc_cache,
    ssm_cache,
    slot_ids,
    parents,
    ancestors,
    norm_gated,
    out_proj,
    norm_ffn,
    ffn_up,
    ffn_down,
):
    rows = lax.axis_size("row")
    cols = lax.axis_size("col")
    row_index = lax.axis_index("row")
    col_index = lax.axis_index("col")
    request = row_index // G
    group_index = row_index % G

    def pick(table, index, axis=0):
        return lax.dynamic_index_in_dim(table, index, axis, keepdims=False)

    slot_index = pick(slot_ids, request)
    start_state = pick(ssm_cache[0], slot_index).astype(BF16).reshape(-1, N)
    early = jnp.concatenate([out_proj.reshape(-1, N), start_state], axis=0)
    early = lax.all_gather(early, "col", axis=0, tiled=False)
    out_weights = early[:, :512].reshape(cols, G, 128, 256)

    small = jnp.concatenate(
        [pick(dt_bias, group_index), pick(a_log, group_index), pick(skip_d, group_index)]
    )
    table = jnp.concatenate(
        [
            pick(conv_x, group_index, 1).astype(F32),
            pick(x_cache[0], slot_index).astype(F32),
            pick(norm_gated, group_index)[None],
            jnp.pad(small, (0, 128 - small.shape[0]))[None],
        ],
        axis=0,
    )
    high, low = two_halves(table)
    packed = jnp.concatenate([high, low[7:9], jnp.zeros((5, 128), BF16)], axis=0)
    sent = jnp.concatenate([hidden_in, packed.reshape(8, 256)], axis=0)
    spread_in = spread(sent, "col")
    hidden = spread_in[:, :32].reshape(512, 256)
    param = spread_in[:, 32:].reshape(cols, 16, 128).astype(F32)
    x_taps = param[:, 0:4].transpose(1, 0, 2).reshape(4, -1)
    x_hist = param[:, 4:7].astype(BF16).transpose(1, 0, 2).reshape(3, -1)
    x_hist = jnp.pad(x_hist, ((0, 13), (0, 0)))
    gain = (param[:, 7] + param[:, 9]).reshape(1, -1)
    head = (param[:, 8] + param[:, 10])[:, 0:6].reshape(cols, 3, 2).transpose(0, 2, 1)
    head = jnp.pad(head.reshape(2 * cols, 3), ((0, 0), (0, 125)))
    bc_hist = jnp.pad(pick(bc_cache[0], slot_index).T, ((0, 0), (0, 61)))
    bc_taps = jnp.pad(pick(conv_bc, group_index, 1).T.astype(F32), ((0, 0), (0, 124)))

    side = jnp.concatenate([bc_proj, dt_proj, jnp.zeros((256, G, 30), BF16)], axis=2)
    side = side.reshape(256, 256).T
    parts = call(
        project_kernel,
        jax.ShapeDtypeStruct((rows // G, G, 80, 256), BF16),
        hidden,
        norm_mixer[None, :],
        mixer_in.reshape(256, -1),
        side,
    )
    parts = lax.all_to_all(parts.reshape(rows, 80, 256), "row", 0, 0, tiled=True)
    combined = call(combine_kernel, jax.ShapeDtypeStruct((80, 256), BF16), parts)
    new = spread(combined, "col")
    operands = [
        x_hist,
        x_taps,
        bc_hist,
        bc_taps,
        head,
        gain,
        early,
        pick(parents, request)[:, None],
        pick(ancestors, request),
    ]

    def whole(shape):
        return pl.BlockSpec(shape, lambda step: (0,) * len(shape))

    specs = [whole(operand.shape) for operand in operands]
    specs[6] = pl.BlockSpec((cols, 128, N), lambda step: (0, 4, 0))
    mixed = pl.pallas_call(
        mixer_kernel,
        grid=(1,),
        out_shape=jax.ShapeDtypeStruct((4, 2048), BF16),
        in_specs=[pl.BlockSpec(memory_space=pltpu.SMEM), whole(new.shape)] + specs,
        out_specs=whole((4, 2048)),
        scratch_shapes=[
            pltpu.VMEM((80, 2048), BF16),
            pltpu.VMEM((64, 2048), BF16),
            pltpu.VMEM((512, 128), BF16),
            pltpu.VMEM((32, 64), F32),
        ],
        compiler_params=pltpu.CompilerParams(vmem_limit_bytes=VMEM_LIMIT),
    )(col_index.astype(jnp.int32)[None], new, *operands)

    heads = lax.all_gather(mixed, "row", axis=0, tiled=False)
    heads = heads.reshape(rows // G, G, 4, cols, 128)
    mixer_out = jnp.einsum("qgtck,cgkd->qtd", heads, out_weights, preferred_element_type=F32)
    residual = lax.dynamic_slice(
        hidden.reshape(8, 64, 256), (0, 4 * col_index, 0), (8, 4, 256)
    ).astype(F32)
    after = (residual + mixer_out).astype(BF16).reshape(32, 256)
    all_after = lax.all_gather(after, "col", axis=0, tiled=False)
    all_after = all_after.reshape(cols, 8, 4, 256).transpose(1, 0, 2, 3).reshape(512, 256)
    after_wide = all_after.astype(F32)
    ffn_part = jnp.sum(after_wide * after_wide, axis=1)
    up_term = jnp.dot(
        (after_wide * norm_ffn[None, :]).astype(BF16), ffn_up, preferred_element_type=F32
    )
    up_term = jnp.concatenate([up_term, ffn_part[:, None]], axis=1).astype(BF16)
    up_sum = sum_parts(up_term.reshape(rows, -1, up_term.shape[1]), "row")
    up_share = up_sum[:, :-1] * lax.rsqrt(up_sum[:, -1:] / D + EPSILON)
    act_share = jnp.square(jax.nn.relu(up_share)).astype(BF16)
    act_all = spread(act_share, "row").reshape(512, -1)
    ffn_term = jnp.dot(act_all, ffn_down, preferred_element_type=F32).astype(BF16)
    ffn_out = sum_parts(ffn_term.reshape(cols, -1, ffn_term.shape[1]), "col")
    own_after = lax.dynamic_slice(all_after, (32 * col_index, 0), (32, 256))
    return (own_after.astype(F32) + ffn_out).astype(BF16)


def solution(mesh):
    return jax.shard_map(
        local,
        mesh=mesh,
        in_specs=(
            P("col", "row"),
            P("row"),
            P("row", None, "col", None),
            P("row", None, "col"),
            P("row", None, "col"),
            P(None, "col"),
            P(None, "col"),
            P(None, "col"),
            P(None, None, "col"),
            P(),
            P("row", None, None, "col"),
            P("row", None, None, None),
            P("row", None, "col", None, None),
            P(),
            P(),
            P(),
            P(None, "col"),
            P(None, "col", "row"),
            P("row"),
            P("row", "col"),
            P("col", "row"),
        ),
        out_specs=P("col", "row"),
        check_vma=False,
    )
```

```python
import jax
import jax.numpy as jnp
from jax import lax
from jax.experimental import pallas as pl
from jax.experimental.pallas import tpu as pltpu
from jax.sharding import PartitionSpec as P

D = 8192
H = 128
P_SIZE = 64
N = 256
G = 4

EPSILON = 1e-05
F32 = jnp.float32
BF16 = jnp.bfloat16
NT = (((1,), (1,)), ((), ()))
VMEM_LIMIT = 48 * 1024 * 1024


def spread(block, axis):
    size = lax.axis_size(axis)
    return lax.all_to_all(
        jnp.broadcast_to(block[None], (size,) + block.shape), axis, 0, 0, tiled=True
    )


def sum_parts(parts, axis):
    received = lax.all_to_all(parts, axis, 0, 0, tiled=True)
    return jnp.sum(received.astype(F32), axis=0)


def call(kernel, out_shape, *operands):
    return pl.pallas_call(
        kernel,
        out_shape=out_shape,
        compiler_params=pltpu.CompilerParams(vmem_limit_bytes=VMEM_LIMIT),
    )(*operands)


def project_side_kernel(hidden_ref, gain_ref, side_ref, out_ref):
    hidden = hidden_ref[...].astype(F32)
    normed = (hidden * gain_ref[...]).astype(BF16)
    squares = (hidden * hidden).astype(BF16)
    ones = jnp.ones((16, hidden.shape[1]), BF16)
    stat = lax.dot_general(ones, squares, NT, preferred_element_type=F32)
    for group in range(G):
        side = lax.dot_general(
            side_ref[group * 64 : (group + 1) * 64, :], normed, NT, preferred_element_type=F32
        )
        for request in range(8):
            nodes = slice(request * 64, (request + 1) * 64)
            pieces = [side[0:16, nodes], side[16:32, nodes], side[32:48, nodes], stat[:, nodes]]
            out_ref[request, group, :, :] = jnp.concatenate(pieces, axis=1).astype(BF16)


def project_main_kernel(hidden_ref, gain_ref, main_ref, out_ref):
    normed = (hidden_ref[...].astype(F32) * gain_ref[...]).astype(BF16)
    for group in range(G):
        main = jnp.dot(
            normed, main_ref[:, group * 256 : (group + 1) * 256], preferred_element_type=F32
        ).astype(BF16)
        for request in range(8):
            out_ref[request, group, :, :] = main[request * 64 : (request + 1) * 64, :]


def combine_side_kernel(parts_ref, bc_ref, local_ref):
    total = parts_ref[0].astype(F32)
    for part in range(1, parts_ref.shape[0]):
        total = total + parts_ref[part].astype(F32)
    scale = lax.rsqrt(total[0:1, 192:256] / D + EPSILON)
    bc_ref[...] = (total[:, 0:128] * jnp.concatenate([scale, scale], axis=1)).astype(BF16)
    local_ref[0:2, :] = total[0:2, 128:192] * scale
    local_ref[2:3, :] = scale
    local_ref[3:8, :] = jnp.zeros((5, 64), F32)


def column_of(row, size):
    eye = lax.broadcasted_iota(jnp.int32, (size, size), 0) == lax.broadcasted_iota(
        jnp.int32, (size, size), 1
    )
    wide = jnp.broadcast_to(row, (size, size))
    return jnp.sum(jnp.where(eye, wide, jnp.zeros_like(wide)), axis=1, keepdims=True)


def mixer_kernel(
    place_ref,
    slot_ref,
    parts_ref,
    bc_new_ref,
    local_ref,
    x_hist_ref,
    bc_hist_ref,
    state_ref,
    x_taps_ref,
    bc_taps_ref,
    head_ref,
    gain_ref,
    parents_ref,
    anc_ref,
    out_ref,
    bc_ref,
):
    request = place_ref[0]
    group = place_ref[1]
    total = parts_ref[0].astype(F32)
    for part in range(1, parts_ref.shape[0]):
        total = total + parts_ref[part].astype(F32)
    total = total * column_of(local_ref[2:3, :], 64)
    x_new = jnp.concatenate([total[:, 0:64], total[:, 128:192]], axis=1)
    gate = jnp.concatenate([total[:, 64:128], total[:, 192:256]], axis=1)

    for col in range(bc_new_ref.shape[0]):
        piece = bc_new_ref[col].astype(F32)
        bc_ref[col * 32 : col * 32 + 16, 0:64] = piece[:, 0:64].astype(BF16)
        bc_ref[col * 32 + 16 : col * 32 + 32, 0:64] = piece[:, 64:128].astype(BF16)
    bc_ref[:, 64:128] = bc_hist_ref[...]

    x_taps = jnp.zeros((4, 128), F32)
    gain = jnp.zeros((1, 128), F32)
    for index in range(G):
        x_taps = jnp.where(group == index, x_taps_ref[:, index, :].astype(F32), x_taps)
        gain = jnp.where(group == index, gain_ref[index : index + 1, :], gain)

    lane = lax.broadcasted_iota(jnp.int32, (64, 64), 1)
    row = lax.broadcasted_iota(jnp.int32, (64, 64), 0)
    anc = anc_ref[0]
    depth = jnp.sum(anc, axis=1, keepdims=True) - 1
    all_parents = parents_ref[...]
    this = lax.broadcasted_iota(jnp.int32, all_parents.shape, 0) == request
    parent_row = jnp.sum(jnp.where(this, all_parents, 0), axis=0, keepdims=True)
    hop = (column_of(parent_row, 64) == lane).astype(BF16)
    hops = [None, hop]
    for _ in range(2):
        hops.append(jnp.dot(hops[-1], hop, preferred_element_type=F32).astype(BF16))

    x_high = x_new.astype(BF16)
    x_low = (x_new - x_high.astype(F32)).astype(BF16)
    x_both = jnp.concatenate([x_high, x_low], axis=1)
    x_hist = x_hist_ref[0, 0].astype(F32)
    x_run = x_new * x_taps[3:4, :]
    for distance in range(1, 4):
        moved = jnp.dot(hops[distance], x_both, preferred_element_type=F32)
        moved = moved[:, 0:128] + moved[:, 128:256]
        for entry in range(3):
            use = (distance > depth) & (entry == 3 - distance + depth)
            moved = moved + jnp.where(use, x_hist[entry : entry + 1, :], 0.0)
        x_run = x_run + moved * x_taps[3 - distance : 4 - distance, :]
    x_conv = x_run * jax.nn.sigmoid(x_run)
    bc_run = bc_ref[:, 0:64].astype(F32) * bc_taps_ref[:, 3:4]
    for distance in range(1, 4):
        pick = ((distance > depth) & (lane == 3 - distance + depth)).astype(BF16)
        mover = jnp.concatenate([hops[distance], pick], axis=1)
        moved = lax.dot_general(bc_ref[...], mover, NT, preferred_element_type=F32)
        bc_run = bc_run + moved * bc_taps_ref[:, 3 - distance : 4 - distance]
    bc_conv = (bc_run * jax.nn.sigmoid(bc_run)).astype(BF16)

    raw = local_ref[0:2, :] + column_of(head_ref[0:1, 0:128], 128)[0:2, :]
    step = jnp.maximum(raw, 0.0) + jnp.log1p(jnp.exp(-jnp.abs(raw)))
    log_decay = -jnp.exp(column_of(head_ref[1:2, 0:128], 128)[0:2, :]) * step
    cum = lax.dot_general(
        jnp.concatenate([log_decay, jnp.zeros((6, 64), F32)], axis=0),
        anc.astype(F32),
        NT,
        precision=lax.Precision.HIGHEST,
        preferred_element_type=F32,
    )

    eye = (lane == row).astype(BF16)
    c_node = lax.dot_general(eye, bc_conv[256:512, :], NT, preferred_element_type=F32).astype(BF16)
    scores = jnp.dot(c_node, bc_conv[0:256, :], preferred_element_type=F32)
    state = state_ref[0, 0].reshape(2 * P_SIZE, N).astype(BF16)
    carried = lax.dot_general(c_node, state, NT, preferred_element_type=F32)
    x_bf = x_conv.astype(BF16)
    is_anc = anc > 0
    inner = []
    start = []
    for head in range(2):
        cum_row = cum[head : head + 1, :]
        cum_col = column_of(cum_row, 64)
        gap = jnp.where(is_anc, cum_col - cum_row, 0.0)
        weight = jnp.where(is_anc, jnp.exp(gap), 0.0) * scores * step[head : head + 1, :]
        inner.append(jnp.dot(weight.astype(BF16), x_bf, preferred_element_type=F32))
        start.append(jnp.exp(cum_col))
    first = lax.broadcasted_iota(jnp.int32, (64, 128), 1) < P_SIZE
    skip = column_of(head_ref[2:3, 0:128], 128)
    mixed = (
        jnp.where(first, inner[0], inner[1])
        + jnp.where(first, start[0], start[1]) * carried
        + jnp.where(first, skip[0:1, :], skip[1:2, :]) * x_conv
    )
    gated = mixed * (gate * jax.nn.sigmoid(gate))
    group_sq = jnp.sum(gated * gated, axis=1, keepdims=True)
    out_ref[:, 0:128] = (gated * gain).astype(BF16)
    out_ref[:, 128:256] = jnp.broadcast_to(group_sq, (64, 128)).astype(BF16)


def scale_heads_kernel(parts_ref, out_ref):
    total = parts_ref[0, :, 128:256].astype(F32)
    for part in range(1, parts_ref.shape[0]):
        total = total + parts_ref[part, :, 128:256].astype(F32)
    scale = lax.rsqrt(total / (H // G * P_SIZE) + EPSILON)
    for part in range(parts_ref.shape[0]):
        piece = parts_ref[part, :, 0:128].astype(F32) * scale
        out_ref[:, part * 128 : (part + 1) * 128] = piece.astype(BF16)


def local(
    hidden_in,
    norm_mixer,
    mixer_in,
    bc_proj,
    dt_proj,
    dt_bias,
    a_log,
    skip_d,
    conv_x,
    conv_bc,
    x_cache,
    bc_cache,
    ssm_cache,
    slot_ids,
    parents,
    ancestors,
    norm_gated,
    out_proj,
    norm_ffn,
    ffn_up,
    ffn_down,
):
    rows = lax.axis_size("row")
    cols = lax.axis_size("col")
    row_index = lax.axis_index("row")
    col_index = lax.axis_index("col")
    request = row_index // G
    group_index = row_index % G

    def pick(table, index, axis=0):
        return lax.dynamic_index_in_dim(table, index, axis, keepdims=False)

    out_weights = lax.all_gather(out_proj, "col", axis=0, tiled=False)

    hidden = spread(hidden_in, "col").reshape(512, 256)
    gain = norm_mixer[None, :]
    side = jnp.concatenate([bc_proj, dt_proj, jnp.zeros((256, G, 30), BF16)], axis=2)
    side = side.reshape(256, 256).T
    side_parts = call(
        project_side_kernel,
        jax.ShapeDtypeStruct((rows // G, G, 16, 256), BF16),
        hidden,
        gain,
        side,
    )
    side_parts = lax.all_to_all(side_parts.reshape(rows, 16, 256), "row", 0, 0, tiled=True)
    bc_own, local_rows = call(
        combine_side_kernel,
        (jax.ShapeDtypeStruct((16, 128), BF16), jax.ShapeDtypeStruct((8, 64), F32)),
        side_parts,
    )
    main_parts = call(
        project_main_kernel,
        jax.ShapeDtypeStruct((rows // G, G, 64, 256), BF16),
        hidden,
        gain,
        mixer_in.reshape(256, -1),
    )
    main_parts, bc_own = lax.optimization_barrier((main_parts, bc_own))
    main_parts = lax.all_to_all(main_parts.reshape(rows, 64, 256), "row", 0, 0, tiled=True)
    bc_new = lax.all_gather(bc_own, "col", axis=0, tiled=False)

    slot_index = pick(slot_ids, request)
    bc_hist = jnp.pad(pick(bc_cache[0], slot_index).T, ((0, 0), (0, 61)))
    bc_taps = jnp.pad(pick(conv_bc, group_index, 1).T.astype(F32), ((0, 0), (0, 124)))
    head = jnp.stack([pick(dt_bias, group_index), pick(a_log, group_index), pick(skip_d, group_index)])
    head = jnp.pad(head, ((0, 5), (0, 126)))
    place = jnp.stack([request, group_index]).astype(jnp.int32)

    def whole(array):
        shape = array.shape
        return pl.BlockSpec(shape, lambda step, place, slots: (0,) * len(shape))

    def slot_block(*shape):
        zeros = (0,) * (len(shape) - 2)
        return pl.BlockSpec(shape, lambda step, place, slots: (0, slots[place[0]]) + zeros)

    operands = [
        (main_parts, whole(main_parts)),
        (bc_new, whole(bc_new)),
        (local_rows, whole(local_rows)),
        (x_cache, slot_block(1, 1, 3, 128)),
        (bc_hist, whole(bc_hist)),
        (ssm_cache, slot_block(1, 1, 2, P_SIZE, N)),
        (conv_x, whole(conv_x)),
        (bc_taps, whole(bc_taps)),
        (head, whole(head)),
        (norm_gated, whole(norm_gated)),
        (parents, whole(parents)),
        (ancestors, pl.BlockSpec((1, 64, 64), lambda step, place, slots: (place[0], 0, 0))),
    ]
    mixed = pl.pallas_call(
        mixer_kernel,
        grid_spec=pltpu.PrefetchScalarGridSpec(
            num_scalar_prefetch=2,
            grid=(1,),
            in_specs=[spec for _, spec in operands],
            out_specs=pl.BlockSpec((64, 256), lambda step, place, slots: (0, 0)),
            scratch_shapes=[pltpu.VMEM((512, 128), BF16)],
        ),
        out_shape=jax.ShapeDtypeStruct((64, 256), BF16),
        compiler_params=pltpu.CompilerParams(vmem_limit_bytes=VMEM_LIMIT),
    )(place, slot_ids, *[operand for operand, _ in operands])

    mixed = lax.all_to_all(mixed.reshape(cols, 4, 256), "col", 0, 0, tiled=True)
    mixed = call(scale_heads_kernel, jax.ShapeDtypeStruct((4, cols * 128), BF16), mixed)
    heads = lax.all_gather(mixed, "row", axis=0, tiled=False)
    heads = heads.reshape(rows // G, G, 4, cols, 128)
    mixer_out = jnp.einsum("qgtck,cgkd->qtd", heads, out_weights, preferred_element_type=F32)
    residual = lax.dynamic_slice(
        hidden.reshape(8, 64, 256), (0, 4 * col_index, 0), (8, 4, 256)
    ).astype(F32)
    after = (residual + mixer_out).astype(BF16).reshape(32, 256)
    all_after = lax.all_gather(after, "col", axis=0, tiled=False)
    all_after = all_after.reshape(cols, 8, 4, 256).transpose(1, 0, 2, 3).reshape(512, 256)
    after_wide = all_after.astype(F32)
    ffn_part = jnp.sum(after_wide * after_wide, axis=1)
    up_term = jnp.dot(
        (after_wide * norm_ffn[None, :]).astype(BF16), ffn_up, preferred_element_type=F32
    )
    up_term = jnp.concatenate([up_term, ffn_part[:, None]], axis=1).astype(BF16)
    up_sum = sum_parts(up_term.reshape(rows, -1, up_term.shape[1]), "row")
    up_share = up_sum[:, :-1] * lax.rsqrt(up_sum[:, -1:] / D + EPSILON)
    act_share = jnp.square(jax.nn.relu(up_share)).astype(BF16)
    act_all = spread(act_share, "row").reshape(512, -1)
    ffn_term = jnp.dot(act_all, ffn_down, preferred_element_type=F32).astype(BF16)
    ffn_out = sum_parts(ffn_term.reshape(cols, -1, ffn_term.shape[1]), "col")
    own_after = lax.dynamic_slice(all_after, (32 * col_index, 0), (32, 256))
    return (own_after.astype(F32) + ffn_out).astype(BF16)


def solution(mesh):
    return jax.shard_map(
        local,
        mesh=mesh,
        in_specs=(
            P("col", "row"),
            P("row"),
            P("row", None, "col", None),
            P("row", None, "col"),
            P("row", None, "col"),
            P(None, "col"),
            P(None, "col"),
            P(None, "col"),
            P(None, None, "col"),
            P(),
            P("row", None, None, "col"),
            P("row", None, None, None),
            P("row", None, "col", None, None),
            P(),
            P(),
            P(),
            P(None, "col"),
            P(None, "col", "row"),
            P("row"),
            P("row", "col"),
            P("col", "row"),
        ),
        out_specs=P("col", "row"),
        check_vma=False,
    )
```

```python
import functools

import jax
import jax.numpy as jnp
from jax import lax
from jax.experimental import pallas as pl
from jax.experimental.pallas import tpu as pltpu
from jax.sharding import PartitionSpec as P

D = 8192
H = 128
P_SIZE = 64
N = 256
G = 4

EPSILON = 1e-05
F32 = jnp.float32
BF16 = jnp.bfloat16
NT = (((1,), (1,)), ((), ()))
VMEM_LIMIT = 48 * 1024 * 1024


def exchange(parts, axis, groups=None):
    return lax.all_to_all(parts, axis, 0, 0, tiled=True, axis_index_groups=groups)


def call(kernel, out_shape, *operands):
    return pl.pallas_call(
        kernel,
        out_shape=out_shape,
        compiler_params=pltpu.CompilerParams(vmem_limit_bytes=VMEM_LIMIT),
    )(*operands)


def project_kernel(hidden_ref, gain_ref, main_ref, side_ref, out_ref):
    hidden = hidden_ref[...].astype(F32)
    normed = (hidden * gain_ref[...]).astype(BF16)
    squares = (hidden * hidden).astype(BF16)
    ones = jnp.ones((16, hidden.shape[1]), BF16)
    stat = lax.dot_general(ones, squares, NT, preferred_element_type=F32)
    for group in range(G):
        main = jnp.dot(
            normed, main_ref[:, group * 256 : (group + 1) * 256], preferred_element_type=F32
        ).astype(BF16)
        side = lax.dot_general(
            side_ref[group * 64 : (group + 1) * 64, :], normed, NT, preferred_element_type=F32
        )
        for request in range(8):
            nodes = slice(request * 64, (request + 1) * 64)
            out_ref[request, group, 0:64, :] = main[nodes, :]
            pieces = [side[0:16, nodes], side[16:32, nodes], side[32:48, nodes], stat[:, nodes]]
            out_ref[request, group, 64:80, :] = jnp.concatenate(pieces, axis=1).astype(BF16)


def column_of(row, size):
    eye = lax.broadcasted_iota(jnp.int32, (size, size), 0) == lax.broadcasted_iota(
        jnp.int32, (size, size), 1
    )
    wide = jnp.broadcast_to(row, (size, size))
    return jnp.sum(jnp.where(eye, wide, jnp.zeros_like(wide)), axis=1, keepdims=True)


def combine_kernel(parts_ref, bc_ref, local_ref):
    total = parts_ref[0].astype(F32)
    for part in range(1, parts_ref.shape[0]):
        total = total + parts_ref[part].astype(F32)
    scale = lax.rsqrt(total[64:65, 192:256] / D + EPSILON)
    bc = (total[64:80, 0:128] * jnp.concatenate([scale, scale], axis=1)).astype(BF16)
    for col in range(bc_ref.shape[0]):
        bc_ref[col] = bc
    main = total[0:64, :]
    main = jnp.concatenate(
        [main[:, 0:64], main[:, 128:192], main[:, 64:128], main[:, 192:256]], axis=1
    )
    local_ref[0:64, :] = main * column_of(scale, 64)
    step = total[64:72, 128:192] * scale
    local_ref[64:72, :] = jnp.concatenate([step] * 4, axis=1)


BASE, ANC, HOPS, SMALL, PACK = 512, 576, 640, 768, 784


def prepare_kernel(
    place_ref,
    slot_ref,
    x_hist_ref,
    bc_hist_ref,
    state_ref,
    x_taps_ref,
    bc_taps_ref,
    offset_ref,
    rate_ref,
    skip_ref,
    gain_ref,
    parents_ref,
    anc_ref,
    pack_ref,
    state_out_ref,
):
    request = place_ref[0]
    group = place_ref[1]

    def of_group(ref):
        table = ref[...]
        this = lax.broadcasted_iota(jnp.int32, table.shape, 0) == group
        return jnp.sum(jnp.where(this, table, 0.0), axis=0, keepdims=True)

    x_taps = jnp.zeros((4, 128), F32)
    bc_taps = jnp.zeros((4, 512), F32)
    for index in range(G):
        x_taps = jnp.where(group == index, x_taps_ref[:, index, :].astype(F32), x_taps)
        bc_taps = jnp.where(group == index, bc_taps_ref[:, index, :].astype(F32), bc_taps)

    lane = lax.broadcasted_iota(jnp.int32, (64, 64), 1)
    anc = anc_ref[0]
    anc_float = anc.astype(F32)
    depth_col = jnp.sum(anc, axis=1, keepdims=True) - 1
    depth_row = lax.dot_general(
        jnp.ones((8, 64), BF16), anc_float.astype(BF16), NT, preferred_element_type=F32
    )
    depth_row = depth_row[0:1, :].astype(jnp.int32) - 1
    all_parents = parents_ref[...]
    this = lax.broadcasted_iota(jnp.int32, all_parents.shape, 0) == request
    parent_row = jnp.sum(jnp.where(this, all_parents, 0), axis=0, keepdims=True)
    hop = (column_of(parent_row, 64) == lane).astype(F32)
    hops = [hop]
    for _ in range(2):
        moved = jnp.dot(
            hops[-1].astype(BF16), hop.astype(BF16), preferred_element_type=F32
        )
        hops.append(moved)
    pack_ref[HOPS : HOPS + 64, :] = jnp.concatenate(hops[0:2], axis=1)
    pack_ref[HOPS + 64 : HOPS + 128, :] = jnp.concatenate([hops[2], hops[2]], axis=1)
    pack_ref[ANC : ANC + 64, :] = jnp.concatenate([anc_float, anc_float], axis=1)

    x_hist = x_hist_ref[0, 0].astype(F32)
    x_base = jnp.zeros((64, 128), F32)
    rows = jnp.concatenate([bc_taps, bc_hist_ref[0, 0].astype(F32), jnp.zeros((9, 512), F32)], axis=0)
    square = (512, 512)
    eye = lax.broadcasted_iota(jnp.int32, square, 0) == lax.broadcasted_iota(jnp.int32, square, 1)
    turned = lax.dot_general(
        eye.astype(BF16), rows.astype(BF16), NT, preferred_element_type=F32
    )
    bc_base = jnp.zeros((512, 64), F32)
    for distance in range(1, 4):
        tap = 3 - distance
        for entry in range(3):
            use = (distance > depth_col) & (entry == tap + depth_col)
            x_base = x_base + jnp.where(
                use, x_hist[entry : entry + 1, :] * x_taps[tap : tap + 1, :], 0.0
            )
            use = (distance > depth_row) & (entry == tap + depth_row)
            share = turned[:, 4 + entry : 5 + entry] * turned[:, tap : tap + 1]
            bc_base = bc_base + jnp.where(use, share, 0.0)
    pack_ref[0:512, :] = jnp.concatenate([bc_base, turned, jnp.zeros((512, 48), F32)], axis=1)
    pack_ref[BASE : BASE + 64, :] = x_base

    first = lax.broadcasted_iota(jnp.int32, (1, 128), 1) < P_SIZE
    offset = column_of(of_group(offset_ref), 2)
    rate = column_of(-jnp.exp(of_group(rate_ref)), 2)
    skip = column_of(of_group(skip_ref), 2)
    pack_ref[SMALL : SMALL + 16, :] = jnp.concatenate(
        [
            x_taps,
            of_group(gain_ref),
            jnp.where(first, skip[0:1, :], skip[1:2, :]),
            jnp.zeros((2, 128), F32),
            jnp.broadcast_to(offset, (2, 128)),
            jnp.broadcast_to(rate, (2, 128)),
            jnp.zeros((4, 128), F32),
        ],
        axis=0,
    )
    state_out_ref[...] = state_ref[0, 0].reshape(2 * P_SIZE, N).astype(BF16)


def mixer_kernel(local_ref, bc_new_ref, pack_ref, state_ref, out_ref, bc_ref):
    for col in range(bc_new_ref.shape[0]):
        piece = bc_new_ref[col].astype(F32)
        bc_ref[col * 32 : col * 32 + 16, :] = piece[:, 0:64].astype(BF16)
        bc_ref[col * 32 + 16 : col * 32 + 32, :] = piece[:, 64:128].astype(BF16)
    hops = [
        pack_ref[HOPS : HOPS + 64, 0:64].astype(BF16),
        pack_ref[HOPS : HOPS + 64, 64:128].astype(BF16),
        pack_ref[HOPS + 64 : HOPS + 128, 0:64].astype(BF16),
    ]
    small = pack_ref[SMALL : SMALL + 16, :]

    x_new = local_ref[0:64, 0:128]
    gate = local_ref[0:64, 128:256]
    x_high = x_new.astype(BF16)
    x_low = (x_new - x_high.astype(F32)).astype(BF16)
    x_both = jnp.concatenate([x_high, x_low], axis=1)
    x_run = pack_ref[BASE : BASE + 64, :] + x_new * small[3:4, :]
    bc_run = pack_ref[0:512, 0:64] + bc_ref[...].astype(F32) * pack_ref[0:512, 67:68]
    for distance in range(1, 4):
        tap = 3 - distance
        moved = jnp.dot(hops[distance - 1], x_both, preferred_element_type=F32)
        x_run = x_run + (moved[:, 0:128] + moved[:, 128:256]) * small[tap : tap + 1, :]
        moved = lax.dot_general(bc_ref[...], hops[distance - 1], NT, preferred_element_type=F32)
        bc_run = bc_run + moved * pack_ref[0:512, 64 + tap : 65 + tap]
    x_conv = x_run * jax.nn.sigmoid(x_run)
    bc_conv = (bc_run * jax.nn.sigmoid(bc_run)).astype(BF16)

    raw = local_ref[64:66, 0:64] + small[8:10, 0:64]
    step = jnp.maximum(raw, 0.0) + jnp.log1p(jnp.exp(-jnp.abs(raw)))
    log_decay = small[10:12, 0:64] * step
    anc = pack_ref[ANC : ANC + 64, 0:64]
    cum = lax.dot_general(
        jnp.concatenate([log_decay, jnp.zeros((6, 64), F32)], axis=0),
        anc,
        NT,
        precision=lax.Precision.HIGHEST,
        preferred_element_type=F32,
    )

    square = (64, 64)
    eye = lax.broadcasted_iota(jnp.int32, square, 0) == lax.broadcasted_iota(jnp.int32, square, 1)
    c_node = lax.dot_general(
        eye.astype(BF16), bc_conv[256:512, :], NT, preferred_element_type=F32
    ).astype(BF16)
    scores = jnp.dot(c_node, bc_conv[0:256, :], preferred_element_type=F32)
    carried = lax.dot_general(c_node, state_ref[...], NT, preferred_element_type=F32)
    x_bf = x_conv.astype(BF16)
    is_anc = anc > 0.5
    inner = []
    start = []
    for head in range(2):
        cum_row = cum[head : head + 1, :]
        cum_col = column_of(cum_row, 64)
        gap = jnp.where(is_anc, cum_col - cum_row, 0.0)
        weight = jnp.where(is_anc, jnp.exp(gap), 0.0) * scores * step[head : head + 1, :]
        inner.append(jnp.dot(weight.astype(BF16), x_bf, preferred_element_type=F32))
        start.append(jnp.exp(cum_col))
    first = lax.broadcasted_iota(jnp.int32, (64, 128), 1) < P_SIZE
    mixed = (
        jnp.where(first, inner[0], inner[1])
        + jnp.where(first, start[0], start[1]) * carried
        + small[5:6, :] * x_conv
    )
    gated = mixed * (gate * jax.nn.sigmoid(gate))
    group_sq = jnp.sum(gated * gated, axis=1, keepdims=True)
    both = jnp.concatenate(
        [gated * small[4:5, :], jnp.broadcast_to(group_sq, (64, 128))], axis=1
    )
    for col in range(out_ref.shape[0]):
        out_ref[col] = both[col * 4 : col * 4 + 4, :].astype(BF16)


def scale_heads_kernel(parts_ref, out_ref):
    total = parts_ref[0, :, 128:256].astype(F32)
    for part in range(1, parts_ref.shape[0]):
        total = total + parts_ref[part, :, 128:256].astype(F32)
    scale = lax.rsqrt(total / (H // G * P_SIZE) + EPSILON)
    for part in range(parts_ref.shape[0]):
        piece = (parts_ref[part, :, 0:128].astype(F32) * scale).astype(BF16)
        for row in range(out_ref.shape[0]):
            out_ref[row, :, part * 128 : (part + 1) * 128] = piece


def out_kernel(heads_ref, weight_ref, residual_ref, out_ref, left_ref, sum_ref):
    group = pl.program_id(0)
    for request in range(8):
        left_ref[request * 4 : request * 4 + 4, :] = heads_ref[request * G + group].astype(F32)
    left = left_ref[...].astype(BF16)
    weight = weight_ref[...].reshape(-1, 256)
    term = jnp.dot(left, weight, preferred_element_type=F32)

    @pl.when(group == 0)
    def _():
        sum_ref[...] = residual_ref[...].astype(F32)

    sum_ref[...] += term

    @pl.when(group == G - 1)
    def _():
        after = sum_ref[...].astype(BF16)
        for col in range(out_ref.shape[0]):
            out_ref[col] = after


def up_kernel(flip, parity_ref, after_ref, gain_ref, weight_ref, out_ref):
    use = parity_ref[0] if not flip else 1 - parity_ref[0]
    after = after_ref[...].astype(F32)
    after = jnp.where(use == 0, after[:, 0:16, :], after[:, 16:32, :]).reshape(256, 256)
    normed = (after * gain_ref[...]).astype(BF16)
    stat = jnp.broadcast_to(jnp.sum(after * after, axis=1, keepdims=True), (256, 128))
    stat = stat.astype(BF16)
    for block in range(4):
        lanes = slice(block * 512, (block + 1) * 512)
        term = jnp.dot(normed, weight_ref[:, lanes], preferred_element_type=F32).astype(BF16)
        for part in range(16):
            out_ref[part, :, lanes] = term[part * 16 : (part + 1) * 16, :]
    for part in range(16):
        out_ref[part, :, 2048:2176] = stat[part * 16 : (part + 1) * 16, :]


def act_kernel(parts_ref, out_ref):
    stat = parts_ref[0, :, 2048:2176].astype(F32)
    for part in range(1, parts_ref.shape[0]):
        stat = stat + parts_ref[part, :, 2048:2176].astype(F32)
    scale = lax.rsqrt(stat / D + EPSILON)
    for block in range(16):
        lanes = slice(block * 128, (block + 1) * 128)
        up = parts_ref[0, :, lanes].astype(F32)
        for part in range(1, parts_ref.shape[0]):
            up = up + parts_ref[part, :, lanes].astype(F32)
        act = jnp.maximum(up * scale, 0.0)
        act = (act * act).astype(BF16)
        for part in range(out_ref.shape[0]):
            out_ref[part, :, lanes] = act


def down_half(act_ref, weight_ref, turn_ref):
    term = jnp.dot(act_ref[...].reshape(256, -1), weight_ref[...], preferred_element_type=F32)
    for col in range(16):
        for request in range(4):
            start = col * 16 + request * 4
            turn_ref[2 * request + col // 8, col % 8 * 4 : col % 8 * 4 + 4, :] = term[
                start : start + 4, :
            ]
    return turn_ref[...].astype(BF16)


def down_mine_kernel(act_ref, weight_ref, out_ref, turn_ref):
    out_ref[...] = down_half(act_ref, weight_ref, turn_ref)


def down_other_kernel(parity_ref, act_ref, weight_ref, mine_ref, out_ref, turn_ref):
    parity = parity_ref[0]
    out_ref[pl.ds(parity * 8, 8)] = mine_ref[...]
    out_ref[pl.ds(8 - parity * 8, 8)] = down_half(act_ref, weight_ref, turn_ref)


def local(
    hidden_in,
    norm_mixer,
    mixer_in,
    bc_proj,
    dt_proj,
    dt_bias,
    a_log,
    skip_d,
    conv_x,
    conv_bc,
    x_cache,
    bc_cache,
    ssm_cache,
    slot_ids,
    parents,
    ancestors,
    norm_gated,
    out_proj,
    norm_ffn,
    ffn_up,
    ffn_down,
):
    rows = lax.axis_size("row")
    cols = lax.axis_size("col")
    row_index = lax.axis_index("row")
    col_index = lax.axis_index("col")
    place = jnp.stack([row_index // G, row_index % G]).astype(jnp.int32)
    parity = (row_index % 2).astype(jnp.int32)[None]
    swap = [(row, row ^ 1) for row in range(rows)]
    halves = [[row for row in range(rows) if row % 2 == half] for half in range(2)]
    smem = pl.BlockSpec(memory_space=pltpu.SMEM)
    vmem = pl.BlockSpec(memory_space=pltpu.VMEM)
    params = pltpu.CompilerParams(vmem_limit_bytes=VMEM_LIMIT)

    out_weights = lax.all_gather(out_proj, "col", axis=0, tiled=False)

    hidden = exchange(jnp.broadcast_to(hidden_in[None], (cols,) + hidden_in.shape), "col")
    side = jnp.concatenate([bc_proj, dt_proj, jnp.zeros((256, G, 30), BF16)], axis=2)
    parts = call(
        project_kernel,
        jax.ShapeDtypeStruct((rows // G, G, 80, 256), BF16),
        hidden.reshape(512, 256),
        norm_mixer[None, :],
        mixer_in.reshape(256, -1),
        side.reshape(256, 256).T,
    )
    parts = exchange(parts.reshape(rows, 80, 256), "row")

    def whole(array):
        shape = array.shape
        return pl.BlockSpec(shape, lambda step, place, slots: (0,) * len(shape))

    def slot_block(*shape):
        zeros = (0,) * (len(shape) - 2)
        return pl.BlockSpec(shape, lambda step, place, slots: (0, slots[place[0]]) + zeros)

    operands = [
        (x_cache, slot_block(1, 1, 3, 128)),
        (bc_cache, slot_block(1, 1, 3, 512)),
        (ssm_cache, slot_block(1, 1, 2, P_SIZE, N)),
        (conv_x, whole(conv_x)),
        (conv_bc, whole(conv_bc)),
        (dt_bias, whole(dt_bias)),
        (a_log, whole(a_log)),
        (skip_d, whole(skip_d)),
        (norm_gated, whole(norm_gated)),
        (parents, whole(parents)),
        (ancestors, pl.BlockSpec((1, 64, 64), lambda step, place, slots: (place[0], 0, 0))),
    ]
    pack, state = pl.pallas_call(
        prepare_kernel,
        grid_spec=pltpu.PrefetchScalarGridSpec(
            num_scalar_prefetch=2,
            grid=(1,),
            in_specs=[spec for _, spec in operands],
            out_specs=[
                pl.BlockSpec((PACK, 128), lambda step, place, slots: (0, 0)),
                pl.BlockSpec((2 * P_SIZE, N), lambda step, place, slots: (0, 0)),
            ],
        ),
        out_shape=[
            jax.ShapeDtypeStruct((PACK, 128), F32),
            jax.ShapeDtypeStruct((2 * P_SIZE, N), BF16),
        ],
        compiler_params=params,
    )(place, slot_ids, *[operand for operand, _ in operands])

    bc_own, local_sums = call(
        combine_kernel,
        (jax.ShapeDtypeStruct((cols, 16, 128), BF16), jax.ShapeDtypeStruct((72, 256), F32)),
        parts,
    )
    bc_new = exchange(bc_own, "col")
    mixed = pl.pallas_call(
        mixer_kernel,
        out_shape=jax.ShapeDtypeStruct((cols, 4, 256), BF16),
        scratch_shapes=[pltpu.VMEM((512, 64), BF16)],
        compiler_params=params,
    )(local_sums, bc_new, pack, state)

    mixed = exchange(mixed, "col")
    heads = call(
        scale_heads_kernel, jax.ShapeDtypeStruct((rows, 4, cols * 128), BF16), mixed
    )
    heads = exchange(heads, "row")
    residual = lax.dynamic_slice(
        hidden.reshape(8, 64, 256), (0, 4 * col_index, 0), (8, 4, 256)
    ).reshape(32, 256)
    after = pl.pallas_call(
        out_kernel,
        grid=(G,),
        out_shape=jax.ShapeDtypeStruct((cols, 32, 256), BF16),
        in_specs=[
            pl.BlockSpec(heads.shape, lambda group: (0, 0, 0)),
            pl.BlockSpec((cols, 1, 128, 256), lambda group: (0, group, 0, 0)),
            pl.BlockSpec((32, 256), lambda group: (0, 0)),
        ],
        out_specs=pl.BlockSpec((cols, 32, 256), lambda group: (0, 0, 0)),
        scratch_shapes=[pltpu.VMEM((32, 2048), F32), pltpu.VMEM((32, 256), F32)],
        compiler_params=params,
    )(heads, out_weights, residual)
    after = exchange(after, "col")

    def up_half(flip):
        return pl.pallas_call(
            functools.partial(up_kernel, flip),
            out_shape=jax.ShapeDtypeStruct((16, 16, 2176), BF16),
            in_specs=[smem, vmem, vmem, vmem],
            out_specs=vmem,
            compiler_params=params,
        )(parity, after, norm_ffn[None, :], ffn_up)

    up_other = lax.ppermute(up_half(True), "row", swap)
    up_sum = (up_half(False).astype(F32) + up_other.astype(F32)).astype(BF16)
    up_parts = exchange(up_sum, "row", halves)
    act = call(act_kernel, jax.ShapeDtypeStruct((16, 16, 2048), BF16), up_parts)
    act_mine = exchange(act, "row", halves)
    act_other = lax.ppermute(act_mine, "row", swap)
    turn = [pltpu.VMEM((8, 32, 256), F32)]
    down_mine = pl.pallas_call(
        down_mine_kernel,
        out_shape=jax.ShapeDtypeStruct((8, 32, 256), BF16),
        scratch_shapes=turn,
        compiler_params=params,
    )(act_mine, ffn_down)
    down = pl.pallas_call(
        down_other_kernel,
        out_shape=jax.ShapeDtypeStruct((cols, 32, 256), BF16),
        in_specs=[smem, vmem, vmem, vmem],
        out_specs=vmem,
        scratch_shapes=turn,
        compiler_params=params,
    )(parity, act_other, ffn_down, down_mine)
    ffn_out = jnp.sum(exchange(down, "col").astype(F32), axis=0)
    own_after = lax.dynamic_slice(
        after, (8 * (col_index % 2), 4 * (col_index // 2), 0), (8, 4, 256)
    ).reshape(32, 256)
    return (own_after.astype(F32) + ffn_out).astype(BF16)


def solution(mesh):
    return jax.shard_map(
        local,
        mesh=mesh,
        in_specs=(
            P("col", "row"),
            P("row"),
            P("row", None, "col", None),
            P("row", None, "col"),
            P("row", None, "col"),
            P(None, "col"),
            P(None, "col"),
            P(None, "col"),
            P(None, None, "col"),
            P(),
            P("row", None, None, "col"),
            P("row", None, None, None),
            P("row", None, "col", None, None),
            P(),
            P(),
            P(),
            P(None, "col"),
            P(None, "col", "row"),
            P("row"),
            P("row", "col"),
            P("col", "row"),
        ),
        out_specs=P("col", "row"),
        check_vma=False,
    )
```

```python
import functools

import jax
import jax.numpy as jnp
from jax import lax
from jax.experimental import pallas as pl
from jax.experimental.pallas import tpu as pltpu
from jax.sharding import PartitionSpec as P

D = 8192
H = 128
P_SIZE = 64
N = 256
G = 4

EPSILON = 1e-05
F32 = jnp.float32
BF16 = jnp.bfloat16
NT = (((1,), (1,)), ((), ()))
VMEM_LIMIT = 48 * 1024 * 1024


def exchange(parts, axis, groups=None):
    return lax.all_to_all(parts, axis, 0, 0, tiled=True, axis_index_groups=groups)


def call(kernel, out_shape, *operands):
    return pl.pallas_call(
        kernel,
        out_shape=out_shape,
        compiler_params=pltpu.CompilerParams(vmem_limit_bytes=VMEM_LIMIT),
    )(*operands)


def copies_kernel(block_ref, out_ref):
    for part in range(out_ref.shape[0]):
        out_ref[part] = block_ref[...]


def project_kernel(flip, parity_ref, hidden_ref, gain_ref, main_ref, side_ref, out_ref):
    use = parity_ref[0] if not flip else 1 - parity_ref[0]
    hidden = hidden_ref[...].astype(F32)
    normed = (hidden * gain_ref[...]).astype(BF16)
    squares = (hidden * hidden).astype(BF16)
    ones = jnp.ones((16, hidden.shape[1]), BF16)
    stat = lax.dot_general(ones, squares, NT, preferred_element_type=F32)
    for half in range(G // 2):
        group = 2 * half + use
        main = main_ref[:, pl.ds(pl.multiple_of(group * 256, 256), 256)]
        main = jnp.dot(normed, main, preferred_element_type=F32).astype(BF16)
        side = side_ref[pl.ds(pl.multiple_of(group * 64, 64), 64), :]
        side = lax.dot_general(side, normed, NT, preferred_element_type=F32)
        for request in range(8):
            part = request * (G // 2) + half
            nodes = slice(request * 64, (request + 1) * 64)
            out_ref[part, 0:64, :] = main[nodes, :]
            pieces = [side[0:16, nodes], side[16:32, nodes], side[32:48, nodes], stat[:, nodes]]
            out_ref[part, 64:80, :] = jnp.concatenate(pieces, axis=1).astype(BF16)


def column_of(row, size):
    eye = lax.broadcasted_iota(jnp.int32, (size, size), 0) == lax.broadcasted_iota(
        jnp.int32, (size, size), 1
    )
    wide = jnp.broadcast_to(row, (size, size))
    return jnp.sum(jnp.where(eye, wide, jnp.zeros_like(wide)), axis=1, keepdims=True)


def combine_kernel(parts_ref, bc_ref, local_ref):
    total = parts_ref[0].astype(F32)
    for part in range(1, parts_ref.shape[0]):
        total = total + parts_ref[part].astype(F32)
    scale = lax.rsqrt(total[64:65, 192:256] / D + EPSILON)
    bc = (total[64:80, 0:128] * jnp.concatenate([scale, scale], axis=1)).astype(BF16)
    for col in range(bc_ref.shape[0]):
        bc_ref[col] = bc
    main = total[0:64, :]
    main = jnp.concatenate(
        [main[:, 0:64], main[:, 128:192], main[:, 64:128], main[:, 192:256]], axis=1
    )
    local_ref[0:64, :] = main * column_of(scale, 64)
    step = total[64:72, 128:192] * scale
    local_ref[64:72, :] = jnp.concatenate([step] * 4, axis=1)


BASE, ANC, HOPS, SMALL, PACK = 512, 576, 640, 768, 784


def prepare_kernel(
    place_ref,
    slot_ref,
    x_hist_ref,
    bc_hist_ref,
    state_ref,
    x_taps_ref,
    bc_taps_ref,
    offset_ref,
    rate_ref,
    skip_ref,
    gain_ref,
    parents_ref,
    anc_ref,
    pack_ref,
    state_out_ref,
):
    request = place_ref[0]
    group = place_ref[1]

    def of_group(ref):
        table = ref[...]
        this = lax.broadcasted_iota(jnp.int32, table.shape, 0) == group
        return jnp.sum(jnp.where(this, table, 0.0), axis=0, keepdims=True)

    x_taps = jnp.zeros((4, 128), F32)
    bc_taps = jnp.zeros((4, 512), F32)
    for index in range(G):
        x_taps = jnp.where(group == index, x_taps_ref[:, index, :].astype(F32), x_taps)
        bc_taps = jnp.where(group == index, bc_taps_ref[:, index, :].astype(F32), bc_taps)

    lane = lax.broadcasted_iota(jnp.int32, (64, 64), 1)
    anc = anc_ref[0]
    anc_float = anc.astype(F32)
    depth_col = jnp.sum(anc, axis=1, keepdims=True) - 1
    depth_row = lax.dot_general(
        jnp.ones((8, 64), BF16), anc_float.astype(BF16), NT, preferred_element_type=F32
    )
    depth_row = depth_row[0:1, :].astype(jnp.int32) - 1
    all_parents = parents_ref[...]
    this = lax.broadcasted_iota(jnp.int32, all_parents.shape, 0) == request
    parent_row = jnp.sum(jnp.where(this, all_parents, 0), axis=0, keepdims=True)
    hop = (column_of(parent_row, 64) == lane).astype(F32)
    hops = [hop]
    for _ in range(2):
        moved = jnp.dot(
            hops[-1].astype(BF16), hop.astype(BF16), preferred_element_type=F32
        )
        hops.append(moved)
    pack_ref[HOPS : HOPS + 64, :] = jnp.concatenate(hops[0:2], axis=1)
    pack_ref[HOPS + 64 : HOPS + 128, :] = jnp.concatenate([hops[2], hops[2]], axis=1)
    pack_ref[ANC : ANC + 64, :] = jnp.concatenate([anc_float, anc_float], axis=1)

    x_hist = x_hist_ref[0, 0].astype(F32)
    x_base = jnp.zeros((64, 128), F32)
    rows = jnp.concatenate([bc_taps, bc_hist_ref[0, 0].astype(F32), jnp.zeros((9, 512), F32)], axis=0)
    square = (512, 512)
    eye = lax.broadcasted_iota(jnp.int32, square, 0) == lax.broadcasted_iota(jnp.int32, square, 1)
    turned = lax.dot_general(
        eye.astype(BF16), rows.astype(BF16), NT, preferred_element_type=F32
    )
    bc_base = jnp.zeros((512, 64), F32)
    for distance in range(1, 4):
        tap = 3 - distance
        for entry in range(3):
            use = (distance > depth_col) & (entry == tap + depth_col)
            x_base = x_base + jnp.where(
                use, x_hist[entry : entry + 1, :] * x_taps[tap : tap + 1, :], 0.0
            )
            use = (distance > depth_row) & (entry == tap + depth_row)
            share = turned[:, 4 + entry : 5 + entry] * turned[:, tap : tap + 1]
            bc_base = bc_base + jnp.where(use, share, 0.0)
    pack_ref[0:512, :] = jnp.concatenate([bc_base, turned, jnp.zeros((512, 48), F32)], axis=1)
    pack_ref[BASE : BASE + 64, :] = x_base

    first = lax.broadcasted_iota(jnp.int32, (1, 128), 1) < P_SIZE
    offset = column_of(of_group(offset_ref), 2)
    rate = column_of(-jnp.exp(of_group(rate_ref)), 2)
    skip = column_of(of_group(skip_ref), 2)
    pack_ref[SMALL : SMALL + 16, :] = jnp.concatenate(
        [
            x_taps,
            of_group(gain_ref),
            jnp.where(first, skip[0:1, :], skip[1:2, :]),
            jnp.zeros((2, 128), F32),
            jnp.broadcast_to(offset, (2, 128)),
            jnp.broadcast_to(rate, (2, 128)),
            jnp.zeros((4, 128), F32),
        ],
        axis=0,
    )
    state_out_ref[...] = state_ref[0, 0].reshape(2 * P_SIZE, N).astype(BF16)


def mixer_kernel(local_ref, bc_new_ref, pack_ref, state_ref, out_ref, bc_ref):
    for col in range(bc_new_ref.shape[0]):
        piece = bc_new_ref[col].astype(F32)
        bc_ref[col * 32 : col * 32 + 16, :] = piece[:, 0:64].astype(BF16)
        bc_ref[col * 32 + 16 : col * 32 + 32, :] = piece[:, 64:128].astype(BF16)
    hops = [
        pack_ref[HOPS : HOPS + 64, 0:64].astype(BF16),
        pack_ref[HOPS : HOPS + 64, 64:128].astype(BF16),
        pack_ref[HOPS + 64 : HOPS + 128, 0:64].astype(BF16),
    ]
    small = pack_ref[SMALL : SMALL + 16, :]

    x_new = local_ref[0:64, 0:128]
    gate = local_ref[0:64, 128:256]
    x_high = x_new.astype(BF16)
    x_low = (x_new - x_high.astype(F32)).astype(BF16)
    x_both = jnp.concatenate([x_high, x_low], axis=1)
    x_run = pack_ref[BASE : BASE + 64, :] + x_new * small[3:4, :]
    bc_run = pack_ref[0:512, 0:64] + bc_ref[...].astype(F32) * pack_ref[0:512, 67:68]
    for distance in range(1, 4):
        tap = 3 - distance
        moved = jnp.dot(hops[distance - 1], x_both, preferred_element_type=F32)
        x_run = x_run + (moved[:, 0:128] + moved[:, 128:256]) * small[tap : tap + 1, :]
        moved = lax.dot_general(bc_ref[...], hops[distance - 1], NT, preferred_element_type=F32)
        bc_run = bc_run + moved * pack_ref[0:512, 64 + tap : 65 + tap]
    x_conv = x_run * jax.nn.sigmoid(x_run)
    bc_conv = (bc_run * jax.nn.sigmoid(bc_run)).astype(BF16)

    raw = local_ref[64:66, 0:64] + small[8:10, 0:64]
    step = jnp.maximum(raw, 0.0) + jnp.log1p(jnp.exp(-jnp.abs(raw)))
    log_decay = small[10:12, 0:64] * step
    anc = pack_ref[ANC : ANC + 64, 0:64]
    cum = lax.dot_general(
        jnp.concatenate([log_decay, jnp.zeros((6, 64), F32)], axis=0),
        anc,
        NT,
        precision=lax.Precision.HIGHEST,
        preferred_element_type=F32,
    )

    square = (64, 64)
    eye = lax.broadcasted_iota(jnp.int32, square, 0) == lax.broadcasted_iota(jnp.int32, square, 1)
    c_node = lax.dot_general(
        eye.astype(BF16), bc_conv[256:512, :], NT, preferred_element_type=F32
    ).astype(BF16)
    scores = jnp.dot(c_node, bc_conv[0:256, :], preferred_element_type=F32)
    carried = lax.dot_general(c_node, state_ref[...], NT, preferred_element_type=F32)
    x_bf = x_conv.astype(BF16)
    is_anc = anc > 0.5
    inner = []
    start = []
    for head in range(2):
        cum_row = cum[head : head + 1, :]
        cum_col = column_of(cum_row, 64)
        gap = jnp.where(is_anc, cum_col - cum_row, 0.0)
        weight = jnp.where(is_anc, jnp.exp(gap), 0.0) * scores * step[head : head + 1, :]
        inner.append(jnp.dot(weight.astype(BF16), x_bf, preferred_element_type=F32))
        start.append(jnp.exp(cum_col))
    first = lax.broadcasted_iota(jnp.int32, (64, 128), 1) < P_SIZE
    mixed = (
        jnp.where(first, inner[0], inner[1])
        + jnp.where(first, start[0], start[1]) * carried
        + small[5:6, :] * x_conv
    )
    gated = mixed * (gate * jax.nn.sigmoid(gate))
    group_sq = jnp.sum(gated * gated, axis=1, keepdims=True)
    both = jnp.concatenate(
        [gated * small[4:5, :], jnp.broadcast_to(group_sq, (64, 128))], axis=1
    )
    for col in range(out_ref.shape[0]):
        out_ref[col] = both[col * 4 : col * 4 + 4, :].astype(BF16)


def scale_heads_kernel(parts_ref, out_ref):
    total = parts_ref[0, :, 128:256].astype(F32)
    for part in range(1, parts_ref.shape[0]):
        total = total + parts_ref[part, :, 128:256].astype(F32)
    scale = lax.rsqrt(total / (H // G * P_SIZE) + EPSILON)
    for part in range(parts_ref.shape[0]):
        piece = (parts_ref[part, :, 0:128].astype(F32) * scale).astype(BF16)
        for row in range(out_ref.shape[0]):
            out_ref[row, :, part * 128 : (part + 1) * 128] = piece


def out_kernel(heads_ref, weight_ref, residual_ref, out_ref, left_ref, sum_ref):
    group = pl.program_id(0)
    for request in range(8):
        left_ref[request * 4 : request * 4 + 4, :] = heads_ref[request * G + group].astype(F32)
    left = left_ref[...].astype(BF16)
    weight = weight_ref[...].reshape(-1, 256)
    term = jnp.dot(left, weight, preferred_element_type=F32)

    @pl.when(group == 0)
    def _():
        sum_ref[...] = residual_ref[...].astype(F32)

    sum_ref[...] += term

    @pl.when(group == G - 1)
    def _():
        after = sum_ref[...].astype(BF16)
        for col in range(out_ref.shape[0]):
            out_ref[col] = after


def up_kernel(flip, parity_ref, after_ref, gain_ref, weight_ref, out_ref):
    use = parity_ref[0] if not flip else 1 - parity_ref[0]
    after = after_ref[...].astype(F32)
    after = jnp.where(use == 0, after[:, 0:16, :], after[:, 16:32, :]).reshape(256, 256)
    normed = (after * gain_ref[...]).astype(BF16)
    stat = jnp.broadcast_to(jnp.sum(after * after, axis=1, keepdims=True), (256, 128))
    stat = stat.astype(BF16)
    for block in range(4):
        lanes = slice(block * 512, (block + 1) * 512)
        term = jnp.dot(normed, weight_ref[:, lanes], preferred_element_type=F32).astype(BF16)
        for part in range(16):
            out_ref[part, :, lanes] = term[part * 16 : (part + 1) * 16, :]
    for part in range(16):
        out_ref[part, :, 2048:2176] = stat[part * 16 : (part + 1) * 16, :]


def act_kernel(parts_ref, out_ref):
    stat = parts_ref[0, :, 2048:2176].astype(F32)
    for part in range(1, parts_ref.shape[0]):
        stat = stat + parts_ref[part, :, 2048:2176].astype(F32)
    scale = lax.rsqrt(stat / D + EPSILON)
    for block in range(16):
        lanes = slice(block * 128, (block + 1) * 128)
        up = parts_ref[0, :, lanes].astype(F32)
        for part in range(1, parts_ref.shape[0]):
            up = up + parts_ref[part, :, lanes].astype(F32)
        act = jnp.maximum(up * scale, 0.0)
        act = (act * act).astype(BF16)
        for part in range(out_ref.shape[0]):
            out_ref[part, :, lanes] = act


def down_half(act_ref, weight_ref, turn_ref):
    term = jnp.dot(act_ref[...].reshape(256, -1), weight_ref[...], preferred_element_type=F32)
    for col in range(16):
        for request in range(4):
            start = col * 16 + request * 4
            turn_ref[2 * request + col // 8, col % 8 * 4 : col % 8 * 4 + 4, :] = term[
                start : start + 4, :
            ]
    return turn_ref[...].astype(BF16)


def down_mine_kernel(act_ref, weight_ref, out_ref, turn_ref):
    out_ref[...] = down_half(act_ref, weight_ref, turn_ref)


def down_other_kernel(parity_ref, act_ref, weight_ref, mine_ref, out_ref, turn_ref):
    parity = parity_ref[0]
    out_ref[pl.ds(parity * 8, 8)] = mine_ref[...]
    out_ref[pl.ds(8 - parity * 8, 8)] = down_half(act_ref, weight_ref, turn_ref)


def local(
    hidden_in,
    norm_mixer,
    mixer_in,
    bc_proj,
    dt_proj,
    dt_bias,
    a_log,
    skip_d,
    conv_x,
    conv_bc,
    x_cache,
    bc_cache,
    ssm_cache,
    slot_ids,
    parents,
    ancestors,
    norm_gated,
    out_proj,
    norm_ffn,
    ffn_up,
    ffn_down,
):
    rows = lax.axis_size("row")
    cols = lax.axis_size("col")
    row_index = lax.axis_index("row")
    col_index = lax.axis_index("col")
    place = jnp.stack([row_index // G, row_index % G]).astype(jnp.int32)
    parity = (row_index % 2).astype(jnp.int32)[None]
    swap = [(row, row ^ 1) for row in range(rows)]
    halves = [[row for row in range(rows) if row % 2 == half] for half in range(2)]
    smem = pl.BlockSpec(memory_space=pltpu.SMEM)
    vmem = pl.BlockSpec(memory_space=pltpu.VMEM)
    params = pltpu.CompilerParams(vmem_limit_bytes=VMEM_LIMIT)

    out_weights = lax.all_gather(out_proj, "col", axis=0, tiled=False)

    copies = call(copies_kernel, jax.ShapeDtypeStruct((cols, 32, 256), BF16), hidden_in)
    hidden = exchange(copies, "col")
    side = jnp.concatenate([bc_proj, dt_proj, jnp.zeros((256, G, 30), BF16)], axis=2)
    side = side.reshape(256, 256).T
    main = mixer_in.reshape(256, -1)

    def pair_sum(half):
        other = lax.ppermute(half(True), "row", swap)
        return (half(False).astype(F32) + other.astype(F32)).astype(BF16)

    def project_half(flip):
        return pl.pallas_call(
            functools.partial(project_kernel, flip),
            out_shape=jax.ShapeDtypeStruct((16, 80, 256), BF16),
            in_specs=[smem, vmem, vmem, vmem, vmem],
            out_specs=vmem,
            compiler_params=params,
        )(parity, hidden.reshape(512, 256), norm_mixer[None, :], main, side)

    parts = exchange(pair_sum(project_half), "row", halves)

    bc_own, local_sums = call(
        combine_kernel,
        (jax.ShapeDtypeStruct((cols, 16, 128), BF16), jax.ShapeDtypeStruct((72, 256), F32)),
        parts,
    )
    bc_own, place = lax.optimization_barrier((bc_own, place))

    def whole(array):
        shape = array.shape
        return pl.BlockSpec(shape, lambda step, place, slots: (0,) * len(shape))

    def slot_block(*shape):
        zeros = (0,) * (len(shape) - 2)
        return pl.BlockSpec(shape, lambda step, place, slots: (0, slots[place[0]]) + zeros)

    operands = [
        (x_cache, slot_block(1, 1, 3, 128)),
        (bc_cache, slot_block(1, 1, 3, 512)),
        (ssm_cache, slot_block(1, 1, 2, P_SIZE, N)),
        (conv_x, whole(conv_x)),
        (conv_bc, whole(conv_bc)),
        (dt_bias, whole(dt_bias)),
        (a_log, whole(a_log)),
        (skip_d, whole(skip_d)),
        (norm_gated, whole(norm_gated)),
        (parents, whole(parents)),
        (ancestors, pl.BlockSpec((1, 64, 64), lambda step, place, slots: (place[0], 0, 0))),
    ]
    pack, state = pl.pallas_call(
        prepare_kernel,
        grid_spec=pltpu.PrefetchScalarGridSpec(
            num_scalar_prefetch=2,
            grid=(1,),
            in_specs=[spec for _, spec in operands],
            out_specs=[
                pl.BlockSpec((PACK, 128), lambda step, place, slots: (0, 0)),
                pl.BlockSpec((2 * P_SIZE, N), lambda step, place, slots: (0, 0)),
            ],
        ),
        out_shape=[
            jax.ShapeDtypeStruct((PACK, 128), F32),
            jax.ShapeDtypeStruct((2 * P_SIZE, N), BF16),
        ],
        compiler_params=params,
    )(place, slot_ids, *[operand for operand, _ in operands])

    bc_new = exchange(bc_own, "col")
    mixed = pl.pallas_call(
        mixer_kernel,
        out_shape=jax.ShapeDtypeStruct((cols, 4, 256), BF16),
        scratch_shapes=[pltpu.VMEM((512, 64), BF16)],
        compiler_params=params,
    )(local_sums, bc_new, pack, state)

    mixed = exchange(mixed, "col")
    heads = call(
        scale_heads_kernel, jax.ShapeDtypeStruct((rows, 4, cols * 128), BF16), mixed
    )
    heads = exchange(heads, "row")
    residual = lax.dynamic_slice(
        hidden.reshape(8, 64, 256), (0, 4 * col_index, 0), (8, 4, 256)
    ).reshape(32, 256)
    after = pl.pallas_call(
        out_kernel,
        grid=(G,),
        out_shape=jax.ShapeDtypeStruct((cols, 32, 256), BF16),
        in_specs=[
            pl.BlockSpec(heads.shape, lambda group: (0, 0, 0)),
            pl.BlockSpec((cols, 1, 128, 256), lambda group: (0, group, 0, 0)),
            pl.BlockSpec((32, 256), lambda group: (0, 0)),
        ],
        out_specs=pl.BlockSpec((cols, 32, 256), lambda group: (0, 0, 0)),
        scratch_shapes=[pltpu.VMEM((32, 2048), F32), pltpu.VMEM((32, 256), F32)],
        compiler_params=pltpu.CompilerParams(vmem_limit_bytes=60 * 1024 * 1024),
    )(heads, out_weights, residual)
    after = exchange(after, "col")

    def up_half(flip):
        return pl.pallas_call(
            functools.partial(up_kernel, flip),
            out_shape=jax.ShapeDtypeStruct((16, 16, 2176), BF16),
            in_specs=[smem, vmem, vmem, vmem],
            out_specs=vmem,
            compiler_params=params,
        )(parity, after, norm_ffn[None, :], ffn_up)

    up_parts = exchange(pair_sum(up_half), "row", halves)
    act = call(act_kernel, jax.ShapeDtypeStruct((16, 16, 2048), BF16), up_parts)
    act_mine = exchange(act, "row", halves)
    act_other = lax.ppermute(act_mine, "row", swap)
    turn = [pltpu.VMEM((8, 32, 256), F32)]
    down_mine = pl.pallas_call(
        down_mine_kernel,
        out_shape=jax.ShapeDtypeStruct((8, 32, 256), BF16),
        scratch_shapes=turn,
        compiler_params=params,
    )(act_mine, ffn_down)
    down = pl.pallas_call(
        down_other_kernel,
        out_shape=jax.ShapeDtypeStruct((cols, 32, 256), BF16),
        in_specs=[smem, vmem, vmem, vmem],
        out_specs=vmem,
        scratch_shapes=turn,
        compiler_params=params,
    )(parity, act_other, ffn_down, down_mine)
    ffn_out = jnp.sum(exchange(down, "col").astype(F32), axis=0)
    own_after = lax.dynamic_slice(
        after, (8 * (col_index % 2), 4 * (col_index // 2), 0), (8, 4, 256)
    ).reshape(32, 256)
    return (own_after.astype(F32) + ffn_out).astype(BF16)


def solution(mesh):
    return jax.shard_map(
        local,
        mesh=mesh,
        in_specs=(
            P("col", "row"),
            P("row"),
            P("row", None, "col", None),
            P("row", None, "col"),
            P("row", None, "col"),
            P(None, "col"),
            P(None, "col"),
            P(None, "col"),
            P(None, None, "col"),
            P(),
            P("row", None, None, "col"),
            P("row", None, None, None),
            P("row", None, "col", None, None),
            P(),
            P(),
            P(),
            P(None, "col"),
            P(None, "col", "row"),
            P("row"),
            P("row", "col"),
            P("col", "row"),
        ),
        out_specs=P("col", "row"),
        check_vma=False,
    )
```

```python
import functools

import jax
import jax.numpy as jnp
from jax import lax
from jax.experimental import pallas as pl
from jax.experimental.pallas import tpu as pltpu
from jax.sharding import PartitionSpec as P

D = 8192
H = 128
P_SIZE = 64
N = 256
G = 4

EPSILON = 1e-05
F32 = jnp.float32
BF16 = jnp.bfloat16
NT = (((1,), (1,)), ((), ()))
VMEM_LIMIT = 48 * 1024 * 1024


def exchange(parts, axis, groups=None):
    return lax.all_to_all(parts, axis, 0, 0, tiled=True, axis_index_groups=groups)


def call(kernel, out_shape, *operands):
    return pl.pallas_call(
        kernel,
        out_shape=out_shape,
        compiler_params=pltpu.CompilerParams(vmem_limit_bytes=VMEM_LIMIT),
    )(*operands)


def copies_kernel(block_ref, out_ref):
    for part in range(out_ref.shape[0]):
        out_ref[part] = block_ref[...]


def project_kernel(flip, parity_ref, hidden_ref, gain_ref, main_ref, side_ref, out_ref):
    use = parity_ref[0] if not flip else 1 - parity_ref[0]
    hidden = hidden_ref[...].astype(F32)
    normed = (hidden * gain_ref[...]).astype(BF16)
    squares = (hidden * hidden).astype(BF16)
    ones = jnp.ones((16, hidden.shape[1]), BF16)
    stat = lax.dot_general(ones, squares, NT, preferred_element_type=F32)
    for half in range(G // 2):
        group = 2 * half + use
        main = main_ref[:, pl.ds(pl.multiple_of(group * 256, 256), 256)]
        main = jnp.dot(normed, main, preferred_element_type=F32).astype(BF16)
        side = side_ref[pl.ds(pl.multiple_of(group * 64, 64), 64), :]
        side = lax.dot_general(side, normed, NT, preferred_element_type=F32)
        for request in range(8):
            part = request * (G // 2) + half
            nodes = slice(request * 64, (request + 1) * 64)
            out_ref[part, 0:64, :] = main[nodes, :]
            pieces = [side[0:16, nodes], side[16:32, nodes], side[32:48, nodes], stat[:, nodes]]
            out_ref[part, 64:80, :] = jnp.concatenate(pieces, axis=1).astype(BF16)


def column_of(row, size):
    eye = lax.broadcasted_iota(jnp.int32, (size, size), 0) == lax.broadcasted_iota(
        jnp.int32, (size, size), 1
    )
    wide = jnp.broadcast_to(row, (size, size))
    return jnp.sum(jnp.where(eye, wide, jnp.zeros_like(wide)), axis=1, keepdims=True)


def combine_kernel(parts_ref, bc_ref, local_ref):
    total = parts_ref[0].astype(F32)
    for part in range(1, parts_ref.shape[0]):
        total = total + parts_ref[part].astype(F32)
    scale = lax.rsqrt(total[64:65, 192:256] / D + EPSILON)
    bc = (total[64:80, 0:128] * jnp.concatenate([scale, scale], axis=1)).astype(BF16)
    for col in range(bc_ref.shape[0]):
        bc_ref[col] = bc
    main = total[0:64, :]
    main = jnp.concatenate(
        [main[:, 0:64], main[:, 128:192], main[:, 64:128], main[:, 192:256]], axis=1
    )
    local_ref[0:64, :] = main * column_of(scale, 64)
    step = total[64:72, 128:192] * scale
    local_ref[64:72, :] = jnp.concatenate([step] * 4, axis=1)


BASE, ANC, HOPS, SMALL, PACK = 512, 576, 640, 768, 784


def prepare_kernel(
    place_ref,
    slot_ref,
    x_hist_ref,
    bc_hist_ref,
    state_ref,
    x_taps_ref,
    bc_taps_ref,
    offset_ref,
    rate_ref,
    skip_ref,
    gain_ref,
    parents_ref,
    anc_ref,
    pack_ref,
    state_out_ref,
):
    request = place_ref[0]
    group = place_ref[1]

    def of_group(ref):
        table = ref[...]
        this = lax.broadcasted_iota(jnp.int32, table.shape, 0) == group
        return jnp.sum(jnp.where(this, table, 0.0), axis=0, keepdims=True)

    x_taps = jnp.zeros((4, 128), F32)
    bc_taps = jnp.zeros((4, 512), F32)
    for index in range(G):
        x_taps = jnp.where(group == index, x_taps_ref[:, index, :].astype(F32), x_taps)
        bc_taps = jnp.where(group == index, bc_taps_ref[:, index, :].astype(F32), bc_taps)

    lane = lax.broadcasted_iota(jnp.int32, (64, 64), 1)
    anc = anc_ref[0]
    anc_float = anc.astype(F32)
    depth_col = jnp.sum(anc, axis=1, keepdims=True) - 1
    depth_row = lax.dot_general(
        jnp.ones((8, 64), BF16), anc_float.astype(BF16), NT, preferred_element_type=F32
    )
    depth_row = depth_row[0:1, :].astype(jnp.int32) - 1
    all_parents = parents_ref[...]
    this = lax.broadcasted_iota(jnp.int32, all_parents.shape, 0) == request
    parent_row = jnp.sum(jnp.where(this, all_parents, 0), axis=0, keepdims=True)
    hop = (column_of(parent_row, 64) == lane).astype(F32)
    hops = [hop]
    for _ in range(2):
        moved = jnp.dot(
            hops[-1].astype(BF16), hop.astype(BF16), preferred_element_type=F32
        )
        hops.append(moved)
    pack_ref[HOPS : HOPS + 64, :] = jnp.concatenate(hops[0:2], axis=1)
    pack_ref[HOPS + 64 : HOPS + 128, :] = jnp.concatenate([hops[2], hops[2]], axis=1)
    pack_ref[ANC : ANC + 64, :] = jnp.concatenate([anc_float, anc_float], axis=1)

    x_hist = x_hist_ref[0, 0].astype(F32)
    x_base = jnp.zeros((64, 128), F32)
    rows = jnp.concatenate([bc_taps, bc_hist_ref[0, 0].astype(F32), jnp.zeros((9, 512), F32)], axis=0)
    square = (512, 512)
    eye = lax.broadcasted_iota(jnp.int32, square, 0) == lax.broadcasted_iota(jnp.int32, square, 1)
    turned = lax.dot_general(
        eye.astype(BF16), rows.astype(BF16), NT, preferred_element_type=F32
    )
    bc_base = jnp.zeros((512, 64), F32)
    for distance in range(1, 4):
        tap = 3 - distance
        for entry in range(3):
            use = (distance > depth_col) & (entry == tap + depth_col)
            x_base = x_base + jnp.where(
                use, x_hist[entry : entry + 1, :] * x_taps[tap : tap + 1, :], 0.0
            )
            use = (distance > depth_row) & (entry == tap + depth_row)
            share = turned[:, 4 + entry : 5 + entry] * turned[:, tap : tap + 1]
            bc_base = bc_base + jnp.where(use, share, 0.0)
    pack_ref[0:512, :] = jnp.concatenate([bc_base, turned, jnp.zeros((512, 48), F32)], axis=1)
    pack_ref[BASE : BASE + 64, :] = x_base

    first = lax.broadcasted_iota(jnp.int32, (1, 128), 1) < P_SIZE
    offset = column_of(of_group(offset_ref), 2)
    rate = column_of(-jnp.exp(of_group(rate_ref)), 2)
    skip = column_of(of_group(skip_ref), 2)
    pack_ref[SMALL : SMALL + 16, :] = jnp.concatenate(
        [
            x_taps,
            of_group(gain_ref),
            jnp.where(first, skip[0:1, :], skip[1:2, :]),
            jnp.zeros((2, 128), F32),
            jnp.broadcast_to(offset, (2, 128)),
            jnp.broadcast_to(rate, (2, 128)),
            jnp.zeros((4, 128), F32),
        ],
        axis=0,
    )
    state_out_ref[...] = state_ref[0, 0].reshape(2 * P_SIZE, N).astype(BF16)


def mixer_kernel(local_ref, bc_new_ref, pack_ref, state_ref, out_ref, bc_ref):
    for col in range(bc_new_ref.shape[0]):
        piece = bc_new_ref[col].astype(F32)
        bc_ref[col * 32 : col * 32 + 16, :] = piece[:, 0:64].astype(BF16)
        bc_ref[col * 32 + 16 : col * 32 + 32, :] = piece[:, 64:128].astype(BF16)
    hops = [
        pack_ref[HOPS : HOPS + 64, 0:64].astype(BF16),
        pack_ref[HOPS : HOPS + 64, 64:128].astype(BF16),
        pack_ref[HOPS + 64 : HOPS + 128, 0:64].astype(BF16),
    ]
    small = pack_ref[SMALL : SMALL + 16, :]

    x_new = local_ref[0:64, 0:128]
    gate = local_ref[0:64, 128:256]
    x_high = x_new.astype(BF16)
    x_low = (x_new - x_high.astype(F32)).astype(BF16)
    x_both = jnp.concatenate([x_high, x_low], axis=1)
    x_run = pack_ref[BASE : BASE + 64, :] + x_new * small[3:4, :]
    bc_run = pack_ref[0:512, 0:64] + bc_ref[...].astype(F32) * pack_ref[0:512, 67:68]
    for distance in range(1, 4):
        tap = 3 - distance
        moved = jnp.dot(hops[distance - 1], x_both, preferred_element_type=F32)
        x_run = x_run + (moved[:, 0:128] + moved[:, 128:256]) * small[tap : tap + 1, :]
        moved = lax.dot_general(bc_ref[...], hops[distance - 1], NT, preferred_element_type=F32)
        bc_run = bc_run + moved * pack_ref[0:512, 64 + tap : 65 + tap]
    x_conv = x_run * jax.nn.sigmoid(x_run)
    bc_conv = (bc_run * jax.nn.sigmoid(bc_run)).astype(BF16)

    raw = local_ref[64:66, 0:64] + small[8:10, 0:64]
    step = jnp.maximum(raw, 0.0) + jnp.log1p(jnp.exp(-jnp.abs(raw)))
    log_decay = small[10:12, 0:64] * step
    anc = pack_ref[ANC : ANC + 64, 0:64]
    cum = lax.dot_general(
        jnp.concatenate([log_decay, jnp.zeros((6, 64), F32)], axis=0),
        anc,
        NT,
        precision=lax.Precision.HIGHEST,
        preferred_element_type=F32,
    )

    square = (64, 64)
    eye = lax.broadcasted_iota(jnp.int32, square, 0) == lax.broadcasted_iota(jnp.int32, square, 1)
    c_node = lax.dot_general(
        eye.astype(BF16), bc_conv[256:512, :], NT, preferred_element_type=F32
    ).astype(BF16)
    scores = jnp.dot(c_node, bc_conv[0:256, :], preferred_element_type=F32)
    carried = lax.dot_general(c_node, state_ref[...], NT, preferred_element_type=F32)
    x_bf = x_conv.astype(BF16)
    is_anc = anc > 0.5
    inner = []
    start = []
    for head in range(2):
        cum_row = cum[head : head + 1, :]
        cum_col = column_of(cum_row, 64)
        gap = jnp.where(is_anc, cum_col - cum_row, 0.0)
        weight = jnp.where(is_anc, jnp.exp(gap), 0.0) * scores * step[head : head + 1, :]
        inner.append(jnp.dot(weight.astype(BF16), x_bf, preferred_element_type=F32))
        start.append(jnp.exp(cum_col))
    first = lax.broadcasted_iota(jnp.int32, (64, 128), 1) < P_SIZE
    mixed = (
        jnp.where(first, inner[0], inner[1])
        + jnp.where(first, start[0], start[1]) * carried
        + small[5:6, :] * x_conv
    )
    gated = mixed * (gate * jax.nn.sigmoid(gate))
    group_sq = jnp.sum(gated * gated, axis=1, keepdims=True)
    both = jnp.concatenate(
        [gated * small[4:5, :], jnp.broadcast_to(group_sq, (64, 128))], axis=1
    )
    for col in range(out_ref.shape[0]):
        out_ref[col] = both[col * 4 : col * 4 + 4, :].astype(BF16)


def scale_heads_kernel(parts_ref, out_ref):
    total = parts_ref[0, :, 128:256].astype(F32)
    for part in range(1, parts_ref.shape[0]):
        total = total + parts_ref[part, :, 128:256].astype(F32)
    scale = lax.rsqrt(total / (H // G * P_SIZE) + EPSILON)
    pieces = [parts_ref[part, :, 0:128].astype(F32) * scale for part in range(parts_ref.shape[0])]
    heads = jnp.concatenate(pieces, axis=0).astype(BF16)
    for row in range(out_ref.shape[0]):
        out_ref[row] = heads


def out_kernel(parity_ref, heads_ref, weight_ref, residual_ref, mine_ref, other_ref, left_ref):
    total = residual_ref[...].astype(F32)
    for group in range(G):
        for request in range(8):
            heads = heads_ref[request * G + group].astype(F32)
            for col in range(16):
                left_ref[request * 4 : request * 4 + 4, col * 128 : (col + 1) * 128] = heads[
                    col * 4 : col * 4 + 4, :
                ]
        left = left_ref[...].astype(BF16)
        weight = weight_ref[:, group].reshape(-1, 256)
        total = total + jnp.dot(left, weight, preferred_element_type=F32)
    after = total.astype(BF16)
    first = parity_ref[0] == 0
    mine_ref[...] = jnp.where(first, after[0:16, :], after[16:32, :])
    other_ref[...] = jnp.where(first, after[16:32, :], after[0:16, :])


def pair_copies_kernel(mine_ref, other_ref, out_ref):
    for col in range(out_ref.shape[0]):
        out_ref[col, :, 0:256] = mine_ref[...]
        out_ref[col, :, 256:512] = other_ref[...]


def up_kernel(after_ref, gain_ref, other_gain_ref, weight_ref, other_weight_ref, out_ref):
    after = after_ref[...].reshape(256, 512).astype(F32)
    stat = jnp.broadcast_to(jnp.sum(after * after, axis=1, keepdims=True), (256, 128))
    stat = stat.astype(BF16)
    mine = (after[:, 0:256] * gain_ref[...]).astype(BF16)
    other = (after[:, 256:512] * other_gain_ref[...]).astype(BF16)
    for block in range(4):
        lanes = slice(block * 512, (block + 1) * 512)
        term = jnp.dot(mine, weight_ref[:, lanes], preferred_element_type=F32)
        term = term + jnp.dot(other, other_weight_ref[:, lanes], preferred_element_type=F32)
        term = term.astype(BF16)
        for part in range(16):
            out_ref[part, :, lanes] = term[part * 16 : (part + 1) * 16, :]
    for part in range(16):
        out_ref[part, :, 2048:2176] = stat[part * 16 : (part + 1) * 16, :]


def act_kernel(parts_ref, out_ref):
    stat = parts_ref[0, :, 2048:2176].astype(F32)
    for part in range(1, parts_ref.shape[0]):
        stat = stat + parts_ref[part, :, 2048:2176].astype(F32)
    scale = lax.rsqrt(stat / D + EPSILON)
    for block in range(16):
        lanes = slice(block * 128, (block + 1) * 128)
        up = parts_ref[0, :, lanes].astype(F32)
        for part in range(1, parts_ref.shape[0]):
            up = up + parts_ref[part, :, lanes].astype(F32)
        act = jnp.maximum(up * scale, 0.0)
        act = (act * act).astype(BF16)
        for part in range(out_ref.shape[0]):
            out_ref[part, :, lanes] = act


def down_kernel(act_ref, weight_ref, out_ref, turn_ref):
    term = jnp.dot(act_ref[...].reshape(256, -1), weight_ref[...], preferred_element_type=F32)
    for col in range(16):
        for request in range(4):
            start = col * 16 + request * 4
            turn_ref[2 * request + col // 8, col % 8 * 4 : col % 8 * 4 + 4, :] = term[
                start : start + 4, :
            ]
    out_ref[...] = turn_ref[...].astype(BF16)


def join_kernel(parity_ref, mine_ref, other_ref, out_ref):
    parity = parity_ref[0]
    out_ref[pl.ds(parity * 8, 8)] = mine_ref[...]
    out_ref[pl.ds(8 - parity * 8, 8)] = other_ref[...]


def local(
    hidden_in,
    norm_mixer,
    mixer_in,
    bc_proj,
    dt_proj,
    dt_bias,
    a_log,
    skip_d,
    conv_x,
    conv_bc,
    x_cache,
    bc_cache,
    ssm_cache,
    slot_ids,
    parents,
    ancestors,
    norm_gated,
    out_proj,
    norm_ffn,
    ffn_up,
    ffn_down,
):
    rows = lax.axis_size("row")
    cols = lax.axis_size("col")
    row_index = lax.axis_index("row")
    col_index = lax.axis_index("col")
    place = jnp.stack([row_index // G, row_index % G]).astype(jnp.int32)
    parity = (row_index % 2).astype(jnp.int32)[None]
    swap = [(row, row ^ 1) for row in range(rows)]
    halves = [[row for row in range(rows) if row % 2 == half] for half in range(2)]
    smem = pl.BlockSpec(memory_space=pltpu.SMEM)
    vmem = pl.BlockSpec(memory_space=pltpu.VMEM)
    params = pltpu.CompilerParams(vmem_limit_bytes=VMEM_LIMIT)

    out_weights = lax.all_gather(out_proj, "col", axis=0, tiled=False)

    copies = call(copies_kernel, jax.ShapeDtypeStruct((cols, 32, 256), BF16), hidden_in)
    hidden = exchange(copies, "col")
    side = jnp.concatenate([bc_proj, dt_proj, jnp.zeros((256, G, 30), BF16)], axis=2)
    side = side.reshape(256, 256).T
    main = mixer_in.reshape(256, -1)

    def pair_sum(half):
        other = lax.ppermute(half(True), "row", swap)
        return (half(False).astype(F32) + other.astype(F32)).astype(BF16)

    def project_half(flip):
        return pl.pallas_call(
            functools.partial(project_kernel, flip),
            out_shape=jax.ShapeDtypeStruct((16, 80, 256), BF16),
            in_specs=[smem, vmem, vmem, vmem, vmem],
            out_specs=vmem,
            compiler_params=params,
        )(parity, hidden.reshape(512, 256), norm_mixer[None, :], main, side)

    parts = pair_sum(project_half)
    parts, up_mine, down_mine, gain_mine = lax.optimization_barrier(
        (parts, ffn_up, ffn_down, norm_ffn[None, :])
    )
    up_other, down_other, gain_other = [
        lax.ppermute(weight, "row", swap) for weight in (up_mine, down_mine, gain_mine)
    ]
    parts = exchange(parts, "row", halves)

    bc_own, local_sums = call(
        combine_kernel,
        (jax.ShapeDtypeStruct((cols, 16, 128), BF16), jax.ShapeDtypeStruct((72, 256), F32)),
        parts,
    )
    bc_own, place = lax.optimization_barrier((bc_own, place))

    def whole(array):
        shape = array.shape
        return pl.BlockSpec(shape, lambda step, place, slots: (0,) * len(shape))

    def slot_block(*shape):
        zeros = (0,) * (len(shape) - 2)
        return pl.BlockSpec(shape, lambda step, place, slots: (0, slots[place[0]]) + zeros)

    operands = [
        (x_cache, slot_block(1, 1, 3, 128)),
        (bc_cache, slot_block(1, 1, 3, 512)),
        (ssm_cache, slot_block(1, 1, 2, P_SIZE, N)),
        (conv_x, whole(conv_x)),
        (conv_bc, whole(conv_bc)),
        (dt_bias, whole(dt_bias)),
        (a_log, whole(a_log)),
        (skip_d, whole(skip_d)),
        (norm_gated, whole(norm_gated)),
        (parents, whole(parents)),
        (ancestors, pl.BlockSpec((1, 64, 64), lambda step, place, slots: (place[0], 0, 0))),
    ]
    pack, state = pl.pallas_call(
        prepare_kernel,
        grid_spec=pltpu.PrefetchScalarGridSpec(
            num_scalar_prefetch=2,
            grid=(1,),
            in_specs=[spec for _, spec in operands],
            out_specs=[
                pl.BlockSpec((PACK, 128), lambda step, place, slots: (0, 0)),
                pl.BlockSpec((2 * P_SIZE, N), lambda step, place, slots: (0, 0)),
            ],
        ),
        out_shape=[
            jax.ShapeDtypeStruct((PACK, 128), F32),
            jax.ShapeDtypeStruct((2 * P_SIZE, N), BF16),
        ],
        compiler_params=params,
    )(place, slot_ids, *[operand for operand, _ in operands])

    bc_new = exchange(bc_own, "col")
    mixed = pl.pallas_call(
        mixer_kernel,
        out_shape=jax.ShapeDtypeStruct((cols, 4, 256), BF16),
        scratch_shapes=[pltpu.VMEM((512, 64), BF16)],
        compiler_params=params,
    )(local_sums, bc_new, pack, state)

    mixed = exchange(mixed, "col")
    heads = call(scale_heads_kernel, jax.ShapeDtypeStruct((rows, cols * 4, 128), BF16), mixed)
    heads, out_weights = lax.optimization_barrier((heads, out_weights))
    heads = exchange(heads, "row")
    residual = lax.dynamic_slice(
        hidden.reshape(8, 64, 256), (0, 4 * col_index, 0), (8, 4, 256)
    ).reshape(32, 256)
    half_after = jax.ShapeDtypeStruct((16, 256), BF16)
    after_mine, after_other = pl.pallas_call(
        out_kernel,
        out_shape=(half_after, half_after),
        in_specs=[smem, vmem, vmem, vmem],
        out_specs=(vmem, vmem),
        scratch_shapes=[pltpu.VMEM((32, 2048), F32)],
        compiler_params=params,
    )(parity, heads, out_weights, residual)

    after_other = lax.ppermute(after_other, "row", swap)
    after = exchange(
        call(
            pair_copies_kernel,
            jax.ShapeDtypeStruct((cols, 16, 512), BF16),
            after_mine,
            after_other,
        ),
        "col",
    )
    up_parts = call(
        up_kernel,
        jax.ShapeDtypeStruct((16, 16, 2176), BF16),
        after,
        gain_mine,
        gain_other,
        up_mine,
        up_other,
    )
    up_parts = exchange(up_parts, "row", halves)
    act = call(act_kernel, jax.ShapeDtypeStruct((16, 16, 2048), BF16), up_parts)
    act = exchange(act, "row", halves)

    def down_half(weight):
        return pl.pallas_call(
            down_kernel,
            out_shape=jax.ShapeDtypeStruct((8, 32, 256), BF16),
            scratch_shapes=[pltpu.VMEM((8, 32, 256), F32)],
            compiler_params=params,
        )(act, weight)

    from_other = lax.ppermute(down_half(down_other), "row", swap)
    down = pl.pallas_call(
        join_kernel,
        out_shape=jax.ShapeDtypeStruct((cols, 32, 256), BF16),
        in_specs=[smem, vmem, vmem],
        out_specs=vmem,
        compiler_params=params,
    )(parity, down_half(down_mine), from_other)
    ffn_out = jnp.sum(exchange(down, "col").astype(F32), axis=0)
    own = lax.dynamic_slice(
        after, (8 * (col_index % 2), 4 * (col_index // 2 % 4), 0), (8, 4, 512)
    ).reshape(32, 512)
    own_other = lax.ppermute(own[:, 256:], "row", swap)
    own_after = jnp.where(col_index // 8 == row_index % 2, own[:, :256], own_other)
    return (own_after.astype(F32) + ffn_out).astype(BF16)


def solution(mesh):
    return jax.shard_map(
        local,
        mesh=mesh,
        in_specs=(
            P("col", "row"),
            P("row"),
            P("row", None, "col", None),
            P("row", None, "col"),
            P("row", None, "col"),
            P(None, "col"),
            P(None, "col"),
            P(None, "col"),
            P(None, None, "col"),
            P(),
            P("row", None, None, "col"),
            P("row", None, None, None),
            P("row", None, "col", None, None),
            P(),
            P(),
            P(),
            P(None, "col"),
            P(None, "col", "row"),
            P("row"),
            P("row", "col"),
            P("col", "row"),
        ),
        out_specs=P("col", "row"),
        check_vma=False,
    )
```

```python
import functools

import jax
import jax.numpy as jnp
from jax import lax
from jax.experimental import pallas as pl
from jax.experimental.pallas import tpu as pltpu
from jax.sharding import PartitionSpec as P

D = 8192
H = 128
P_SIZE = 64
N = 256
G = 4

EPSILON = 1e-05
F32 = jnp.float32
BF16 = jnp.bfloat16
NT = (((1,), (1,)), ((), ()))
VMEM_LIMIT = 48 * 1024 * 1024


def exchange(parts, axis, groups=None):
    return lax.all_to_all(parts, axis, 0, 0, tiled=True, axis_index_groups=groups)


def call(kernel, out_shape, *operands):
    return pl.pallas_call(
        kernel,
        out_shape=out_shape,
        compiler_params=pltpu.CompilerParams(vmem_limit_bytes=VMEM_LIMIT),
    )(*operands)


def copies_kernel(block_ref, out_ref):
    for part in range(out_ref.shape[0]):
        out_ref[part] = block_ref[...]


def project_kernel(flip, parity_ref, hidden_ref, gain_ref, main_ref, side_ref, out_ref):
    use = parity_ref[0] if not flip else 1 - parity_ref[0]
    hidden = hidden_ref[...].astype(F32)
    normed = (hidden * gain_ref[...]).astype(BF16)
    squares = (hidden * hidden).astype(BF16)
    ones = jnp.ones((16, hidden.shape[1]), BF16)
    stat = lax.dot_general(ones, squares, NT, preferred_element_type=F32)
    for half in range(G // 2):
        group = 2 * half + use
        main = main_ref[:, pl.ds(pl.multiple_of(group * 256, 256), 256)]
        main = jnp.dot(normed, main, preferred_element_type=F32).astype(BF16)
        side = side_ref[pl.ds(pl.multiple_of(group * 64, 64), 64), :]
        side = lax.dot_general(side, normed, NT, preferred_element_type=F32)
        for request in range(8):
            part = request * (G // 2) + half
            nodes = slice(request * 64, (request + 1) * 64)
            out_ref[part, 0:64, :] = main[nodes, :]
            pieces = [side[0:16, nodes], side[16:32, nodes], side[32:48, nodes], stat[:, nodes]]
            out_ref[part, 64:80, :] = jnp.concatenate(pieces, axis=1).astype(BF16)


def column_of(row, size):
    eye = lax.broadcasted_iota(jnp.int32, (size, size), 0) == lax.broadcasted_iota(
        jnp.int32, (size, size), 1
    )
    wide = jnp.broadcast_to(row, (size, size))
    return jnp.sum(jnp.where(eye, wide, jnp.zeros_like(wide)), axis=1, keepdims=True)


def combine_kernel(parts_ref, bc_ref, local_ref):
    total = parts_ref[0].astype(F32)
    for part in range(1, parts_ref.shape[0]):
        total = total + parts_ref[part].astype(F32)
    scale = lax.rsqrt(total[64:65, 192:256] / D + EPSILON)
    bc = (total[64:80, 0:128] * jnp.concatenate([scale, scale], axis=1)).astype(BF16)
    for col in range(bc_ref.shape[0]):
        bc_ref[col] = bc
    main = total[0:64, :]
    main = jnp.concatenate(
        [main[:, 0:64], main[:, 128:192], main[:, 64:128], main[:, 192:256]], axis=1
    )
    local_ref[0:64, :] = main * column_of(scale, 64)
    step = total[64:72, 128:192] * scale
    local_ref[64:72, :] = jnp.concatenate([step] * 4, axis=1)


BASE, ANC, HOPS, SMALL, PACK = 512, 576, 640, 768, 784


def prepare_kernel(
    place_ref,
    slot_ref,
    x_hist_ref,
    bc_hist_ref,
    state_ref,
    x_taps_ref,
    bc_taps_ref,
    offset_ref,
    rate_ref,
    skip_ref,
    gain_ref,
    parents_ref,
    anc_ref,
    pack_ref,
    state_out_ref,
):
    request = place_ref[0]
    group = place_ref[1]

    def of_group(ref):
        table = ref[...]
        this = lax.broadcasted_iota(jnp.int32, table.shape, 0) == group
        return jnp.sum(jnp.where(this, table, 0.0), axis=0, keepdims=True)

    x_taps = jnp.zeros((4, 128), F32)
    bc_taps = jnp.zeros((4, 512), F32)
    for index in range(G):
        x_taps = jnp.where(group == index, x_taps_ref[:, index, :].astype(F32), x_taps)
        bc_taps = jnp.where(group == index, bc_taps_ref[:, index, :].astype(F32), bc_taps)

    lane = lax.broadcasted_iota(jnp.int32, (64, 64), 1)
    anc = anc_ref[0]
    anc_float = anc.astype(F32)
    depth_col = jnp.sum(anc, axis=1, keepdims=True) - 1
    depth_row = lax.dot_general(
        jnp.ones((8, 64), BF16), anc_float.astype(BF16), NT, preferred_element_type=F32
    )
    depth_row = depth_row[0:1, :].astype(jnp.int32) - 1
    all_parents = parents_ref[...]
    this = lax.broadcasted_iota(jnp.int32, all_parents.shape, 0) == request
    parent_row = jnp.sum(jnp.where(this, all_parents, 0), axis=0, keepdims=True)
    hop = (column_of(parent_row, 64) == lane).astype(F32)
    hops = [hop]
    for _ in range(2):
        moved = jnp.dot(
            hops[-1].astype(BF16), hop.astype(BF16), preferred_element_type=F32
        )
        hops.append(moved)
    pack_ref[HOPS : HOPS + 64, :] = jnp.concatenate(hops[0:2], axis=1)
    pack_ref[HOPS + 64 : HOPS + 128, :] = jnp.concatenate([hops[2], hops[2]], axis=1)
    pack_ref[ANC : ANC + 64, :] = jnp.concatenate([anc_float, anc_float], axis=1)

    x_hist = x_hist_ref[0, 0].astype(F32)
    x_base = jnp.zeros((64, 128), F32)
    rows = jnp.concatenate([bc_taps, bc_hist_ref[0, 0].astype(F32), jnp.zeros((9, 512), F32)], axis=0)
    square = (512, 512)
    eye = lax.broadcasted_iota(jnp.int32, square, 0) == lax.broadcasted_iota(jnp.int32, square, 1)
    turned = lax.dot_general(
        eye.astype(BF16), rows.astype(BF16), NT, preferred_element_type=F32
    )
    bc_base = jnp.zeros((512, 64), F32)
    for distance in range(1, 4):
        tap = 3 - distance
        for entry in range(3):
            use = (distance > depth_col) & (entry == tap + depth_col)
            x_base = x_base + jnp.where(
                use, x_hist[entry : entry + 1, :] * x_taps[tap : tap + 1, :], 0.0
            )
            use = (distance > depth_row) & (entry == tap + depth_row)
            share = turned[:, 4 + entry : 5 + entry] * turned[:, tap : tap + 1]
            bc_base = bc_base + jnp.where(use, share, 0.0)
    pack_ref[0:512, :] = jnp.concatenate([bc_base, turned, jnp.zeros((512, 48), F32)], axis=1)
    pack_ref[BASE : BASE + 64, :] = x_base

    first = lax.broadcasted_iota(jnp.int32, (1, 128), 1) < P_SIZE
    offset = column_of(of_group(offset_ref), 2)
    rate = column_of(-jnp.exp(of_group(rate_ref)), 2)
    skip = column_of(of_group(skip_ref), 2)
    pack_ref[SMALL : SMALL + 16, :] = jnp.concatenate(
        [
            x_taps,
            of_group(gain_ref),
            jnp.where(first, skip[0:1, :], skip[1:2, :]),
            jnp.zeros((2, 128), F32),
            jnp.broadcast_to(offset, (2, 128)),
            jnp.broadcast_to(rate, (2, 128)),
            jnp.zeros((4, 128), F32),
        ],
        axis=0,
    )
    state_out_ref[...] = state_ref[0, 0].reshape(2 * P_SIZE, N).astype(BF16)


def mixer_kernel(local_ref, bc_new_ref, pack_ref, state_ref, out_ref, bc_ref):
    for col in range(bc_new_ref.shape[0]):
        piece = bc_new_ref[col].astype(F32)
        bc_ref[col * 32 : col * 32 + 16, :] = piece[:, 0:64].astype(BF16)
        bc_ref[col * 32 + 16 : col * 32 + 32, :] = piece[:, 64:128].astype(BF16)
    hops = [
        pack_ref[HOPS : HOPS + 64, 0:64].astype(BF16),
        pack_ref[HOPS : HOPS + 64, 64:128].astype(BF16),
        pack_ref[HOPS + 64 : HOPS + 128, 0:64].astype(BF16),
    ]
    small = pack_ref[SMALL : SMALL + 16, :]

    x_new = local_ref[0:64, 0:128]
    gate = local_ref[0:64, 128:256]
    x_high = x_new.astype(BF16)
    x_low = (x_new - x_high.astype(F32)).astype(BF16)
    x_both = jnp.concatenate([x_high, x_low], axis=1)
    x_run = pack_ref[BASE : BASE + 64, :] + x_new * small[3:4, :]
    bc_run = pack_ref[0:512, 0:64] + bc_ref[...].astype(F32) * pack_ref[0:512, 67:68]
    for distance in range(1, 4):
        tap = 3 - distance
        moved = jnp.dot(hops[distance - 1], x_both, preferred_element_type=F32)
        x_run = x_run + (moved[:, 0:128] + moved[:, 128:256]) * small[tap : tap + 1, :]
        moved = lax.dot_general(bc_ref[...], hops[distance - 1], NT, preferred_element_type=F32)
        bc_run = bc_run + moved * pack_ref[0:512, 64 + tap : 65 + tap]
    x_conv = x_run * jax.nn.sigmoid(x_run)
    bc_conv = (bc_run * jax.nn.sigmoid(bc_run)).astype(BF16)

    raw = local_ref[64:66, 0:64] + small[8:10, 0:64]
    step = jnp.maximum(raw, 0.0) + jnp.log1p(jnp.exp(-jnp.abs(raw)))
    log_decay = small[10:12, 0:64] * step
    anc = pack_ref[ANC : ANC + 64, 0:64]
    cum = lax.dot_general(
        jnp.concatenate([log_decay, jnp.zeros((6, 64), F32)], axis=0),
        anc,
        NT,
        precision=lax.Precision.HIGHEST,
        preferred_element_type=F32,
    )

    square = (64, 64)
    eye = lax.broadcasted_iota(jnp.int32, square, 0) == lax.broadcasted_iota(jnp.int32, square, 1)
    c_node = lax.dot_general(
        eye.astype(BF16), bc_conv[256:512, :], NT, preferred_element_type=F32
    ).astype(BF16)
    scores = jnp.dot(c_node, bc_conv[0:256, :], preferred_element_type=F32)
    carried = lax.dot_general(c_node, state_ref[...], NT, preferred_element_type=F32)
    x_bf = x_conv.astype(BF16)
    is_anc = anc > 0.5
    inner = []
    start = []
    for head in range(2):
        cum_row = cum[head : head + 1, :]
        cum_col = column_of(cum_row, 64)
        gap = jnp.where(is_anc, cum_col - cum_row, 0.0)
        weight = jnp.where(is_anc, jnp.exp(gap), 0.0) * scores * step[head : head + 1, :]
        inner.append(jnp.dot(weight.astype(BF16), x_bf, preferred_element_type=F32))
        start.append(jnp.exp(cum_col))
    first = lax.broadcasted_iota(jnp.int32, (64, 128), 1) < P_SIZE
    mixed = (
        jnp.where(first, inner[0], inner[1])
        + jnp.where(first, start[0], start[1]) * carried
        + small[5:6, :] * x_conv
    )
    gated = mixed * (gate * jax.nn.sigmoid(gate))
    group_sq = jnp.sum(gated * gated, axis=1, keepdims=True)
    both = jnp.concatenate(
        [gated * small[4:5, :], jnp.broadcast_to(group_sq, (64, 128))], axis=1
    )
    for col in range(out_ref.shape[0]):
        out_ref[col] = both[col * 4 : col * 4 + 4, :].astype(BF16)


def scale_heads_kernel(parts_ref, out_ref):
    total = parts_ref[0, :, 128:256].astype(F32)
    for part in range(1, parts_ref.shape[0]):
        total = total + parts_ref[part, :, 128:256].astype(F32)
    scale = lax.rsqrt(total / (H // G * P_SIZE) + EPSILON)
    pieces = [parts_ref[part, :, 0:128].astype(F32) * scale for part in range(parts_ref.shape[0])]
    heads = jnp.concatenate(pieces, axis=0).astype(BF16)
    for row in range(out_ref.shape[0]):
        out_ref[row] = heads


def by_group_kernel(weight_ref, out_ref):
    out_ref[0] = weight_ref[...].reshape(-1, 256)


def out_kernel(parity_ref, heads_ref, weight_ref, residual_ref, mine_ref, other_ref, left_ref):
    total = residual_ref[...].astype(F32)
    for group in range(G):
        for request in range(8):
            heads = heads_ref[request * G + group].astype(F32)
            for col in range(16):
                left_ref[request * 4 : request * 4 + 4, col * 128 : (col + 1) * 128] = heads[
                    col * 4 : col * 4 + 4, :
                ]
        left = left_ref[...].astype(BF16)
        total = total + jnp.dot(left, weight_ref[group], preferred_element_type=F32)
    after = total.astype(BF16)
    first = parity_ref[0] == 0
    mine_ref[...] = jnp.where(first, after[0:16, :], after[16:32, :])
    other_ref[...] = jnp.where(first, after[16:32, :], after[0:16, :])


def pair_copies_kernel(mine_ref, other_ref, out_ref):
    for col in range(out_ref.shape[0]):
        out_ref[col, :, 0:256] = mine_ref[...]
        out_ref[col, :, 256:512] = other_ref[...]


def up_kernel(after_ref, gain_ref, other_gain_ref, weight_ref, other_weight_ref, out_ref):
    after = after_ref[...].reshape(256, 512).astype(F32)
    stat = jnp.broadcast_to(jnp.sum(after * after, axis=1, keepdims=True), (256, 128))
    stat = stat.astype(BF16)
    mine = (after[:, 0:256] * gain_ref[...]).astype(BF16)
    other = (after[:, 256:512] * other_gain_ref[...]).astype(BF16)
    for block in range(4):
        lanes = slice(block * 512, (block + 1) * 512)
        term = jnp.dot(mine, weight_ref[:, lanes], preferred_element_type=F32)
        term = term + jnp.dot(other, other_weight_ref[:, lanes], preferred_element_type=F32)
        term = term.astype(BF16)
        for part in range(16):
            out_ref[part, :, lanes] = term[part * 16 : (part + 1) * 16, :]
    for part in range(16):
        out_ref[part, :, 2048:2176] = stat[part * 16 : (part + 1) * 16, :]


def act_kernel(parts_ref, out_ref):
    stat = parts_ref[0, :, 2048:2176].astype(F32)
    for part in range(1, parts_ref.shape[0]):
        stat = stat + parts_ref[part, :, 2048:2176].astype(F32)
    scale = lax.rsqrt(stat / D + EPSILON)
    for block in range(16):
        lanes = slice(block * 128, (block + 1) * 128)
        up = parts_ref[0, :, lanes].astype(F32)
        for part in range(1, parts_ref.shape[0]):
            up = up + parts_ref[part, :, lanes].astype(F32)
        act = jnp.maximum(up * scale, 0.0)
        act = (act * act).astype(BF16)
        for part in range(out_ref.shape[0]):
            out_ref[part, :, lanes] = act


def down_kernel(act_ref, weight_ref, out_ref, turn_ref):
    term = jnp.dot(act_ref[...].reshape(256, -1), weight_ref[...], preferred_element_type=F32)
    for col in range(16):
        for request in range(4):
            start = col * 16 + request * 4
            turn_ref[2 * request + col // 8, col % 8 * 4 : col % 8 * 4 + 4, :] = term[
                start : start + 4, :
            ]
    out_ref[...] = turn_ref[...].astype(BF16)


def join_kernel(parity_ref, mine_ref, other_ref, out_ref):
    parity = parity_ref[0]
    out_ref[pl.ds(parity * 8, 8)] = mine_ref[...]
    out_ref[pl.ds(8 - parity * 8, 8)] = other_ref[...]


def local(
    hidden_in,
    norm_mixer,
    mixer_in,
    bc_proj,
    dt_proj,
    dt_bias,
    a_log,
    skip_d,
    conv_x,
    conv_bc,
    x_cache,
    bc_cache,
    ssm_cache,
    slot_ids,
    parents,
    ancestors,
    norm_gated,
    out_proj,
    norm_ffn,
    ffn_up,
    ffn_down,
):
    rows = lax.axis_size("row")
    cols = lax.axis_size("col")
    row_index = lax.axis_index("row")
    col_index = lax.axis_index("col")
    place = jnp.stack([row_index // G, row_index % G]).astype(jnp.int32)
    parity = (row_index % 2).astype(jnp.int32)[None]
    swap = [(row, row ^ 1) for row in range(rows)]
    halves = [[row for row in range(rows) if row % 2 == half] for half in range(2)]
    smem = pl.BlockSpec(memory_space=pltpu.SMEM)
    vmem = pl.BlockSpec(memory_space=pltpu.VMEM)
    params = pltpu.CompilerParams(vmem_limit_bytes=VMEM_LIMIT)

    out_weights = lax.all_gather(out_proj, "col", axis=0, tiled=False)

    copies = call(copies_kernel, jax.ShapeDtypeStruct((cols, 32, 256), BF16), hidden_in)
    hidden = exchange(copies, "col")
    side = jnp.concatenate([bc_proj, dt_proj, jnp.zeros((256, G, 30), BF16)], axis=2)
    side = side.reshape(256, 256).T
    main = mixer_in.reshape(256, -1)

    def pair_sum(half):
        other = lax.ppermute(half(True), "row", swap)
        return (half(False).astype(F32) + other.astype(F32)).astype(BF16)

    def project_half(flip):
        return pl.pallas_call(
            functools.partial(project_kernel, flip),
            out_shape=jax.ShapeDtypeStruct((16, 80, 256), BF16),
            in_specs=[smem, vmem, vmem, vmem, vmem],
            out_specs=vmem,
            compiler_params=params,
        )(parity, hidden.reshape(512, 256), norm_mixer[None, :], main, side)

    parts = pair_sum(project_half)
    parts = exchange(parts, "row", halves)

    bc_own, local_sums = call(
        combine_kernel,
        (jax.ShapeDtypeStruct((cols, 16, 128), BF16), jax.ShapeDtypeStruct((72, 256), F32)),
        parts,
    )
    bc_own, place = lax.optimization_barrier((bc_own, place))

    def whole(array):
        shape = array.shape
        return pl.BlockSpec(shape, lambda step, place, slots: (0,) * len(shape))

    def slot_block(*shape):
        zeros = (0,) * (len(shape) - 2)
        return pl.BlockSpec(shape, lambda step, place, slots: (0, slots[place[0]]) + zeros)

    operands = [
        (x_cache, slot_block(1, 1, 3, 128)),
        (bc_cache, slot_block(1, 1, 3, 512)),
        (ssm_cache, slot_block(1, 1, 2, P_SIZE, N)),
        (conv_x, whole(conv_x)),
        (conv_bc, whole(conv_bc)),
        (dt_bias, whole(dt_bias)),
        (a_log, whole(a_log)),
        (skip_d, whole(skip_d)),
        (norm_gated, whole(norm_gated)),
        (parents, whole(parents)),
        (ancestors, pl.BlockSpec((1, 64, 64), lambda step, place, slots: (place[0], 0, 0))),
    ]
    pack, state = pl.pallas_call(
        prepare_kernel,
        grid_spec=pltpu.PrefetchScalarGridSpec(
            num_scalar_prefetch=2,
            grid=(1,),
            in_specs=[spec for _, spec in operands],
            out_specs=[
                pl.BlockSpec((PACK, 128), lambda step, place, slots: (0, 0)),
                pl.BlockSpec((2 * P_SIZE, N), lambda step, place, slots: (0, 0)),
            ],
        ),
        out_shape=[
            jax.ShapeDtypeStruct((PACK, 128), F32),
            jax.ShapeDtypeStruct((2 * P_SIZE, N), BF16),
        ],
        compiler_params=params,
    )(place, slot_ids, *[operand for operand, _ in operands])

    bc_new = exchange(bc_own, "col")
    bc_new, up_mine, down_mine, gain_mine = lax.optimization_barrier(
        (bc_new, ffn_up, ffn_down, norm_ffn[None, :])
    )
    up_other, down_other, gain_other = [
        lax.ppermute(weight, "row", swap) for weight in (up_mine, down_mine, gain_mine)
    ]
    mixed = pl.pallas_call(
        mixer_kernel,
        out_shape=jax.ShapeDtypeStruct((cols, 4, 256), BF16),
        scratch_shapes=[pltpu.VMEM((512, 64), BF16)],
        compiler_params=params,
    )(local_sums, bc_new, pack, state)

    mixed = exchange(mixed, "col")
    heads = call(scale_heads_kernel, jax.ShapeDtypeStruct((rows, cols * 4, 128), BF16), mixed)
    heads, out_weights = lax.optimization_barrier((heads, out_weights))
    out_weights = pl.pallas_call(
        by_group_kernel,
        grid=(G,),
        out_shape=jax.ShapeDtypeStruct((G, cols * 128, 256), BF16),
        in_specs=[pl.BlockSpec((cols, 1, 128, 256), lambda group: (0, group, 0, 0))],
        out_specs=pl.BlockSpec((1, cols * 128, 256), lambda group: (group, 0, 0)),
        compiler_params=params,
    )(out_weights)
    heads = exchange(heads, "row")
    residual = lax.dynamic_slice(
        hidden.reshape(8, 64, 256), (0, 4 * col_index, 0), (8, 4, 256)
    ).reshape(32, 256)
    half_after = jax.ShapeDtypeStruct((16, 256), BF16)
    after_mine, after_other = pl.pallas_call(
        out_kernel,
        out_shape=(half_after, half_after),
        in_specs=[smem, vmem, vmem, vmem],
        out_specs=(vmem, vmem),
        scratch_shapes=[pltpu.VMEM((32, 2048), F32)],
        compiler_params=params,
    )(parity, heads, out_weights, residual)

    after_other = lax.ppermute(after_other, "row", swap)
    after = exchange(
        call(
            pair_copies_kernel,
            jax.ShapeDtypeStruct((cols, 16, 512), BF16),
            after_mine,
            after_other,
        ),
        "col",
    )
    up_parts = call(
        up_kernel,
        jax.ShapeDtypeStruct((16, 16, 2176), BF16),
        after,
        gain_mine,
        gain_other,
        up_mine,
        up_other,
    )
    up_parts, down_other = lax.optimization_barrier((up_parts, down_other))
    up_parts = exchange(up_parts, "row", halves)
    act = call(act_kernel, jax.ShapeDtypeStruct((16, 16, 2048), BF16), up_parts)
    act = exchange(act, "row", halves)

    def down_half(weight):
        return pl.pallas_call(
            down_kernel,
            out_shape=jax.ShapeDtypeStruct((8, 32, 256), BF16),
            scratch_shapes=[pltpu.VMEM((8, 32, 256), F32)],
            compiler_params=params,
        )(act, weight)

    from_other = lax.ppermute(down_half(down_other), "row", swap)
    down = pl.pallas_call(
        join_kernel,
        out_shape=jax.ShapeDtypeStruct((cols, 32, 256), BF16),
        in_specs=[smem, vmem, vmem],
        out_specs=vmem,
        compiler_params=params,
    )(parity, down_half(down_mine), from_other)
    ffn_out = jnp.sum(exchange(down, "col").astype(F32), axis=0)
    own = lax.dynamic_slice(
        after, (8 * (col_index % 2), 4 * (col_index // 2 % 4), 0), (8, 4, 512)
    ).reshape(32, 512)
    own_other = lax.ppermute(own[:, 256:], "row", swap)
    own_after = jnp.where(col_index // 8 == row_index % 2, own[:, :256], own_other)
    return (own_after.astype(F32) + ffn_out).astype(BF16)


def solution(mesh):
    return jax.shard_map(
        local,
        mesh=mesh,
        in_specs=(
            P("col", "row"),
            P("row"),
            P("row", None, "col", None),
            P("row", None, "col"),
            P("row", None, "col"),
            P(None, "col"),
            P(None, "col"),
            P(None, "col"),
            P(None, None, "col"),
            P(),
            P("row", None, None, "col"),
            P("row", None, None, None),
            P("row", None, "col", None, None),
            P(),
            P(),
            P(),
            P(None, "col"),
            P(None, "col", "row"),
            P("row"),
            P("row", "col"),
            P("col", "row"),
        ),
        out_specs=P("col", "row"),
        check_vma=False,
    )
```

```python
import functools

import jax
import jax.numpy as jnp
from jax import lax
from jax.experimental import pallas as pl
from jax.experimental.pallas import tpu as pltpu
from jax.sharding import PartitionSpec as P

D = 8192
H = 128
P_SIZE = 64
N = 256
G = 4

EPSILON = 1e-05
F32 = jnp.float32
BF16 = jnp.bfloat16
NT = (((1,), (1,)), ((), ()))
VMEM_LIMIT = 48 * 1024 * 1024


def exchange(parts, axis, groups=None):
    return lax.all_to_all(parts, axis, 0, 0, tiled=True, axis_index_groups=groups)


def call(kernel, out_shape, *operands):
    return pl.pallas_call(
        kernel,
        out_shape=out_shape,
        compiler_params=pltpu.CompilerParams(vmem_limit_bytes=VMEM_LIMIT),
    )(*operands)


def copies_kernel(block_ref, out_ref):
    for part in range(out_ref.shape[0]):
        out_ref[part] = block_ref[...]


def project_kernel(flip, parity_ref, hidden_ref, gain_ref, main_ref, side_ref, out_ref):
    use = parity_ref[0] if not flip else 1 - parity_ref[0]
    hidden = hidden_ref[...].astype(F32)
    normed = (hidden * gain_ref[...]).astype(BF16)
    squares = (hidden * hidden).astype(BF16)
    ones = jnp.ones((16, hidden.shape[1]), BF16)
    stat = lax.dot_general(ones, squares, NT, preferred_element_type=F32)
    for half in range(G // 2):
        group = 2 * half + use
        main = main_ref[:, pl.ds(pl.multiple_of(group * 256, 256), 256)]
        main = jnp.dot(normed, main, preferred_element_type=F32).astype(BF16)
        side = side_ref[pl.ds(pl.multiple_of(group * 64, 64), 64), :]
        side = lax.dot_general(side, normed, NT, preferred_element_type=F32)
        for request in range(8):
            part = request * (G // 2) + half
            nodes = slice(request * 64, (request + 1) * 64)
            out_ref[part, 0:64, :] = main[nodes, :]
            pieces = [side[0:16, nodes], side[16:32, nodes], side[32:48, nodes], stat[:, nodes]]
            out_ref[part, 64:80, :] = jnp.concatenate(pieces, axis=1).astype(BF16)


def column_of(row, size):
    eye = lax.broadcasted_iota(jnp.int32, (size, size), 0) == lax.broadcasted_iota(
        jnp.int32, (size, size), 1
    )
    wide = jnp.broadcast_to(row, (size, size))
    return jnp.sum(jnp.where(eye, wide, jnp.zeros_like(wide)), axis=1, keepdims=True)


def combine_kernel(parts_ref, bc_ref, local_ref):
    total = parts_ref[0].astype(F32)
    for part in range(1, parts_ref.shape[0]):
        total = total + parts_ref[part].astype(F32)
    scale = lax.rsqrt(total[64:65, 192:256] / D + EPSILON)
    bc = (total[64:80, 0:128] * jnp.concatenate([scale, scale], axis=1)).astype(BF16)
    for col in range(bc_ref.shape[0]):
        bc_ref[col] = bc
    main = total[0:64, :]
    main = jnp.concatenate(
        [main[:, 0:64], main[:, 128:192], main[:, 64:128], main[:, 192:256]], axis=1
    )
    local_ref[0:64, :] = main * column_of(scale, 64)
    step = total[64:72, 128:192] * scale
    local_ref[64:72, :] = jnp.concatenate([step] * 4, axis=1)


BASE, ANC, HOPS, SMALL, PACK = 512, 576, 640, 768, 784


def prepare_kernel(
    place_ref,
    slot_ref,
    x_hist_ref,
    bc_hist_ref,
    state_ref,
    x_taps_ref,
    bc_taps_ref,
    offset_ref,
    rate_ref,
    skip_ref,
    gain_ref,
    parents_ref,
    anc_ref,
    pack_ref,
    state_out_ref,
):
    request = place_ref[0]
    group = place_ref[1]

    def of_group(ref):
        table = ref[...]
        this = lax.broadcasted_iota(jnp.int32, table.shape, 0) == group
        return jnp.sum(jnp.where(this, table, 0.0), axis=0, keepdims=True)

    x_taps = jnp.zeros((4, 128), F32)
    bc_taps = jnp.zeros((4, 512), F32)
    for index in range(G):
        x_taps = jnp.where(group == index, x_taps_ref[:, index, :].astype(F32), x_taps)
        bc_taps = jnp.where(group == index, bc_taps_ref[:, index, :].astype(F32), bc_taps)

    lane = lax.broadcasted_iota(jnp.int32, (64, 64), 1)
    anc = anc_ref[0]
    anc_float = anc.astype(F32)
    depth_col = jnp.sum(anc, axis=1, keepdims=True) - 1
    depth_row = lax.dot_general(
        jnp.ones((8, 64), BF16), anc_float.astype(BF16), NT, preferred_element_type=F32
    )
    depth_row = depth_row[0:1, :].astype(jnp.int32) - 1
    all_parents = parents_ref[...]
    this = lax.broadcasted_iota(jnp.int32, all_parents.shape, 0) == request
    parent_row = jnp.sum(jnp.where(this, all_parents, 0), axis=0, keepdims=True)
    hop = (column_of(parent_row, 64) == lane).astype(F32)
    hops = [hop]
    for _ in range(2):
        moved = jnp.dot(
            hops[-1].astype(BF16), hop.astype(BF16), preferred_element_type=F32
        )
        hops.append(moved)
    pack_ref[HOPS : HOPS + 64, :] = jnp.concatenate(hops[0:2], axis=1)
    pack_ref[HOPS + 64 : HOPS + 128, :] = jnp.concatenate([hops[2], hops[2]], axis=1)
    pack_ref[ANC : ANC + 64, :] = jnp.concatenate([anc_float, anc_float], axis=1)

    x_hist = x_hist_ref[0, 0].astype(F32)
    x_base = jnp.zeros((64, 128), F32)
    rows = jnp.concatenate([bc_taps, bc_hist_ref[0, 0].astype(F32), jnp.zeros((9, 512), F32)], axis=0)
    square = (512, 512)
    eye = lax.broadcasted_iota(jnp.int32, square, 0) == lax.broadcasted_iota(jnp.int32, square, 1)
    turned = lax.dot_general(
        eye.astype(BF16), rows.astype(BF16), NT, preferred_element_type=F32
    )
    bc_base = jnp.zeros((512, 64), F32)
    for distance in range(1, 4):
        tap = 3 - distance
        for entry in range(3):
            use = (distance > depth_col) & (entry == tap + depth_col)
            x_base = x_base + jnp.where(
                use, x_hist[entry : entry + 1, :] * x_taps[tap : tap + 1, :], 0.0
            )
            use = (distance > depth_row) & (entry == tap + depth_row)
            share = turned[:, 4 + entry : 5 + entry] * turned[:, tap : tap + 1]
            bc_base = bc_base + jnp.where(use, share, 0.0)
    pack_ref[0:512, :] = jnp.concatenate([bc_base, turned, jnp.zeros((512, 48), F32)], axis=1)
    pack_ref[BASE : BASE + 64, :] = x_base

    first = lax.broadcasted_iota(jnp.int32, (1, 128), 1) < P_SIZE
    offset = column_of(of_group(offset_ref), 2)
    rate = column_of(-jnp.exp(of_group(rate_ref)), 2)
    skip = column_of(of_group(skip_ref), 2)
    pack_ref[SMALL : SMALL + 16, :] = jnp.concatenate(
        [
            x_taps,
            of_group(gain_ref),
            jnp.where(first, skip[0:1, :], skip[1:2, :]),
            jnp.zeros((2, 128), F32),
            jnp.broadcast_to(offset, (2, 128)),
            jnp.broadcast_to(rate, (2, 128)),
            jnp.zeros((4, 128), F32),
        ],
        axis=0,
    )
    state_out_ref[...] = state_ref[0, 0].reshape(2 * P_SIZE, N).astype(BF16)


def mixer_kernel(local_ref, bc_new_ref, pack_ref, state_ref, out_ref, bc_ref):
    for col in range(bc_new_ref.shape[0]):
        piece = bc_new_ref[col].astype(F32)
        bc_ref[col * 32 : col * 32 + 16, :] = piece[:, 0:64].astype(BF16)
        bc_ref[col * 32 + 16 : col * 32 + 32, :] = piece[:, 64:128].astype(BF16)
    hops = [
        pack_ref[HOPS : HOPS + 64, 0:64].astype(BF16),
        pack_ref[HOPS : HOPS + 64, 64:128].astype(BF16),
        pack_ref[HOPS + 64 : HOPS + 128, 0:64].astype(BF16),
    ]
    small = pack_ref[SMALL : SMALL + 16, :]

    x_new = local_ref[0:64, 0:128]
    gate = local_ref[0:64, 128:256]
    x_high = x_new.astype(BF16)
    x_low = (x_new - x_high.astype(F32)).astype(BF16)
    x_both = jnp.concatenate([x_high, x_low], axis=1)
    x_run = pack_ref[BASE : BASE + 64, :] + x_new * small[3:4, :]
    bc_run = pack_ref[0:512, 0:64] + bc_ref[...].astype(F32) * pack_ref[0:512, 67:68]
    for distance in range(1, 4):
        tap = 3 - distance
        moved = jnp.dot(hops[distance - 1], x_both, preferred_element_type=F32)
        x_run = x_run + (moved[:, 0:128] + moved[:, 128:256]) * small[tap : tap + 1, :]
        moved = lax.dot_general(bc_ref[...], hops[distance - 1], NT, preferred_element_type=F32)
        bc_run = bc_run + moved * pack_ref[0:512, 64 + tap : 65 + tap]
    x_conv = x_run * jax.nn.sigmoid(x_run)
    bc_conv = (bc_run * jax.nn.sigmoid(bc_run)).astype(BF16)

    raw = local_ref[64:66, 0:64] + small[8:10, 0:64]
    step = jnp.maximum(raw, 0.0) + jnp.log1p(jnp.exp(-jnp.abs(raw)))
    log_decay = small[10:12, 0:64] * step
    anc = pack_ref[ANC : ANC + 64, 0:64]
    cum = lax.dot_general(
        jnp.concatenate([log_decay, jnp.zeros((6, 64), F32)], axis=0),
        anc,
        NT,
        precision=lax.Precision.HIGHEST,
        preferred_element_type=F32,
    )

    square = (64, 64)
    eye = lax.broadcasted_iota(jnp.int32, square, 0) == lax.broadcasted_iota(jnp.int32, square, 1)
    c_node = lax.dot_general(
        eye.astype(BF16), bc_conv[256:512, :], NT, preferred_element_type=F32
    ).astype(BF16)
    scores = jnp.dot(c_node, bc_conv[0:256, :], preferred_element_type=F32)
    carried = lax.dot_general(c_node, state_ref[...], NT, preferred_element_type=F32)
    x_bf = x_conv.astype(BF16)
    is_anc = anc > 0.5
    inner = []
    start = []
    for head in range(2):
        cum_row = cum[head : head + 1, :]
        cum_col = column_of(cum_row, 64)
        gap = jnp.where(is_anc, cum_col - cum_row, 0.0)
        weight = jnp.where(is_anc, jnp.exp(gap), 0.0) * scores * step[head : head + 1, :]
        inner.append(jnp.dot(weight.astype(BF16), x_bf, preferred_element_type=F32))
        start.append(jnp.exp(cum_col))
    first = lax.broadcasted_iota(jnp.int32, (64, 128), 1) < P_SIZE
    mixed = (
        jnp.where(first, inner[0], inner[1])
        + jnp.where(first, start[0], start[1]) * carried
        + small[5:6, :] * x_conv
    )
    gated = mixed * (gate * jax.nn.sigmoid(gate))
    group_sq = jnp.sum(gated * gated, axis=1, keepdims=True)
    both = jnp.concatenate(
        [gated * small[4:5, :], jnp.broadcast_to(group_sq, (64, 128))], axis=1
    )
    for col in range(out_ref.shape[0]):
        out_ref[col] = both[col * 4 : col * 4 + 4, :].astype(BF16)


def scale_heads_kernel(parts_ref, out_ref):
    total = parts_ref[0, :, 128:256].astype(F32)
    for part in range(1, parts_ref.shape[0]):
        total = total + parts_ref[part, :, 128:256].astype(F32)
    scale = lax.rsqrt(total / (H // G * P_SIZE) + EPSILON)
    pieces = [parts_ref[part, :, 0:128].astype(F32) * scale for part in range(parts_ref.shape[0])]
    heads = jnp.concatenate(pieces, axis=0).astype(BF16)
    for row in range(out_ref.shape[0]):
        out_ref[row] = heads


def out_kernel(parity_ref, heads_ref, weight_ref, residual_ref, mine_ref, other_ref, left_ref):
    total = residual_ref[...].astype(F32)
    for group in range(G):
        for request in range(8):
            heads = heads_ref[request * G + group].astype(F32)
            for col in range(16):
                left_ref[request * 4 : request * 4 + 4, col * 128 : (col + 1) * 128] = heads[
                    col * 4 : col * 4 + 4, :
                ]
        left = left_ref[...].astype(BF16)
        weight = weight_ref[:, group].reshape(-1, 256)
        total = total + jnp.dot(left, weight, preferred_element_type=F32)
    after = total.astype(BF16)
    first = parity_ref[0] == 0
    mine_ref[...] = jnp.where(first, after[0:16, :], after[16:32, :])
    other_ref[...] = jnp.where(first, after[16:32, :], after[0:16, :])


def pair_copies_kernel(mine_ref, other_ref, out_ref):
    for col in range(out_ref.shape[0]):
        out_ref[col, :, 0:256] = mine_ref[...]
        out_ref[col, :, 256:512] = other_ref[...]


def up_kernel(after_ref, gain_ref, other_gain_ref, weight_ref, other_weight_ref, out_ref):
    after = after_ref[...].reshape(256, 512).astype(F32)
    stat = jnp.broadcast_to(jnp.sum(after * after, axis=1, keepdims=True), (256, 128))
    stat = stat.astype(BF16)
    mine = (after[:, 0:256] * gain_ref[...]).astype(BF16)
    other = (after[:, 256:512] * other_gain_ref[...]).astype(BF16)
    for block in range(4):
        lanes = slice(block * 512, (block + 1) * 512)
        term = jnp.dot(mine, weight_ref[:, lanes], preferred_element_type=F32)
        term = term + jnp.dot(other, other_weight_ref[:, lanes], preferred_element_type=F32)
        term = term.astype(BF16)
        for part in range(16):
            out_ref[part, :, lanes] = term[part * 16 : (part + 1) * 16, :]
    for part in range(16):
        out_ref[part, :, 2048:2176] = stat[part * 16 : (part + 1) * 16, :]


def act_kernel(parts_ref, out_ref):
    stat = parts_ref[0, :, 2048:2176].astype(F32)
    for part in range(1, parts_ref.shape[0]):
        stat = stat + parts_ref[part, :, 2048:2176].astype(F32)
    scale = lax.rsqrt(stat / D + EPSILON)
    for block in range(16):
        lanes = slice(block * 128, (block + 1) * 128)
        up = parts_ref[0, :, lanes].astype(F32)
        for part in range(1, parts_ref.shape[0]):
            up = up + parts_ref[part, :, lanes].astype(F32)
        act = jnp.maximum(up * scale, 0.0)
        act = (act * act).astype(BF16)
        for part in range(out_ref.shape[0]):
            out_ref[part, :, lanes] = act


def turn(term, turn_ref):
    for col in range(16):
        for request in range(4):
            start = col * 16 + request * 4
            turn_ref[2 * request + col // 8, col % 8 * 4 : col % 8 * 4 + 4, :] = term[
                start : start + 4, :
            ]
    return turn_ref[...].astype(BF16)


def down_mine_kernel(act_ref, weight_ref, out_ref, turn_ref):
    act = act_ref[...].reshape(256, -1)
    out_ref[...] = turn(jnp.dot(act, weight_ref[...], preferred_element_type=F32), turn_ref)


def down_other_kernel(act_ref, far_ref, out_ref, turn_ref, weight_ref, done_ref):
    copies = [
        pltpu.make_async_copy(
            far_ref.at[pl.ds(part * 512, 512)], weight_ref.at[part], done_ref.at[part]
        )
        for part in range(4)
    ]
    for copy in copies:
        copy.start()
    term = jnp.zeros((256, 256), F32)
    for part in range(4):
        act = act_ref[:, :, part * 512 : (part + 1) * 512].reshape(256, 512)
        copies[part].wait()
        term = term + jnp.dot(act, weight_ref[part], preferred_element_type=F32)
    out_ref[...] = turn(term, turn_ref)


def join_kernel(parity_ref, mine_ref, other_ref, out_ref):
    parity = parity_ref[0]
    out_ref[pl.ds(parity * 8, 8)] = mine_ref[...]
    out_ref[pl.ds(8 - parity * 8, 8)] = other_ref[...]


def local(
    hidden_in,
    norm_mixer,
    mixer_in,
    bc_proj,
    dt_proj,
    dt_bias,
    a_log,
    skip_d,
    conv_x,
    conv_bc,
    x_cache,
    bc_cache,
    ssm_cache,
    slot_ids,
    parents,
    ancestors,
    norm_gated,
    out_proj,
    norm_ffn,
    ffn_up,
    ffn_down,
):
    rows = lax.axis_size("row")
    cols = lax.axis_size("col")
    row_index = lax.axis_index("row")
    col_index = lax.axis_index("col")
    place = jnp.stack([row_index // G, row_index % G]).astype(jnp.int32)
    parity = (row_index % 2).astype(jnp.int32)[None]
    swap = [(row, row ^ 1) for row in range(rows)]
    halves = [[row for row in range(rows) if row % 2 == half] for half in range(2)]
    smem = pl.BlockSpec(memory_space=pltpu.SMEM)
    vmem = pl.BlockSpec(memory_space=pltpu.VMEM)
    hbm = pl.BlockSpec(memory_space=pltpu.HBM)
    params = pltpu.CompilerParams(vmem_limit_bytes=VMEM_LIMIT)

    out_weights = lax.all_gather(out_proj, "col", axis=0, tiled=False)

    copies = call(copies_kernel, jax.ShapeDtypeStruct((cols, 32, 256), BF16), hidden_in)
    hidden = exchange(copies, "col")
    side = jnp.concatenate([bc_proj, dt_proj, jnp.zeros((256, G, 30), BF16)], axis=2)
    side = side.reshape(256, 256).T
    main = mixer_in.reshape(256, -1)

    def pair_sum(half):
        other = lax.ppermute(half(True), "row", swap)
        return (half(False).astype(F32) + other.astype(F32)).astype(BF16)

    def project_half(flip):
        return pl.pallas_call(
            functools.partial(project_kernel, flip),
            out_shape=jax.ShapeDtypeStruct((16, 80, 256), BF16),
            in_specs=[smem, vmem, vmem, vmem, vmem],
            out_specs=vmem,
            compiler_params=params,
        )(parity, hidden.reshape(512, 256), norm_mixer[None, :], main, side)

    parts = pair_sum(project_half)
    parts = exchange(parts, "row", halves)

    bc_own, local_sums = call(
        combine_kernel,
        (jax.ShapeDtypeStruct((cols, 16, 128), BF16), jax.ShapeDtypeStruct((72, 256), F32)),
        parts,
    )
    bc_own, place = lax.optimization_barrier((bc_own, place))

    def whole(array):
        shape = array.shape
        return pl.BlockSpec(shape, lambda step, place, slots: (0,) * len(shape))

    def slot_block(*shape):
        zeros = (0,) * (len(shape) - 2)
        return pl.BlockSpec(shape, lambda step, place, slots: (0, slots[place[0]]) + zeros)

    operands = [
        (x_cache, slot_block(1, 1, 3, 128)),
        (bc_cache, slot_block(1, 1, 3, 512)),
        (ssm_cache, slot_block(1, 1, 2, P_SIZE, N)),
        (conv_x, whole(conv_x)),
        (conv_bc, whole(conv_bc)),
        (dt_bias, whole(dt_bias)),
        (a_log, whole(a_log)),
        (skip_d, whole(skip_d)),
        (norm_gated, whole(norm_gated)),
        (parents, whole(parents)),
        (ancestors, pl.BlockSpec((1, 64, 64), lambda step, place, slots: (place[0], 0, 0))),
    ]
    pack, state = pl.pallas_call(
        prepare_kernel,
        grid_spec=pltpu.PrefetchScalarGridSpec(
            num_scalar_prefetch=2,
            grid=(1,),
            in_specs=[spec for _, spec in operands],
            out_specs=[
                pl.BlockSpec((PACK, 128), lambda step, place, slots: (0, 0)),
                pl.BlockSpec((2 * P_SIZE, N), lambda step, place, slots: (0, 0)),
            ],
        ),
        out_shape=[
            jax.ShapeDtypeStruct((PACK, 128), F32),
            jax.ShapeDtypeStruct((2 * P_SIZE, N), BF16),
        ],
        compiler_params=params,
    )(place, slot_ids, *[operand for operand, _ in operands])

    bc_new = exchange(bc_own, "col")
    bc_new, up_mine, down_mine, gain_mine = lax.optimization_barrier(
        (bc_new, ffn_up, ffn_down, norm_ffn[None, :])
    )
    up_other, down_other, gain_other = [
        lax.ppermute(weight, "row", swap) for weight in (up_mine, down_mine, gain_mine)
    ]
    mixed = pl.pallas_call(
        mixer_kernel,
        out_shape=jax.ShapeDtypeStruct((cols, 4, 256), BF16),
        scratch_shapes=[pltpu.VMEM((512, 64), BF16)],
        compiler_params=params,
    )(local_sums, bc_new, pack, state)

    mixed = exchange(mixed, "col")
    heads = call(scale_heads_kernel, jax.ShapeDtypeStruct((rows, cols * 4, 128), BF16), mixed)
    heads = exchange(heads, "row")
    residual = lax.dynamic_slice(
        hidden.reshape(8, 64, 256), (0, 4 * col_index, 0), (8, 4, 256)
    ).reshape(32, 256)
    half_after = jax.ShapeDtypeStruct((16, 256), BF16)
    after_mine, after_other = pl.pallas_call(
        out_kernel,
        out_shape=(half_after, half_after),
        in_specs=[smem, vmem, vmem, vmem],
        out_specs=(vmem, vmem),
        scratch_shapes=[pltpu.VMEM((32, 2048), F32)],
        compiler_params=params,
    )(parity, heads, out_weights, residual)

    after_other = lax.ppermute(after_other, "row", swap)
    after = exchange(
        call(
            pair_copies_kernel,
            jax.ShapeDtypeStruct((cols, 16, 512), BF16),
            after_mine,
            after_other,
        ),
        "col",
    )
    up_parts = call(
        up_kernel,
        jax.ShapeDtypeStruct((16, 16, 2176), BF16),
        after,
        gain_mine,
        gain_other,
        up_mine,
        up_other,
    )
    up_parts, down_other = lax.optimization_barrier((up_parts, down_other))
    up_parts = exchange(up_parts, "row", halves)
    act = call(act_kernel, jax.ShapeDtypeStruct((16, 16, 2048), BF16), up_parts)
    act = exchange(act, "row", halves)

    down_shape = jax.ShapeDtypeStruct((8, 32, 256), BF16)
    turn_shape = pltpu.VMEM((8, 32, 256), F32)
    for_other = pl.pallas_call(
        down_other_kernel,
        out_shape=down_shape,
        in_specs=[vmem, hbm],
        out_specs=vmem,
        scratch_shapes=[
            turn_shape,
            pltpu.VMEM((4, 512, 256), BF16),
            pltpu.SemaphoreType.DMA((4,)),
        ],
        compiler_params=params,
    )(act, down_other)
    from_other = lax.ppermute(for_other, "row", swap)
    for_mine = pl.pallas_call(
        down_mine_kernel,
        out_shape=down_shape,
        in_specs=[vmem, vmem],
        out_specs=vmem,
        scratch_shapes=[turn_shape],
        compiler_params=params,
    )(act, down_mine)
    down = pl.pallas_call(
        join_kernel,
        out_shape=jax.ShapeDtypeStruct((cols, 32, 256), BF16),
        in_specs=[smem, vmem, vmem],
        out_specs=vmem,
        compiler_params=params,
    )(parity, for_mine, from_other)
    ffn_out = jnp.sum(exchange(down, "col").astype(F32), axis=0)
    own = lax.dynamic_slice(
        after, (8 * (col_index % 2), 4 * (col_index // 2 % 4), 0), (8, 4, 512)
    ).reshape(32, 512)
    own_other = lax.ppermute(own[:, 256:], "row", swap)
    own_after = jnp.where(col_index // 8 == row_index % 2, own[:, :256], own_other)
    return (own_after.astype(F32) + ffn_out).astype(BF16)


def solution(mesh):
    return jax.shard_map(
        local,
        mesh=mesh,
        in_specs=(
            P("col", "row"),
            P("row"),
            P("row", None, "col", None),
            P("row", None, "col"),
            P("row", None, "col"),
            P(None, "col"),
            P(None, "col"),
            P(None, "col"),
            P(None, None, "col"),
            P(),
            P("row", None, None, "col"),
            P("row", None, None, None),
            P("row", None, "col", None, None),
            P(),
            P(),
            P(),
            P(None, "col"),
            P(None, "col", "row"),
            P("row"),
            P("row", "col"),
            P("col", "row"),
        ),
        out_specs=P("col", "row"),
        check_vma=False,
    )
```

```python
import functools

import jax
import jax.numpy as jnp
from jax import lax
from jax.experimental import pallas as pl
from jax.experimental.pallas import tpu as pltpu
from jax.sharding import PartitionSpec as P

D = 8192
H = 128
P_SIZE = 64
N = 256
G = 4

EPSILON = 1e-05
F32 = jnp.float32
BF16 = jnp.bfloat16
NT = (((1,), (1,)), ((), ()))
VMEM_LIMIT = 48 * 1024 * 1024


def exchange(parts, axis, groups=None):
    return lax.all_to_all(parts, axis, 0, 0, tiled=True, axis_index_groups=groups)


def call(kernel, out_shape, *operands):
    return pl.pallas_call(
        kernel,
        out_shape=out_shape,
        compiler_params=pltpu.CompilerParams(vmem_limit_bytes=VMEM_LIMIT),
    )(*operands)


def copies_kernel(block_ref, out_ref):
    for part in range(out_ref.shape[0]):
        out_ref[part] = block_ref[...]


def project_kernel(flip, parity_ref, hidden_ref, gain_ref, main_ref, side_ref, out_ref):
    use = parity_ref[0] if not flip else 1 - parity_ref[0]
    hidden = hidden_ref[...].astype(F32)
    normed = (hidden * gain_ref[...]).astype(BF16)
    squares = (hidden * hidden).astype(BF16)
    ones = jnp.ones((16, hidden.shape[1]), BF16)
    stat = lax.dot_general(ones, squares, NT, preferred_element_type=F32)
    for half in range(G // 2):
        group = 2 * half + use
        main = main_ref[:, pl.ds(pl.multiple_of(group * 256, 256), 256)]
        main = jnp.dot(normed, main, preferred_element_type=F32).astype(BF16)
        side = side_ref[pl.ds(pl.multiple_of(group * 64, 64), 64), :]
        side = lax.dot_general(side, normed, NT, preferred_element_type=F32)
        for request in range(8):
            part = request * (G // 2) + half
            nodes = slice(request * 64, (request + 1) * 64)
            out_ref[part, 0:64, :] = main[nodes, :]
            pieces = [side[0:16, nodes], side[16:32, nodes], side[32:48, nodes], stat[:, nodes]]
            out_ref[part, 64:80, :] = jnp.concatenate(pieces, axis=1).astype(BF16)


def column_of(row, size):
    eye = lax.broadcasted_iota(jnp.int32, (size, size), 0) == lax.broadcasted_iota(
        jnp.int32, (size, size), 1
    )
    wide = jnp.broadcast_to(row, (size, size))
    return jnp.sum(jnp.where(eye, wide, jnp.zeros_like(wide)), axis=1, keepdims=True)


def combine_kernel(parts_ref, bc_ref, local_ref):
    total = parts_ref[0].astype(F32)
    for part in range(1, parts_ref.shape[0]):
        total = total + parts_ref[part].astype(F32)
    scale = lax.rsqrt(total[64:65, 192:256] / D + EPSILON)
    bc = (total[64:80, 0:128] * jnp.concatenate([scale, scale], axis=1)).astype(BF16)
    for col in range(bc_ref.shape[0]):
        bc_ref[col] = bc
    main = total[0:64, :]
    main = jnp.concatenate(
        [main[:, 0:64], main[:, 128:192], main[:, 64:128], main[:, 192:256]], axis=1
    )
    local_ref[0:64, :] = main * column_of(scale, 64)
    step = total[64:72, 128:192] * scale
    local_ref[64:72, :] = jnp.concatenate([step] * 4, axis=1)


BASE, ANC, HOPS, SMALL, PACK = 512, 576, 640, 768, 784


def prepare_kernel(
    place_ref,
    slot_ref,
    x_hist_ref,
    bc_hist_ref,
    state_ref,
    x_taps_ref,
    bc_taps_ref,
    offset_ref,
    rate_ref,
    skip_ref,
    gain_ref,
    parents_ref,
    anc_ref,
    pack_ref,
    state_out_ref,
):
    request = place_ref[0]
    group = place_ref[1]

    def of_group(ref):
        table = ref[...]
        this = lax.broadcasted_iota(jnp.int32, table.shape, 0) == group
        return jnp.sum(jnp.where(this, table, 0.0), axis=0, keepdims=True)

    x_taps = jnp.zeros((4, 128), F32)
    bc_taps = jnp.zeros((4, 512), F32)
    for index in range(G):
        x_taps = jnp.where(group == index, x_taps_ref[:, index, :].astype(F32), x_taps)
        bc_taps = jnp.where(group == index, bc_taps_ref[:, index, :].astype(F32), bc_taps)

    lane = lax.broadcasted_iota(jnp.int32, (64, 64), 1)
    anc = anc_ref[0]
    anc_float = anc.astype(F32)
    depth_col = jnp.sum(anc, axis=1, keepdims=True) - 1
    depth_row = lax.dot_general(
        jnp.ones((8, 64), BF16), anc_float.astype(BF16), NT, preferred_element_type=F32
    )
    depth_row = depth_row[0:1, :].astype(jnp.int32) - 1
    all_parents = parents_ref[...]
    this = lax.broadcasted_iota(jnp.int32, all_parents.shape, 0) == request
    parent_row = jnp.sum(jnp.where(this, all_parents, 0), axis=0, keepdims=True)
    hop = (column_of(parent_row, 64) == lane).astype(F32)
    hops = [hop]
    for _ in range(2):
        moved = jnp.dot(
            hops[-1].astype(BF16), hop.astype(BF16), preferred_element_type=F32
        )
        hops.append(moved)
    pack_ref[HOPS : HOPS + 64, :] = jnp.concatenate(hops[0:2], axis=1)
    pack_ref[HOPS + 64 : HOPS + 128, :] = jnp.concatenate([hops[2], hops[2]], axis=1)
    pack_ref[ANC : ANC + 64, :] = jnp.concatenate([anc_float, anc_float], axis=1)

    x_hist = x_hist_ref[0, 0].astype(F32)
    x_base = jnp.zeros((64, 128), F32)
    rows = jnp.concatenate([bc_taps, bc_hist_ref[0, 0].astype(F32), jnp.zeros((9, 512), F32)], axis=0)
    square = (512, 512)
    eye = lax.broadcasted_iota(jnp.int32, square, 0) == lax.broadcasted_iota(jnp.int32, square, 1)
    turned = lax.dot_general(
        eye.astype(BF16), rows.astype(BF16), NT, preferred_element_type=F32
    )
    bc_base = jnp.zeros((512, 64), F32)
    for distance in range(1, 4):
        tap = 3 - distance
        for entry in range(3):
            use = (distance > depth_col) & (entry == tap + depth_col)
            x_base = x_base + jnp.where(
                use, x_hist[entry : entry + 1, :] * x_taps[tap : tap + 1, :], 0.0
            )
            use = (distance > depth_row) & (entry == tap + depth_row)
            share = turned[:, 4 + entry : 5 + entry] * turned[:, tap : tap + 1]
            bc_base = bc_base + jnp.where(use, share, 0.0)
    pack_ref[0:512, :] = jnp.concatenate([bc_base, turned, jnp.zeros((512, 48), F32)], axis=1)
    pack_ref[BASE : BASE + 64, :] = x_base

    first = lax.broadcasted_iota(jnp.int32, (1, 128), 1) < P_SIZE
    offset = column_of(of_group(offset_ref), 2)
    rate = column_of(-jnp.exp(of_group(rate_ref)), 2)
    skip = column_of(of_group(skip_ref), 2)
    pack_ref[SMALL : SMALL + 16, :] = jnp.concatenate(
        [
            x_taps,
            of_group(gain_ref),
            jnp.where(first, skip[0:1, :], skip[1:2, :]),
            jnp.zeros((2, 128), F32),
            jnp.broadcast_to(offset, (2, 128)),
            jnp.broadcast_to(rate, (2, 128)),
            jnp.zeros((4, 128), F32),
        ],
        axis=0,
    )
    state_out_ref[...] = state_ref[0, 0].reshape(2 * P_SIZE, N).astype(BF16)


def mixer_kernel(local_ref, bc_new_ref, pack_ref, state_ref, out_ref, bc_ref):
    for col in range(bc_new_ref.shape[0]):
        piece = bc_new_ref[col].astype(F32)
        bc_ref[col * 32 : col * 32 + 16, :] = piece[:, 0:64].astype(BF16)
        bc_ref[col * 32 + 16 : col * 32 + 32, :] = piece[:, 64:128].astype(BF16)
    hops = [
        pack_ref[HOPS : HOPS + 64, 0:64].astype(BF16),
        pack_ref[HOPS : HOPS + 64, 64:128].astype(BF16),
        pack_ref[HOPS + 64 : HOPS + 128, 0:64].astype(BF16),
    ]
    small = pack_ref[SMALL : SMALL + 16, :]

    x_new = local_ref[0:64, 0:128]
    gate = local_ref[0:64, 128:256]
    x_high = x_new.astype(BF16)
    x_low = (x_new - x_high.astype(F32)).astype(BF16)
    x_both = jnp.concatenate([x_high, x_low], axis=1)
    x_run = pack_ref[BASE : BASE + 64, :] + x_new * small[3:4, :]
    bc_run = pack_ref[0:512, 0:64] + bc_ref[...].astype(F32) * pack_ref[0:512, 67:68]
    for distance in range(1, 4):
        tap = 3 - distance
        moved = jnp.dot(hops[distance - 1], x_both, preferred_element_type=F32)
        x_run = x_run + (moved[:, 0:128] + moved[:, 128:256]) * small[tap : tap + 1, :]
        moved = lax.dot_general(bc_ref[...], hops[distance - 1], NT, preferred_element_type=F32)
        bc_run = bc_run + moved * pack_ref[0:512, 64 + tap : 65 + tap]
    x_conv = x_run * jax.nn.sigmoid(x_run)
    bc_conv = (bc_run * jax.nn.sigmoid(bc_run)).astype(BF16)

    raw = local_ref[64:66, 0:64] + small[8:10, 0:64]
    step = jnp.maximum(raw, 0.0) + jnp.log1p(jnp.exp(-jnp.abs(raw)))
    log_decay = small[10:12, 0:64] * step
    anc = pack_ref[ANC : ANC + 64, 0:64]
    cum = lax.dot_general(
        jnp.concatenate([log_decay, jnp.zeros((6, 64), F32)], axis=0),
        anc,
        NT,
        precision=lax.Precision.HIGHEST,
        preferred_element_type=F32,
    )

    square = (64, 64)
    eye = lax.broadcasted_iota(jnp.int32, square, 0) == lax.broadcasted_iota(jnp.int32, square, 1)
    c_node = lax.dot_general(
        eye.astype(BF16), bc_conv[256:512, :], NT, preferred_element_type=F32
    ).astype(BF16)
    scores = jnp.dot(c_node, bc_conv[0:256, :], preferred_element_type=F32)
    carried = lax.dot_general(c_node, state_ref[...], NT, preferred_element_type=F32)
    x_bf = x_conv.astype(BF16)
    is_anc = anc > 0.5
    inner = []
    start = []
    for head in range(2):
        cum_row = cum[head : head + 1, :]
        cum_col = column_of(cum_row, 64)
        gap = jnp.where(is_anc, cum_col - cum_row, 0.0)
        weight = jnp.where(is_anc, jnp.exp(gap), 0.0) * scores * step[head : head + 1, :]
        inner.append(jnp.dot(weight.astype(BF16), x_bf, preferred_element_type=F32))
        start.append(jnp.exp(cum_col))
    first = lax.broadcasted_iota(jnp.int32, (64, 128), 1) < P_SIZE
    mixed = (
        jnp.where(first, inner[0], inner[1])
        + jnp.where(first, start[0], start[1]) * carried
        + small[5:6, :] * x_conv
    )
    gated = mixed * (gate * jax.nn.sigmoid(gate))
    group_sq = jnp.sum(gated * gated, axis=1, keepdims=True)
    both = jnp.concatenate(
        [gated * small[4:5, :], jnp.broadcast_to(group_sq, (64, 128))], axis=1
    )
    for col in range(out_ref.shape[0]):
        out_ref[col] = both[col * 4 : col * 4 + 4, :].astype(BF16)


def scale_heads_kernel(parts_ref, out_ref):
    total = parts_ref[0, :, 128:256].astype(F32)
    for part in range(1, parts_ref.shape[0]):
        total = total + parts_ref[part, :, 128:256].astype(F32)
    scale = lax.rsqrt(total / (H // G * P_SIZE) + EPSILON)
    pieces = [parts_ref[part, :, 0:128].astype(F32) * scale for part in range(parts_ref.shape[0])]
    heads = jnp.concatenate(pieces, axis=0).astype(BF16)
    for row in range(out_ref.shape[0]):
        out_ref[row] = heads


def out_kernel(
    parity_ref, heads_ref, weight_ref, residual_ref, gain_ref, mine_ref, other_ref, left_ref
):
    total = residual_ref[...].astype(F32)
    for group in range(G):
        for request in range(8):
            heads = heads_ref[request * G + group].astype(F32)
            for col in range(16):
                left_ref[request * 4 : request * 4 + 4, col * 128 : (col + 1) * 128] = heads[
                    col * 4 : col * 4 + 4, :
                ]
        left = left_ref[...].astype(BF16)
        weight = weight_ref[:, group].reshape(-1, 256)
        total = total + jnp.dot(left, weight, preferred_element_type=F32)
    after = total.astype(BF16)
    first = parity_ref[0] == 0
    mine_ref[...] = jnp.where(first, after[0:16, :], after[16:32, :])
    other_ref[0:16, :] = jnp.where(first, after[16:32, :], after[0:16, :])
    gain = jnp.broadcast_to(gain_ref[...], (16, 256))
    high = gain.astype(BF16).astype(F32)
    top = lax.broadcasted_iota(jnp.int32, (16, 256), 0) < 8
    other_ref[16:32, :] = jnp.where(top, high, gain - high).astype(BF16)


def pair_copies_kernel(mine_ref, other_ref, out_ref, gain_ref):
    for col in range(out_ref.shape[0]):
        out_ref[col, :, 0:256] = mine_ref[...]
        out_ref[col, :, 256:512] = other_ref[0:16, :]
    terms = other_ref[16:32, :].astype(F32)
    gain_ref[...] = terms[0:1, :] + terms[8:9, :]


def up_kernel(after_ref, gain_ref, other_gain_ref, weight_ref, other_weight_ref, out_ref):
    after = after_ref[...].reshape(256, 512).astype(F32)
    stat = jnp.broadcast_to(jnp.sum(after * after, axis=1, keepdims=True), (256, 128))
    stat = stat.astype(BF16)
    mine = (after[:, 0:256] * gain_ref[...]).astype(BF16)
    other = (after[:, 256:512] * other_gain_ref[...]).astype(BF16)
    for block in range(4):
        lanes = slice(block * 512, (block + 1) * 512)
        term = jnp.dot(mine, weight_ref[:, lanes], preferred_element_type=F32)
        term = term + jnp.dot(other, other_weight_ref[:, lanes], preferred_element_type=F32)
        term = term.astype(BF16)
        for part in range(16):
            out_ref[part, :, lanes] = term[part * 16 : (part + 1) * 16, :]
    for part in range(16):
        out_ref[part, :, 2048:2176] = stat[part * 16 : (part + 1) * 16, :]


def act_kernel(parts_ref, far_ref, out_ref, near_ref, done_ref):
    copies = [
        pltpu.make_async_copy(
            far_ref.at[pl.ds(part * 512, 512)],
            near_ref.at[pl.ds(part * 512, 512)],
            done_ref.at[part],
        )
        for part in range(4)
    ]
    for copy in copies:
        copy.start()
    stat = parts_ref[0, :, 2048:2176].astype(F32)
    for part in range(1, parts_ref.shape[0]):
        stat = stat + parts_ref[part, :, 2048:2176].astype(F32)
    scale = lax.rsqrt(stat / D + EPSILON)
    for block in range(16):
        lanes = slice(block * 128, (block + 1) * 128)
        up = parts_ref[0, :, lanes].astype(F32)
        for part in range(1, parts_ref.shape[0]):
            up = up + parts_ref[part, :, lanes].astype(F32)
        act = jnp.maximum(up * scale, 0.0)
        act = (act * act).astype(BF16)
        for part in range(out_ref.shape[0]):
            out_ref[part, :, lanes] = act
    for copy in copies:
        copy.wait()


def turn(term, turn_ref):
    for col in range(16):
        for request in range(4):
            start = col * 16 + request * 4
            turn_ref[2 * request + col // 8, col % 8 * 4 : col % 8 * 4 + 4, :] = term[
                start : start + 4, :
            ]
    return turn_ref[...].astype(BF16)


def down_kernel(act_ref, weight_ref, out_ref, turn_ref):
    act = act_ref[...].reshape(256, -1)
    out_ref[...] = turn(jnp.dot(act, weight_ref[...], preferred_element_type=F32), turn_ref)


def join_kernel(parity_ref, mine_ref, other_ref, out_ref):
    parity = parity_ref[0]
    out_ref[pl.ds(parity * 8, 8)] = mine_ref[...]
    out_ref[pl.ds(8 - parity * 8, 8)] = other_ref[...]


def local(
    hidden_in,
    norm_mixer,
    mixer_in,
    bc_proj,
    dt_proj,
    dt_bias,
    a_log,
    skip_d,
    conv_x,
    conv_bc,
    x_cache,
    bc_cache,
    ssm_cache,
    slot_ids,
    parents,
    ancestors,
    norm_gated,
    out_proj,
    norm_ffn,
    ffn_up,
    ffn_down,
):
    rows = lax.axis_size("row")
    cols = lax.axis_size("col")
    row_index = lax.axis_index("row")
    col_index = lax.axis_index("col")
    place = jnp.stack([row_index // G, row_index % G]).astype(jnp.int32)
    parity = (row_index % 2).astype(jnp.int32)[None]
    swap = [(row, row ^ 1) for row in range(rows)]
    halves = [[row for row in range(rows) if row % 2 == half] for half in range(2)]
    smem = pl.BlockSpec(memory_space=pltpu.SMEM)
    vmem = pl.BlockSpec(memory_space=pltpu.VMEM)
    hbm = pl.BlockSpec(memory_space=pltpu.HBM)
    params = pltpu.CompilerParams(vmem_limit_bytes=VMEM_LIMIT)

    out_weights = lax.all_gather(out_proj, "col", axis=0, tiled=False)

    copies = call(copies_kernel, jax.ShapeDtypeStruct((cols, 32, 256), BF16), hidden_in)
    hidden = exchange(copies, "col")
    side = jnp.concatenate([bc_proj, dt_proj, jnp.zeros((256, G, 30), BF16)], axis=2)
    side = side.reshape(256, 256).T
    main = mixer_in.reshape(256, -1)

    def pair_sum(half):
        other = lax.ppermute(half(True), "row", swap)
        return (half(False).astype(F32) + other.astype(F32)).astype(BF16)

    def project_half(flip):
        return pl.pallas_call(
            functools.partial(project_kernel, flip),
            out_shape=jax.ShapeDtypeStruct((16, 80, 256), BF16),
            in_specs=[smem, vmem, vmem, vmem, vmem],
            out_specs=vmem,
            compiler_params=params,
        )(parity, hidden.reshape(512, 256), norm_mixer[None, :], main, side)

    parts = pair_sum(project_half)
    parts = exchange(parts, "row", halves)

    bc_own, local_sums = call(
        combine_kernel,
        (jax.ShapeDtypeStruct((cols, 16, 128), BF16), jax.ShapeDtypeStruct((72, 256), F32)),
        parts,
    )
    bc_own, place = lax.optimization_barrier((bc_own, place))

    def whole(array):
        shape = array.shape
        return pl.BlockSpec(shape, lambda step, place, slots: (0,) * len(shape))

    def slot_block(*shape):
        zeros = (0,) * (len(shape) - 2)
        return pl.BlockSpec(shape, lambda step, place, slots: (0, slots[place[0]]) + zeros)

    operands = [
        (x_cache, slot_block(1, 1, 3, 128)),
        (bc_cache, slot_block(1, 1, 3, 512)),
        (ssm_cache, slot_block(1, 1, 2, P_SIZE, N)),
        (conv_x, whole(conv_x)),
        (conv_bc, whole(conv_bc)),
        (dt_bias, whole(dt_bias)),
        (a_log, whole(a_log)),
        (skip_d, whole(skip_d)),
        (norm_gated, whole(norm_gated)),
        (parents, whole(parents)),
        (ancestors, pl.BlockSpec((1, 64, 64), lambda step, place, slots: (place[0], 0, 0))),
    ]
    pack, state = pl.pallas_call(
        prepare_kernel,
        grid_spec=pltpu.PrefetchScalarGridSpec(
            num_scalar_prefetch=2,
            grid=(1,),
            in_specs=[spec for _, spec in operands],
            out_specs=[
                pl.BlockSpec((PACK, 128), lambda step, place, slots: (0, 0)),
                pl.BlockSpec((2 * P_SIZE, N), lambda step, place, slots: (0, 0)),
            ],
        ),
        out_shape=[
            jax.ShapeDtypeStruct((PACK, 128), F32),
            jax.ShapeDtypeStruct((2 * P_SIZE, N), BF16),
        ],
        compiler_params=params,
    )(place, slot_ids, *[operand for operand, _ in operands])

    bc_new = exchange(bc_own, "col")
    bc_new, up_mine, down_mine = lax.optimization_barrier((bc_new, ffn_up, ffn_down))
    up_other, down_other = [
        lax.ppermute(weight, "row", swap) for weight in (up_mine, down_mine)
    ]
    mixed = pl.pallas_call(
        mixer_kernel,
        out_shape=jax.ShapeDtypeStruct((cols, 4, 256), BF16),
        scratch_shapes=[pltpu.VMEM((512, 64), BF16)],
        compiler_params=params,
    )(local_sums, bc_new, pack, state)

    mixed = exchange(mixed, "col")
    heads = call(scale_heads_kernel, jax.ShapeDtypeStruct((rows, cols * 4, 128), BF16), mixed)
    heads = exchange(heads, "row")
    residual = lax.dynamic_slice(
        hidden.reshape(8, 64, 256), (0, 4 * col_index, 0), (8, 4, 256)
    ).reshape(32, 256)
    gain_mine = norm_ffn[None, :]
    after_mine, after_other = pl.pallas_call(
        out_kernel,
        out_shape=(
            jax.ShapeDtypeStruct((16, 256), BF16),
            jax.ShapeDtypeStruct((32, 256), BF16),
        ),
        in_specs=[smem, vmem, vmem, vmem, vmem],
        out_specs=(vmem, vmem),
        scratch_shapes=[pltpu.VMEM((32, 2048), F32)],
        compiler_params=params,
    )(parity, heads, out_weights, residual, gain_mine)

    after_other = lax.ppermute(after_other, "row", swap)
    copies, gain_other = call(
        pair_copies_kernel,
        (
            jax.ShapeDtypeStruct((cols, 16, 512), BF16),
            jax.ShapeDtypeStruct((1, 256), F32),
        ),
        after_mine,
        after_other,
    )
    after = exchange(copies, "col")
    up_parts = call(
        up_kernel,
        jax.ShapeDtypeStruct((16, 16, 2176), BF16),
        after,
        gain_mine,
        gain_other,
        up_mine,
        up_other,
    )
    up_parts, down_other = lax.optimization_barrier((up_parts, down_other))
    up_parts = exchange(up_parts, "row", halves)
    act, down_other = pl.pallas_call(
        act_kernel,
        out_shape=(
            jax.ShapeDtypeStruct((16, 16, 2048), BF16),
            jax.ShapeDtypeStruct((2048, 256), BF16),
        ),
        in_specs=[vmem, hbm],
        out_specs=(vmem, vmem),
        scratch_shapes=[pltpu.SemaphoreType.DMA((4,))],
        compiler_params=params,
    )(up_parts, down_other)
    act = exchange(act, "row", halves)

    def down_half(weight):
        return pl.pallas_call(
            down_kernel,
            out_shape=jax.ShapeDtypeStruct((8, 32, 256), BF16),
            scratch_shapes=[pltpu.VMEM((8, 32, 256), F32)],
            compiler_params=params,
        )(act, weight)

    from_other = lax.ppermute(down_half(down_other), "row", swap)
    down = pl.pallas_call(
        join_kernel,
        out_shape=jax.ShapeDtypeStruct((cols, 32, 256), BF16),
        in_specs=[smem, vmem, vmem],
        out_specs=vmem,
        compiler_params=params,
    )(parity, down_half(down_mine), from_other)
    ffn_out = jnp.sum(exchange(down, "col").astype(F32), axis=0)
    own = lax.dynamic_slice(
        after, (8 * (col_index % 2), 4 * (col_index // 2 % 4), 0), (8, 4, 512)
    ).reshape(32, 512)
    own_other = lax.ppermute(own[:, 256:], "row", swap)
    own_after = jnp.where(col_index // 8 == row_index % 2, own[:, :256], own_other)
    return (own_after.astype(F32) + ffn_out).astype(BF16)


def solution(mesh):
    return jax.shard_map(
        local,
        mesh=mesh,
        in_specs=(
            P("col", "row"),
            P("row"),
            P("row", None, "col", None),
            P("row", None, "col"),
            P("row", None, "col"),
            P(None, "col"),
            P(None, "col"),
            P(None, "col"),
            P(None, None, "col"),
            P(),
            P("row", None, None, "col"),
            P("row", None, None, None),
            P("row", None, "col", None, None),
            P(),
            P(),
            P(),
            P(None, "col"),
            P(None, "col", "row"),
            P("row"),
            P("row", "col"),
            P("col", "row"),
        ),
        out_specs=P("col", "row"),
        check_vma=False,
    )
```

```python
import functools

import jax
import jax.numpy as jnp
from jax import lax
from jax.experimental import pallas as pl
from jax.experimental.pallas import tpu as pltpu
from jax.sharding import PartitionSpec as P

D = 8192
H = 128
P_SIZE = 64
N = 256
G = 4

EPSILON = 1e-05
F32 = jnp.float32
BF16 = jnp.bfloat16
NT = (((1,), (1,)), ((), ()))
VMEM_LIMIT = 48 * 1024 * 1024


def exchange(parts, axis, groups=None):
    return lax.all_to_all(parts, axis, 0, 0, tiled=True, axis_index_groups=groups)


def call(kernel, out_shape, *operands):
    return pl.pallas_call(
        kernel,
        out_shape=out_shape,
        compiler_params=pltpu.CompilerParams(vmem_limit_bytes=VMEM_LIMIT),
    )(*operands)


def copies_kernel(block_ref, out_ref):
    for part in range(out_ref.shape[0]):
        out_ref[part] = block_ref[...]


def project_kernel(flip, place_ref, hidden_ref, gain_ref, main_ref, side_ref, out_ref):
    use = place_ref[2] if not flip else 1 - place_ref[2]
    hidden = hidden_ref[...].astype(F32)
    normed = (hidden * gain_ref[...]).astype(BF16)
    squares = (hidden * hidden).astype(BF16)
    ones = jnp.ones((16, hidden.shape[1]), BF16)
    stat = lax.dot_general(ones, squares, NT, preferred_element_type=F32)
    for half in range(G // 2):
        group = 2 * half + use
        main = main_ref[:, pl.ds(pl.multiple_of(group * 256, 256), 256)]
        main = jnp.dot(normed, main, preferred_element_type=F32).astype(BF16)
        side = side_ref[pl.ds(pl.multiple_of(group * 64, 64), 64), :]
        side = lax.dot_general(side, normed, NT, preferred_element_type=F32)
        for request in range(8):
            part = request * (G // 2) + half
            nodes = slice(request * 64, (request + 1) * 64)
            out_ref[part, 0:64, :] = main[nodes, :]
            pieces = [side[0:16, nodes], side[16:32, nodes], side[32:48, nodes], stat[:, nodes]]
            out_ref[part, 64:80, :] = jnp.concatenate(pieces, axis=1).astype(BF16)


def column_of(row, size):
    eye = lax.broadcasted_iota(jnp.int32, (size, size), 0) == lax.broadcasted_iota(
        jnp.int32, (size, size), 1
    )
    wide = jnp.broadcast_to(row, (size, size))
    return jnp.sum(jnp.where(eye, wide, jnp.zeros_like(wide)), axis=1, keepdims=True)


def combine_kernel(parts_ref, bc_ref, local_ref):
    total = parts_ref[0].astype(F32)
    for part in range(1, parts_ref.shape[0]):
        total = total + parts_ref[part].astype(F32)
    scale = lax.rsqrt(total[64:65, 192:256] / D + EPSILON)
    bc = (total[64:80, 0:128] * jnp.concatenate([scale, scale], axis=1)).astype(BF16)
    for col in range(bc_ref.shape[0]):
        bc_ref[col] = bc
    main = total[0:64, :]
    main = jnp.concatenate(
        [main[:, 0:64], main[:, 128:192], main[:, 64:128], main[:, 192:256]], axis=1
    )
    local_ref[0:64, :] = main * column_of(scale, 64)
    step = total[64:72, 128:192] * scale
    local_ref[64:72, :] = jnp.concatenate([step] * 4, axis=1)


BASE, ANC, HOPS, SMALL, PACK = 512, 576, 640, 768, 784


def prepare_kernel(
    place_ref,
    slot_ref,
    x_hist_ref,
    bc_hist_ref,
    state_ref,
    x_taps_ref,
    bc_taps_ref,
    offset_ref,
    rate_ref,
    skip_ref,
    gain_ref,
    parents_ref,
    anc_ref,
    pack_ref,
    state_out_ref,
):
    request = place_ref[0]
    group = place_ref[1]

    def of_group(ref):
        table = ref[...]
        this = lax.broadcasted_iota(jnp.int32, table.shape, 0) == group
        return jnp.sum(jnp.where(this, table, 0.0), axis=0, keepdims=True)

    x_taps = jnp.zeros((4, 128), F32)
    bc_taps = jnp.zeros((4, 512), F32)
    for index in range(G):
        x_taps = jnp.where(group == index, x_taps_ref[:, index, :].astype(F32), x_taps)
        bc_taps = jnp.where(group == index, bc_taps_ref[:, index, :].astype(F32), bc_taps)

    lane = lax.broadcasted_iota(jnp.int32, (64, 64), 1)
    anc = anc_ref[0]
    anc_float = anc.astype(F32)
    depth_col = jnp.sum(anc, axis=1, keepdims=True) - 1
    depth_row = lax.dot_general(
        jnp.ones((8, 64), BF16), anc_float.astype(BF16), NT, preferred_element_type=F32
    )
    depth_row = depth_row[0:1, :].astype(jnp.int32) - 1
    all_parents = parents_ref[...]
    this = lax.broadcasted_iota(jnp.int32, all_parents.shape, 0) == request
    parent_row = jnp.sum(jnp.where(this, all_parents, 0), axis=0, keepdims=True)
    hop = (column_of(parent_row, 64) == lane).astype(F32)
    hops = [hop]
    for _ in range(2):
        moved = jnp.dot(
            hops[-1].astype(BF16), hop.astype(BF16), preferred_element_type=F32
        )
        hops.append(moved)
    pack_ref[HOPS : HOPS + 64, :] = jnp.concatenate(hops[0:2], axis=1)
    pack_ref[HOPS + 64 : HOPS + 128, :] = jnp.concatenate([hops[2], hops[2]], axis=1)
    pack_ref[ANC : ANC + 64, :] = jnp.concatenate([anc_float, anc_float], axis=1)

    x_hist = x_hist_ref[0, 0].astype(F32)
    x_base = jnp.zeros((64, 128), F32)
    rows = jnp.concatenate([bc_taps, bc_hist_ref[0, 0].astype(F32), jnp.zeros((9, 512), F32)], axis=0)
    square = (512, 512)
    eye = lax.broadcasted_iota(jnp.int32, square, 0) == lax.broadcasted_iota(jnp.int32, square, 1)
    turned = lax.dot_general(
        eye.astype(BF16), rows.astype(BF16), NT, preferred_element_type=F32
    )
    bc_base = jnp.zeros((512, 64), F32)
    for distance in range(1, 4):
        tap = 3 - distance
        for entry in range(3):
            use = (distance > depth_col) & (entry == tap + depth_col)
            x_base = x_base + jnp.where(
                use, x_hist[entry : entry + 1, :] * x_taps[tap : tap + 1, :], 0.0
            )
            use = (distance > depth_row) & (entry == tap + depth_row)
            share = turned[:, 4 + entry : 5 + entry] * turned[:, tap : tap + 1]
            bc_base = bc_base + jnp.where(use, share, 0.0)
    pack_ref[0:512, :] = jnp.concatenate([bc_base, turned, jnp.zeros((512, 48), F32)], axis=1)
    pack_ref[BASE : BASE + 64, :] = x_base

    first = lax.broadcasted_iota(jnp.int32, (1, 128), 1) < P_SIZE
    offset = column_of(of_group(offset_ref), 2)
    rate = column_of(-jnp.exp(of_group(rate_ref)), 2)
    skip = column_of(of_group(skip_ref), 2)
    pack_ref[SMALL : SMALL + 16, :] = jnp.concatenate(
        [
            x_taps,
            of_group(gain_ref),
            jnp.where(first, skip[0:1, :], skip[1:2, :]),
            jnp.zeros((2, 128), F32),
            jnp.broadcast_to(offset, (2, 128)),
            jnp.broadcast_to(rate, (2, 128)),
            jnp.zeros((4, 128), F32),
        ],
        axis=0,
    )
    state_out_ref[...] = state_ref[0, 0].reshape(2 * P_SIZE, N).astype(BF16)


def mixer_kernel(local_ref, bc_new_ref, pack_ref, state_ref, out_ref, bc_ref):
    for col in range(bc_new_ref.shape[0]):
        piece = bc_new_ref[col].astype(F32)
        bc_ref[col * 32 : col * 32 + 16, :] = piece[:, 0:64].astype(BF16)
        bc_ref[col * 32 + 16 : col * 32 + 32, :] = piece[:, 64:128].astype(BF16)
    hops = [
        pack_ref[HOPS : HOPS + 64, 0:64].astype(BF16),
        pack_ref[HOPS : HOPS + 64, 64:128].astype(BF16),
        pack_ref[HOPS + 64 : HOPS + 128, 0:64].astype(BF16),
    ]
    small = pack_ref[SMALL : SMALL + 16, :]

    x_new = local_ref[0:64, 0:128]
    gate = local_ref[0:64, 128:256]
    x_high = x_new.astype(BF16)
    x_low = (x_new - x_high.astype(F32)).astype(BF16)
    x_both = jnp.concatenate([x_high, x_low], axis=1)
    x_run = pack_ref[BASE : BASE + 64, :] + x_new * small[3:4, :]
    bc_run = pack_ref[0:512, 0:64] + bc_ref[...].astype(F32) * pack_ref[0:512, 67:68]
    for distance in range(1, 4):
        tap = 3 - distance
        moved = jnp.dot(hops[distance - 1], x_both, preferred_element_type=F32)
        x_run = x_run + (moved[:, 0:128] + moved[:, 128:256]) * small[tap : tap + 1, :]
        moved = lax.dot_general(bc_ref[...], hops[distance - 1], NT, preferred_element_type=F32)
        bc_run = bc_run + moved * pack_ref[0:512, 64 + tap : 65 + tap]
    x_conv = x_run * jax.nn.sigmoid(x_run)
    bc_conv = (bc_run * jax.nn.sigmoid(bc_run)).astype(BF16)

    raw = local_ref[64:66, 0:64] + small[8:10, 0:64]
    step = jnp.maximum(raw, 0.0) + jnp.log1p(jnp.exp(-jnp.abs(raw)))
    log_decay = small[10:12, 0:64] * step
    anc = pack_ref[ANC : ANC + 64, 0:64]
    cum = lax.dot_general(
        jnp.concatenate([log_decay, jnp.zeros((6, 64), F32)], axis=0),
        anc,
        NT,
        precision=lax.Precision.HIGHEST,
        preferred_element_type=F32,
    )

    square = (64, 64)
    eye = lax.broadcasted_iota(jnp.int32, square, 0) == lax.broadcasted_iota(jnp.int32, square, 1)
    c_node = lax.dot_general(
        eye.astype(BF16), bc_conv[256:512, :], NT, preferred_element_type=F32
    ).astype(BF16)
    scores = jnp.dot(c_node, bc_conv[0:256, :], preferred_element_type=F32)
    carried = lax.dot_general(c_node, state_ref[...], NT, preferred_element_type=F32)
    x_bf = x_conv.astype(BF16)
    is_anc = anc > 0.5
    inner = []
    start = []
    for head in range(2):
        cum_row = cum[head : head + 1, :]
        cum_col = column_of(cum_row, 64)
        gap = jnp.where(is_anc, cum_col - cum_row, 0.0)
        weight = jnp.where(is_anc, jnp.exp(gap), 0.0) * scores * step[head : head + 1, :]
        inner.append(jnp.dot(weight.astype(BF16), x_bf, preferred_element_type=F32))
        start.append(jnp.exp(cum_col))
    first = lax.broadcasted_iota(jnp.int32, (64, 128), 1) < P_SIZE
    mixed = (
        jnp.where(first, inner[0], inner[1])
        + jnp.where(first, start[0], start[1]) * carried
        + small[5:6, :] * x_conv
    )
    gated = mixed * (gate * jax.nn.sigmoid(gate))
    group_sq = jnp.sum(gated * gated, axis=1, keepdims=True)
    both = jnp.concatenate(
        [gated * small[4:5, :], jnp.broadcast_to(group_sq, (64, 128))], axis=1
    )
    for col in range(out_ref.shape[0]):
        out_ref[col] = both[col * 4 : col * 4 + 4, :].astype(BF16)


def scale_heads_kernel(parts_ref, out_ref):
    total = parts_ref[0, :, 128:256].astype(F32)
    for part in range(1, parts_ref.shape[0]):
        total = total + parts_ref[part, :, 128:256].astype(F32)
    scale = lax.rsqrt(total / (H // G * P_SIZE) + EPSILON)
    pieces = [parts_ref[part, :, 0:128].astype(F32) * scale for part in range(parts_ref.shape[0])]
    heads = jnp.concatenate(pieces, axis=0).astype(BF16)
    for row in range(out_ref.shape[0]):
        out_ref[row] = heads


def out_kernel(
    place_ref, heads_ref, weight_ref, residual_ref, gain_ref, mine_ref, other_ref, left_ref
):
    total = residual_ref[...].astype(F32)
    for group in range(G):
        for request in range(8):
            heads = heads_ref[request * G + group].astype(F32)
            for col in range(16):
                left_ref[request * 4 : request * 4 + 4, col * 128 : (col + 1) * 128] = heads[
                    col * 4 : col * 4 + 4, :
                ]
        left = left_ref[...].astype(BF16)
        weight = weight_ref[:, group].reshape(-1, 256)
        total = total + jnp.dot(left, weight, preferred_element_type=F32)
    after = total.astype(BF16)
    first = place_ref[2] == 0
    mine_ref[...] = jnp.where(first, after[0:16, :], after[16:32, :])
    other_ref[0:16, :] = jnp.where(first, after[16:32, :], after[0:16, :])
    gain = jnp.broadcast_to(gain_ref[...], (16, 256))
    high = gain.astype(BF16).astype(F32)
    top = lax.broadcasted_iota(jnp.int32, (16, 256), 0) < 8
    other_ref[16:32, :] = jnp.where(top, high, gain - high).astype(BF16)


def pair_copies_kernel(mine_ref, other_ref, out_ref, gain_ref):
    for col in range(out_ref.shape[0]):
        out_ref[col, :, 0:256] = mine_ref[...]
        out_ref[col, :, 256:512] = other_ref[0:16, :]
    terms = other_ref[16:32, :].astype(F32)
    gain_ref[...] = terms[0:1, :] + terms[8:9, :]


def up_kernel(after_ref, gain_ref, other_gain_ref, weight_ref, other_weight_ref, out_ref):
    after = after_ref[...].reshape(256, 512).astype(F32)
    stat = jnp.broadcast_to(jnp.sum(after * after, axis=1, keepdims=True), (256, 128))
    stat = stat.astype(BF16)
    mine = (after[:, 0:256] * gain_ref[...]).astype(BF16)
    other = (after[:, 256:512] * other_gain_ref[...]).astype(BF16)
    for block in range(4):
        lanes = slice(block * 512, (block + 1) * 512)
        term = jnp.dot(mine, weight_ref[:, lanes], preferred_element_type=F32)
        term = term + jnp.dot(other, other_weight_ref[:, lanes], preferred_element_type=F32)
        term = term.astype(BF16)
        for part in range(16):
            out_ref[part, :, lanes] = term[part * 16 : (part + 1) * 16, :]
    for part in range(16):
        out_ref[part, :, 2048:2176] = stat[part * 16 : (part + 1) * 16, :]


def act_kernel(parts_ref, far_ref, out_ref, near_ref, done_ref):
    copies = [
        pltpu.make_async_copy(
            far_ref.at[pl.ds(part * 512, 512)],
            near_ref.at[pl.ds(part * 512, 512)],
            done_ref.at[part],
        )
        for part in range(4)
    ]
    for copy in copies:
        copy.start()
    stat = parts_ref[0, :, 2048:2176].astype(F32)
    for part in range(1, parts_ref.shape[0]):
        stat = stat + parts_ref[part, :, 2048:2176].astype(F32)
    scale = lax.rsqrt(stat / D + EPSILON)
    for block in range(16):
        lanes = slice(block * 128, (block + 1) * 128)
        up = parts_ref[0, :, lanes].astype(F32)
        for part in range(1, parts_ref.shape[0]):
            up = up + parts_ref[part, :, lanes].astype(F32)
        act = jnp.maximum(up * scale, 0.0)
        act = (act * act).astype(BF16)
        for part in range(out_ref.shape[0]):
            out_ref[part, :, lanes] = act
    for copy in copies:
        copy.wait()


def turn(term, turn_ref):
    for col in range(16):
        for request in range(4):
            start = col * 16 + request * 4
            turn_ref[2 * request + col // 8, col % 8 * 4 : col % 8 * 4 + 4, :] = term[
                start : start + 4, :
            ]
    return turn_ref[...].astype(BF16)


def down_kernel(act_ref, weight_ref, out_ref, turn_ref):
    act = act_ref[...].reshape(256, -1)
    out_ref[...] = turn(jnp.dot(act, weight_ref[...], preferred_element_type=F32), turn_ref)


def join_kernel(place_ref, mine_ref, other_ref, out_ref):
    parity = place_ref[2]
    out_ref[pl.ds(parity * 8, 8)] = mine_ref[...]
    out_ref[pl.ds(8 - parity * 8, 8)] = other_ref[...]


def local(
    hidden_in,
    norm_mixer,
    mixer_in,
    bc_proj,
    dt_proj,
    dt_bias,
    a_log,
    skip_d,
    conv_x,
    conv_bc,
    x_cache,
    bc_cache,
    ssm_cache,
    slot_ids,
    parents,
    ancestors,
    norm_gated,
    out_proj,
    norm_ffn,
    ffn_up,
    ffn_down,
):
    rows = lax.axis_size("row")
    cols = lax.axis_size("col")
    row_index = lax.axis_index("row")
    col_index = lax.axis_index("col")
    place = jnp.stack([row_index // G, row_index % G, row_index % 2]).astype(jnp.int32)
    swap = [(row, row ^ 1) for row in range(rows)]
    halves = [[row for row in range(rows) if row % 2 == half] for half in range(2)]
    smem = pl.BlockSpec(memory_space=pltpu.SMEM)
    vmem = pl.BlockSpec(memory_space=pltpu.VMEM)
    hbm = pl.BlockSpec(memory_space=pltpu.HBM)
    params = pltpu.CompilerParams(vmem_limit_bytes=VMEM_LIMIT)

    out_weights = lax.all_gather(out_proj, "col", axis=0, tiled=False)

    copies = call(copies_kernel, jax.ShapeDtypeStruct((cols, 32, 256), BF16), hidden_in)
    hidden = exchange(copies, "col")
    side = jnp.concatenate([bc_proj, dt_proj, jnp.zeros((256, G, 30), BF16)], axis=2)
    side = side.reshape(256, 256).T
    main = mixer_in.reshape(256, -1)

    def pair_sum(half):
        other = lax.ppermute(half(True), "row", swap)
        return (half(False).astype(F32) + other.astype(F32)).astype(BF16)

    def project_half(flip):
        return pl.pallas_call(
            functools.partial(project_kernel, flip),
            out_shape=jax.ShapeDtypeStruct((16, 80, 256), BF16),
            in_specs=[smem, vmem, vmem, vmem, vmem],
            out_specs=vmem,
            compiler_params=params,
        )(place, hidden.reshape(512, 256), norm_mixer[None, :], main, side)

    parts = pair_sum(project_half)
    parts = exchange(parts, "row", halves)

    bc_own, local_sums = call(
        combine_kernel,
        (jax.ShapeDtypeStruct((cols, 16, 128), BF16), jax.ShapeDtypeStruct((72, 256), F32)),
        parts,
    )
    bc_own, place_later = lax.optimization_barrier((bc_own, place))

    def whole(array):
        shape = array.shape
        return pl.BlockSpec(shape, lambda step, place, slots: (0,) * len(shape))

    def slot_block(*shape):
        zeros = (0,) * (len(shape) - 2)
        return pl.BlockSpec(shape, lambda step, place, slots: (0, slots[place[0]]) + zeros)

    operands = [
        (x_cache, slot_block(1, 1, 3, 128)),
        (bc_cache, slot_block(1, 1, 3, 512)),
        (ssm_cache, slot_block(1, 1, 2, P_SIZE, N)),
        (conv_x, whole(conv_x)),
        (conv_bc, whole(conv_bc)),
        (dt_bias, whole(dt_bias)),
        (a_log, whole(a_log)),
        (skip_d, whole(skip_d)),
        (norm_gated, whole(norm_gated)),
        (parents, whole(parents)),
        (ancestors, pl.BlockSpec((1, 64, 64), lambda step, place, slots: (place[0], 0, 0))),
    ]
    pack, state = pl.pallas_call(
        prepare_kernel,
        grid_spec=pltpu.PrefetchScalarGridSpec(
            num_scalar_prefetch=2,
            grid=(1,),
            in_specs=[spec for _, spec in operands],
            out_specs=[
                pl.BlockSpec((PACK, 128), lambda step, place, slots: (0, 0)),
                pl.BlockSpec((2 * P_SIZE, N), lambda step, place, slots: (0, 0)),
            ],
        ),
        out_shape=[
            jax.ShapeDtypeStruct((PACK, 128), F32),
            jax.ShapeDtypeStruct((2 * P_SIZE, N), BF16),
        ],
        compiler_params=params,
    )(place_later, slot_ids, *[operand for operand, _ in operands])

    bc_new = exchange(bc_own, "col")
    bc_new, up_mine, down_mine = lax.optimization_barrier((bc_new, ffn_up, ffn_down))
    up_other, down_other = [
        lax.ppermute(weight, "row", swap) for weight in (up_mine, down_mine)
    ]
    mixed = pl.pallas_call(
        mixer_kernel,
        out_shape=jax.ShapeDtypeStruct((cols, 4, 256), BF16),
        scratch_shapes=[pltpu.VMEM((512, 64), BF16)],
        compiler_params=params,
    )(local_sums, bc_new, pack, state)

    mixed = exchange(mixed, "col")
    heads = call(scale_heads_kernel, jax.ShapeDtypeStruct((rows, cols * 4, 128), BF16), mixed)
    heads = exchange(heads, "row")
    residual = lax.dynamic_slice(
        hidden.reshape(8, 64, 256), (0, 4 * col_index, 0), (8, 4, 256)
    ).reshape(32, 256)
    gain_mine = norm_ffn[None, :]
    after_mine, after_other = pl.pallas_call(
        out_kernel,
        out_shape=(
            jax.ShapeDtypeStruct((16, 256), BF16),
            jax.ShapeDtypeStruct((32, 256), BF16),
        ),
        in_specs=[smem, vmem, vmem, vmem, vmem],
        out_specs=(vmem, vmem),
        scratch_shapes=[pltpu.VMEM((32, 2048), F32)],
        compiler_params=params,
    )(place, heads, out_weights, residual, gain_mine)

    after_other = lax.ppermute(after_other, "row", swap)
    copies, gain_other = call(
        pair_copies_kernel,
        (
            jax.ShapeDtypeStruct((cols, 16, 512), BF16),
            jax.ShapeDtypeStruct((1, 256), F32),
        ),
        after_mine,
        after_other,
    )
    after = exchange(copies, "col")
    up_parts = call(
        up_kernel,
        jax.ShapeDtypeStruct((16, 16, 2176), BF16),
        after,
        gain_mine,
        gain_other,
        up_mine,
        up_other,
    )
    up_parts, down_other = lax.optimization_barrier((up_parts, down_other))
    up_parts = exchange(up_parts, "row", halves)
    act, down_other = pl.pallas_call(
        act_kernel,
        out_shape=(
            jax.ShapeDtypeStruct((16, 16, 2048), BF16),
            jax.ShapeDtypeStruct((2048, 256), BF16),
        ),
        in_specs=[vmem, hbm],
        out_specs=(vmem, vmem),
        scratch_shapes=[pltpu.SemaphoreType.DMA((4,))],
        compiler_params=params,
    )(up_parts, down_other)
    act = exchange(act, "row", halves)

    def down_half(weight):
        return pl.pallas_call(
            down_kernel,
            out_shape=jax.ShapeDtypeStruct((8, 32, 256), BF16),
            scratch_shapes=[pltpu.VMEM((8, 32, 256), F32)],
            compiler_params=params,
        )(act, weight)

    from_other = lax.ppermute(down_half(down_other), "row", swap)
    down = pl.pallas_call(
        join_kernel,
        out_shape=jax.ShapeDtypeStruct((cols, 32, 256), BF16),
        in_specs=[smem, vmem, vmem],
        out_specs=vmem,
        compiler_params=params,
    )(place, down_half(down_mine), from_other)
    ffn_out = jnp.sum(exchange(down, "col").astype(F32), axis=0)
    own = lax.dynamic_slice(
        after, (8 * (col_index % 2), 4 * (col_index // 2 % 4), 0), (8, 4, 512)
    ).reshape(32, 512)
    own_other = lax.ppermute(own[:, 256:], "row", swap)
    own_after = jnp.where(col_index // 8 == row_index % 2, own[:, :256], own_other)
    return (own_after.astype(F32) + ffn_out).astype(BF16)


def solution(mesh):
    return jax.shard_map(
        local,
        mesh=mesh,
        in_specs=(
            P("col", "row"),
            P("row"),
            P("row", None, "col", None),
            P("row", None, "col"),
            P("row", None, "col"),
            P(None, "col"),
            P(None, "col"),
            P(None, "col"),
            P(None, None, "col"),
            P(),
            P("row", None, None, "col"),
            P("row", None, None, None),
            P("row", None, "col", None, None),
            P(),
            P(),
            P(),
            P(None, "col"),
            P(None, "col", "row"),
            P("row"),
            P("row", "col"),
            P("col", "row"),
        ),
        out_specs=P("col", "row"),
        check_vma=False,
    )
```

```python
import functools

import jax
import jax.numpy as jnp
from jax import lax
from jax.experimental import pallas as pl
from jax.experimental.pallas import tpu as pltpu
from jax.sharding import PartitionSpec as P

D = 8192
H = 128
P_SIZE = 64
N = 256
G = 4

EPSILON = 1e-05
F32 = jnp.float32
BF16 = jnp.bfloat16
NT = (((1,), (1,)), ((), ()))
VMEM_LIMIT = 48 * 1024 * 1024


def exchange(parts, axis, groups=None):
    return lax.all_to_all(parts, axis, 0, 0, tiled=True, axis_index_groups=groups)


def call(kernel, out_shape, *operands):
    return pl.pallas_call(
        kernel,
        out_shape=out_shape,
        compiler_params=pltpu.CompilerParams(vmem_limit_bytes=VMEM_LIMIT),
    )(*operands)


def copies_kernel(block_ref, out_ref):
    for part in range(out_ref.shape[0]):
        out_ref[part] = block_ref[...]


def project_kernel(flip, parity_ref, hidden_ref, gain_ref, main_ref, side_ref, out_ref):
    use = parity_ref[0] if not flip else 1 - parity_ref[0]
    hidden = hidden_ref[...].astype(F32)
    normed = (hidden * gain_ref[...]).astype(BF16)
    squares = (hidden * hidden).astype(BF16)
    ones = jnp.ones((16, hidden.shape[1]), BF16)
    stat = lax.dot_general(ones, squares, NT, preferred_element_type=F32)
    for half in range(G // 2):
        group = 2 * half + use
        main = main_ref[:, pl.ds(pl.multiple_of(group * 256, 256), 256)]
        main = jnp.dot(normed, main, preferred_element_type=F32).astype(BF16)
        side = side_ref[pl.ds(pl.multiple_of(group * 64, 64), 64), :]
        side = lax.dot_general(side, normed, NT, preferred_element_type=F32)
        for request in range(8):
            part = request * (G // 2) + half
            nodes = slice(request * 64, (request + 1) * 64)
            out_ref[part, 0:64, :] = main[nodes, :]
            pieces = [side[0:16, nodes], side[16:32, nodes], side[32:48, nodes], stat[:, nodes]]
            out_ref[part, 64:80, :] = jnp.concatenate(pieces, axis=1).astype(BF16)


def column_of(row, size):
    eye = lax.broadcasted_iota(jnp.int32, (size, size), 0) == lax.broadcasted_iota(
        jnp.int32, (size, size), 1
    )
    wide = jnp.broadcast_to(row, (size, size))
    return jnp.sum(jnp.where(eye, wide, jnp.zeros_like(wide)), axis=1, keepdims=True)


def combine_kernel(parts_ref, bc_ref, local_ref):
    total = parts_ref[0].astype(F32)
    for part in range(1, parts_ref.shape[0]):
        total = total + parts_ref[part].astype(F32)
    scale = lax.rsqrt(total[64:65, 192:256] / D + EPSILON)
    bc = (total[64:80, 0:128] * jnp.concatenate([scale, scale], axis=1)).astype(BF16)
    for col in range(bc_ref.shape[0]):
        bc_ref[col] = bc
    main = total[0:64, :]
    main = jnp.concatenate(
        [main[:, 0:64], main[:, 128:192], main[:, 64:128], main[:, 192:256]], axis=1
    )
    local_ref[0:64, :] = main * column_of(scale, 64)
    step = total[64:72, 128:192] * scale
    local_ref[64:72, :] = jnp.concatenate([step] * 4, axis=1)


BASE, ANC, HOPS, SMALL, PACK = 512, 576, 640, 768, 784


def prepare_kernel(
    request_ref,
    group_ref,
    slot_ref,
    x_hist_ref,
    bc_hist_ref,
    state_ref,
    x_taps_ref,
    bc_taps_ref,
    offset_ref,
    rate_ref,
    skip_ref,
    gain_ref,
    parents_ref,
    anc_ref,
    pack_ref,
    state_out_ref,
):
    request = request_ref[0]
    group = group_ref[0]

    def of_group(ref):
        table = ref[...]
        this = lax.broadcasted_iota(jnp.int32, table.shape, 0) == group
        return jnp.sum(jnp.where(this, table, 0.0), axis=0, keepdims=True)

    x_taps = jnp.zeros((4, 128), F32)
    bc_taps = jnp.zeros((4, 512), F32)
    for index in range(G):
        x_taps = jnp.where(group == index, x_taps_ref[:, index, :].astype(F32), x_taps)
        bc_taps = jnp.where(group == index, bc_taps_ref[:, index, :].astype(F32), bc_taps)

    lane = lax.broadcasted_iota(jnp.int32, (64, 64), 1)
    anc = anc_ref[0]
    anc_float = anc.astype(F32)
    depth_col = jnp.sum(anc, axis=1, keepdims=True) - 1
    depth_row = lax.dot_general(
        jnp.ones((8, 64), BF16), anc_float.astype(BF16), NT, preferred_element_type=F32
    )
    depth_row = depth_row[0:1, :].astype(jnp.int32) - 1
    all_parents = parents_ref[...]
    this = lax.broadcasted_iota(jnp.int32, all_parents.shape, 0) == request
    parent_row = jnp.sum(jnp.where(this, all_parents, 0), axis=0, keepdims=True)
    hop = (column_of(parent_row, 64) == lane).astype(F32)
    hops = [hop]
    for _ in range(2):
        moved = jnp.dot(
            hops[-1].astype(BF16), hop.astype(BF16), preferred_element_type=F32
        )
        hops.append(moved)
    pack_ref[HOPS : HOPS + 64, :] = jnp.concatenate(hops[0:2], axis=1)
    pack_ref[HOPS + 64 : HOPS + 128, :] = jnp.concatenate([hops[2], hops[2]], axis=1)
    pack_ref[ANC : ANC + 64, :] = jnp.concatenate([anc_float, anc_float], axis=1)

    x_hist = x_hist_ref[0, 0].astype(F32)
    x_base = jnp.zeros((64, 128), F32)
    rows = jnp.concatenate([bc_taps, bc_hist_ref[0, 0].astype(F32), jnp.zeros((9, 512), F32)], axis=0)
    square = (512, 512)
    eye = lax.broadcasted_iota(jnp.int32, square, 0) == lax.broadcasted_iota(jnp.int32, square, 1)
    turned = lax.dot_general(
        eye.astype(BF16), rows.astype(BF16), NT, preferred_element_type=F32
    )
    bc_base = jnp.zeros((512, 64), F32)
    for distance in range(1, 4):
        tap = 3 - distance
        for entry in range(3):
            use = (distance > depth_col) & (entry == tap + depth_col)
            x_base = x_base + jnp.where(
                use, x_hist[entry : entry + 1, :] * x_taps[tap : tap + 1, :], 0.0
            )
            use = (distance > depth_row) & (entry == tap + depth_row)
            share = turned[:, 4 + entry : 5 + entry] * turned[:, tap : tap + 1]
            bc_base = bc_base + jnp.where(use, share, 0.0)
    pack_ref[0:512, :] = jnp.concatenate([bc_base, turned, jnp.zeros((512, 48), F32)], axis=1)
    pack_ref[BASE : BASE + 64, :] = x_base

    first = lax.broadcasted_iota(jnp.int32, (1, 128), 1) < P_SIZE
    offset = column_of(of_group(offset_ref), 2)
    rate = column_of(-jnp.exp(of_group(rate_ref)), 2)
    skip = column_of(of_group(skip_ref), 2)
    pack_ref[SMALL : SMALL + 16, :] = jnp.concatenate(
        [
            x_taps,
            of_group(gain_ref),
            jnp.where(first, skip[0:1, :], skip[1:2, :]),
            jnp.zeros((2, 128), F32),
            jnp.broadcast_to(offset, (2, 128)),
            jnp.broadcast_to(rate, (2, 128)),
            jnp.zeros((4, 128), F32),
        ],
        axis=0,
    )
    state_out_ref[...] = state_ref[0, 0].reshape(2 * P_SIZE, N).astype(BF16)


def mixer_kernel(local_ref, bc_new_ref, pack_ref, state_ref, out_ref, bc_ref):
    for col in range(bc_new_ref.shape[0]):
        piece = bc_new_ref[col].astype(F32)
        bc_ref[col * 32 : col * 32 + 16, :] = piece[:, 0:64].astype(BF16)
        bc_ref[col * 32 + 16 : col * 32 + 32, :] = piece[:, 64:128].astype(BF16)
    hops = [
        pack_ref[HOPS : HOPS + 64, 0:64].astype(BF16),
        pack_ref[HOPS : HOPS + 64, 64:128].astype(BF16),
        pack_ref[HOPS + 64 : HOPS + 128, 0:64].astype(BF16),
    ]
    small = pack_ref[SMALL : SMALL + 16, :]

    x_new = local_ref[0:64, 0:128]
    gate = local_ref[0:64, 128:256]
    x_high = x_new.astype(BF16)
    x_low = (x_new - x_high.astype(F32)).astype(BF16)
    x_both = jnp.concatenate([x_high, x_low], axis=1)
    x_run = pack_ref[BASE : BASE + 64, :] + x_new * small[3:4, :]
    bc_run = pack_ref[0:512, 0:64] + bc_ref[...].astype(F32) * pack_ref[0:512, 67:68]
    for distance in range(1, 4):
        tap = 3 - distance
        moved = jnp.dot(hops[distance - 1], x_both, preferred_element_type=F32)
        x_run = x_run + (moved[:, 0:128] + moved[:, 128:256]) * small[tap : tap + 1, :]
        moved = lax.dot_general(bc_ref[...], hops[distance - 1], NT, preferred_element_type=F32)
        bc_run = bc_run + moved * pack_ref[0:512, 64 + tap : 65 + tap]
    x_conv = x_run * jax.nn.sigmoid(x_run)
    bc_conv = (bc_run * jax.nn.sigmoid(bc_run)).astype(BF16)

    raw = local_ref[64:66, 0:64] + small[8:10, 0:64]
    step = jnp.maximum(raw, 0.0) + jnp.log1p(jnp.exp(-jnp.abs(raw)))
    log_decay = small[10:12, 0:64] * step
    anc = pack_ref[ANC : ANC + 64, 0:64]
    cum = lax.dot_general(
        jnp.concatenate([log_decay, jnp.zeros((6, 64), F32)], axis=0),
        anc,
        NT,
        precision=lax.Precision.HIGHEST,
        preferred_element_type=F32,
    )

    square = (64, 64)
    eye = lax.broadcasted_iota(jnp.int32, square, 0) == lax.broadcasted_iota(jnp.int32, square, 1)
    c_node = lax.dot_general(
        eye.astype(BF16), bc_conv[256:512, :], NT, preferred_element_type=F32
    ).astype(BF16)
    scores = jnp.dot(c_node, bc_conv[0:256, :], preferred_element_type=F32)
    carried = lax.dot_general(c_node, state_ref[...], NT, preferred_element_type=F32)
    x_bf = x_conv.astype(BF16)
    is_anc = anc > 0.5
    inner = []
    start = []
    for head in range(2):
        cum_row = cum[head : head + 1, :]
        cum_col = column_of(cum_row, 64)
        gap = jnp.where(is_anc, cum_col - cum_row, 0.0)
        weight = jnp.where(is_anc, jnp.exp(gap), 0.0) * scores * step[head : head + 1, :]
        inner.append(jnp.dot(weight.astype(BF16), x_bf, preferred_element_type=F32))
        start.append(jnp.exp(cum_col))
    first = lax.broadcasted_iota(jnp.int32, (64, 128), 1) < P_SIZE
    mixed = (
        jnp.where(first, inner[0], inner[1])
        + jnp.where(first, start[0], start[1]) * carried
        + small[5:6, :] * x_conv
    )
    gated = mixed * (gate * jax.nn.sigmoid(gate))
    group_sq = jnp.sum(gated * gated, axis=1, keepdims=True)
    both = jnp.concatenate(
        [gated * small[4:5, :], jnp.broadcast_to(group_sq, (64, 128))], axis=1
    )
    for col in range(out_ref.shape[0]):
        out_ref[col] = both[col * 4 : col * 4 + 4, :].astype(BF16)


def scale_heads_kernel(parts_ref, out_ref):
    total = parts_ref[0, :, 128:256].astype(F32)
    for part in range(1, parts_ref.shape[0]):
        total = total + parts_ref[part, :, 128:256].astype(F32)
    scale = lax.rsqrt(total / (H // G * P_SIZE) + EPSILON)
    pieces = [parts_ref[part, :, 0:128].astype(F32) * scale for part in range(parts_ref.shape[0])]
    heads = jnp.concatenate(pieces, axis=0).astype(BF16)
    for row in range(out_ref.shape[0]):
        out_ref[row] = heads


def out_kernel(
    parity_ref, heads_ref, weight_ref, residual_ref, gain_ref, mine_ref, other_ref, left_ref
):
    total = residual_ref[...].astype(F32)
    for group in range(G):
        for request in range(8):
            heads = heads_ref[request * G + group].astype(F32)
            for col in range(16):
                left_ref[request * 4 : request * 4 + 4, col * 128 : (col + 1) * 128] = heads[
                    col * 4 : col * 4 + 4, :
                ]
        left = left_ref[...].astype(BF16)
        weight = weight_ref[:, group].reshape(-1, 256)
        total = total + jnp.dot(left, weight, preferred_element_type=F32)
    after = total.astype(BF16)
    first = parity_ref[0] == 0
    mine_ref[...] = jnp.where(first, after[0:16, :], after[16:32, :])
    other_ref[0:16, :] = jnp.where(first, after[16:32, :], after[0:16, :])
    gain = jnp.broadcast_to(gain_ref[...], (16, 256))
    high = gain.astype(BF16).astype(F32)
    top = lax.broadcasted_iota(jnp.int32, (16, 256), 0) < 8
    other_ref[16:32, :] = jnp.where(top, high, gain - high).astype(BF16)


def pair_copies_kernel(mine_ref, other_ref, out_ref, gain_ref):
    for col in range(out_ref.shape[0]):
        out_ref[col, :, 0:256] = mine_ref[...]
        out_ref[col, :, 256:512] = other_ref[0:16, :]
    terms = other_ref[16:32, :].astype(F32)
    gain_ref[...] = terms[0:1, :] + terms[8:9, :]


def up_kernel(after_ref, gain_ref, other_gain_ref, weight_ref, other_weight_ref, out_ref):
    after = after_ref[...].reshape(256, 512).astype(F32)
    stat = jnp.broadcast_to(jnp.sum(after * after, axis=1, keepdims=True), (256, 128))
    stat = stat.astype(BF16)
    mine = (after[:, 0:256] * gain_ref[...]).astype(BF16)
    other = (after[:, 256:512] * other_gain_ref[...]).astype(BF16)
    for block in range(4):
        lanes = slice(block * 512, (block + 1) * 512)
        term = jnp.dot(mine, weight_ref[:, lanes], preferred_element_type=F32)
        term = term + jnp.dot(other, other_weight_ref[:, lanes], preferred_element_type=F32)
        term = term.astype(BF16)
        for part in range(16):
            out_ref[part, :, lanes] = term[part * 16 : (part + 1) * 16, :]
    for part in range(16):
        out_ref[part, :, 2048:2176] = stat[part * 16 : (part + 1) * 16, :]


def act_kernel(parts_ref, far_ref, out_ref, near_ref, done_ref):
    copies = [
        pltpu.make_async_copy(
            far_ref.at[pl.ds(part * 512, 512)],
            near_ref.at[pl.ds(part * 512, 512)],
            done_ref.at[part],
        )
        for part in range(4)
    ]
    for copy in copies:
        copy.start()
    stat = parts_ref[0, :, 2048:2176].astype(F32)
    for part in range(1, parts_ref.shape[0]):
        stat = stat + parts_ref[part, :, 2048:2176].astype(F32)
    scale = lax.rsqrt(stat / D + EPSILON)
    for block in range(16):
        lanes = slice(block * 128, (block + 1) * 128)
        up = parts_ref[0, :, lanes].astype(F32)
        for part in range(1, parts_ref.shape[0]):
            up = up + parts_ref[part, :, lanes].astype(F32)
        act = jnp.maximum(up * scale, 0.0)
        act = (act * act).astype(BF16)
        for part in range(out_ref.shape[0]):
            out_ref[part, :, lanes] = act
    for copy in copies:
        copy.wait()


def turn(term, turn_ref):
    for col in range(16):
        for request in range(4):
            start = col * 16 + request * 4
            turn_ref[2 * request + col // 8, col % 8 * 4 : col % 8 * 4 + 4, :] = term[
                start : start + 4, :
            ]
    return turn_ref[...].astype(BF16)


def down_kernel(act_ref, weight_ref, out_ref, turn_ref):
    act = act_ref[...].reshape(256, -1)
    out_ref[...] = turn(jnp.dot(act, weight_ref[...], preferred_element_type=F32), turn_ref)


def join_kernel(parity_ref, mine_ref, other_ref, out_ref):
    parity = parity_ref[0]
    out_ref[pl.ds(parity * 8, 8)] = mine_ref[...]
    out_ref[pl.ds(8 - parity * 8, 8)] = other_ref[...]


def local(
    hidden_in,
    norm_mixer,
    mixer_in,
    bc_proj,
    dt_proj,
    dt_bias,
    a_log,
    skip_d,
    conv_x,
    conv_bc,
    x_cache,
    bc_cache,
    ssm_cache,
    slot_ids,
    parents,
    ancestors,
    norm_gated,
    out_proj,
    norm_ffn,
    ffn_up,
    ffn_down,
):
    rows = lax.axis_size("row")
    cols = lax.axis_size("col")
    row_index = lax.axis_index("row")
    col_index = lax.axis_index("col")
    request = (row_index // G).astype(jnp.int32)[None]
    group = (row_index % G).astype(jnp.int32)[None]
    parity = (row_index % 2).astype(jnp.int32)[None]
    request, group, parity = lax.optimization_barrier((request, group, parity))
    swap = [(row, row ^ 1) for row in range(rows)]
    halves = [[row for row in range(rows) if row % 2 == half] for half in range(2)]
    smem = pl.BlockSpec(memory_space=pltpu.SMEM)
    vmem = pl.BlockSpec(memory_space=pltpu.VMEM)
    hbm = pl.BlockSpec(memory_space=pltpu.HBM)
    params = pltpu.CompilerParams(vmem_limit_bytes=VMEM_LIMIT)

    out_weights = lax.all_gather(out_proj, "col", axis=0, tiled=False)

    copies = call(copies_kernel, jax.ShapeDtypeStruct((cols, 32, 256), BF16), hidden_in)
    hidden = exchange(copies, "col")
    side = jnp.concatenate([bc_proj, dt_proj, jnp.zeros((256, G, 30), BF16)], axis=2)
    side = side.reshape(256, 256).T
    main = mixer_in.reshape(256, -1)

    def pair_sum(half):
        other = lax.ppermute(half(True), "row", swap)
        return (half(False).astype(F32) + other.astype(F32)).astype(BF16)

    def project_half(flip):
        return pl.pallas_call(
            functools.partial(project_kernel, flip),
            out_shape=jax.ShapeDtypeStruct((16, 80, 256), BF16),
            in_specs=[smem, vmem, vmem, vmem, vmem],
            out_specs=vmem,
            compiler_params=params,
        )(parity, hidden.reshape(512, 256), norm_mixer[None, :], main, side)

    parts = pair_sum(project_half)
    parts = exchange(parts, "row", halves)

    bc_own, local_sums = call(
        combine_kernel,
        (jax.ShapeDtypeStruct((cols, 16, 128), BF16), jax.ShapeDtypeStruct((72, 256), F32)),
        parts,
    )
    bc_own, request = lax.optimization_barrier((bc_own, request))

    def whole(array):
        shape = array.shape
        return pl.BlockSpec(shape, lambda step, request, group, slots: (0,) * len(shape))

    def slot_block(*shape):
        zeros = (0,) * (len(shape) - 2)
        return pl.BlockSpec(
            shape, lambda step, request, group, slots: (0, slots[request[0]]) + zeros
        )

    operands = [
        (x_cache, slot_block(1, 1, 3, 128)),
        (bc_cache, slot_block(1, 1, 3, 512)),
        (ssm_cache, slot_block(1, 1, 2, P_SIZE, N)),
        (conv_x, whole(conv_x)),
        (conv_bc, whole(conv_bc)),
        (dt_bias, whole(dt_bias)),
        (a_log, whole(a_log)),
        (skip_d, whole(skip_d)),
        (norm_gated, whole(norm_gated)),
        (parents, whole(parents)),
        (
            ancestors,
            pl.BlockSpec((1, 64, 64), lambda step, request, group, slots: (request[0], 0, 0)),
        ),
    ]
    pack, state = pl.pallas_call(
        prepare_kernel,
        grid_spec=pltpu.PrefetchScalarGridSpec(
            num_scalar_prefetch=3,
            grid=(1,),
            in_specs=[spec for _, spec in operands],
            out_specs=[
                pl.BlockSpec((PACK, 128), lambda step, request, group, slots: (0, 0)),
                pl.BlockSpec((2 * P_SIZE, N), lambda step, request, group, slots: (0, 0)),
            ],
        ),
        out_shape=[
            jax.ShapeDtypeStruct((PACK, 128), F32),
            jax.ShapeDtypeStruct((2 * P_SIZE, N), BF16),
        ],
        compiler_params=params,
    )(request, group, slot_ids, *[operand for operand, _ in operands])

    bc_new = exchange(bc_own, "col")
    bc_new, up_mine, down_mine = lax.optimization_barrier((bc_new, ffn_up, ffn_down))
    up_other, down_other = [
        lax.ppermute(weight, "row", swap) for weight in (up_mine, down_mine)
    ]
    mixed = pl.pallas_call(
        mixer_kernel,
        out_shape=jax.ShapeDtypeStruct((cols, 4, 256), BF16),
        scratch_shapes=[pltpu.VMEM((512, 64), BF16)],
        compiler_params=params,
    )(local_sums, bc_new, pack, state)

    mixed = exchange(mixed, "col")
    heads = call(scale_heads_kernel, jax.ShapeDtypeStruct((rows, cols * 4, 128), BF16), mixed)
    heads = exchange(heads, "row")
    residual = lax.dynamic_slice(
        hidden.reshape(8, 64, 256), (0, 4 * col_index, 0), (8, 4, 256)
    ).reshape(32, 256)
    gain_mine = norm_ffn[None, :]
    after_mine, after_other = pl.pallas_call(
        out_kernel,
        out_shape=(
            jax.ShapeDtypeStruct((16, 256), BF16),
            jax.ShapeDtypeStruct((32, 256), BF16),
        ),
        in_specs=[smem, vmem, vmem, vmem, vmem],
        out_specs=(vmem, vmem),
        scratch_shapes=[pltpu.VMEM((32, 2048), F32)],
        compiler_params=params,
    )(parity, heads, out_weights, residual, gain_mine)

    after_other = lax.ppermute(after_other, "row", swap)
    copies, gain_other = call(
        pair_copies_kernel,
        (
            jax.ShapeDtypeStruct((cols, 16, 512), BF16),
            jax.ShapeDtypeStruct((1, 256), F32),
        ),
        after_mine,
        after_other,
    )
    after = exchange(copies, "col")
    up_parts = call(
        up_kernel,
        jax.ShapeDtypeStruct((16, 16, 2176), BF16),
        after,
        gain_mine,
        gain_other,
        up_mine,
        up_other,
    )
    up_parts, down_other = lax.optimization_barrier((up_parts, down_other))
    up_parts = exchange(up_parts, "row", halves)
    act, down_other = pl.pallas_call(
        act_kernel,
        out_shape=(
            jax.ShapeDtypeStruct((16, 16, 2048), BF16),
            jax.ShapeDtypeStruct((2048, 256), BF16),
        ),
        in_specs=[vmem, hbm],
        out_specs=(vmem, vmem),
        scratch_shapes=[pltpu.SemaphoreType.DMA((4,))],
        compiler_params=params,
    )(up_parts, down_other)
    act = exchange(act, "row", halves)

    def down_half(weight):
        return pl.pallas_call(
            down_kernel,
            out_shape=jax.ShapeDtypeStruct((8, 32, 256), BF16),
            scratch_shapes=[pltpu.VMEM((8, 32, 256), F32)],
            compiler_params=params,
        )(act, weight)

    from_other = lax.ppermute(down_half(down_other), "row", swap)
    down = pl.pallas_call(
        join_kernel,
        out_shape=jax.ShapeDtypeStruct((cols, 32, 256), BF16),
        in_specs=[smem, vmem, vmem],
        out_specs=vmem,
        compiler_params=params,
    )(parity, down_half(down_mine), from_other)
    ffn_out = jnp.sum(exchange(down, "col").astype(F32), axis=0)
    own = lax.dynamic_slice(
        after, (8 * (col_index % 2), 4 * (col_index // 2 % 4), 0), (8, 4, 512)
    ).reshape(32, 512)
    own_other = lax.ppermute(own[:, 256:], "row", swap)
    own_after = jnp.where(col_index // 8 == row_index % 2, own[:, :256], own_other)
    return (own_after.astype(F32) + ffn_out).astype(BF16)


def solution(mesh):
    return jax.shard_map(
        local,
        mesh=mesh,
        in_specs=(
            P("col", "row"),
            P("row"),
            P("row", None, "col", None),
            P("row", None, "col"),
            P("row", None, "col"),
            P(None, "col"),
            P(None, "col"),
            P(None, "col"),
            P(None, None, "col"),
            P(),
            P("row", None, None, "col"),
            P("row", None, None, None),
            P("row", None, "col", None, None),
            P(),
            P(),
            P(),
            P(None, "col"),
            P(None, "col", "row"),
            P("row"),
            P("row", "col"),
            P("col", "row"),
        ),
        out_specs=P("col", "row"),
        check_vma=False,
    )
```

```python
import functools

import jax
import jax.numpy as jnp
from jax import lax
from jax.experimental import pallas as pl
from jax.experimental.pallas import tpu as pltpu
from jax.sharding import PartitionSpec as P

D = 8192
H = 128
P_SIZE = 64
N = 256
G = 4

EPSILON = 1e-05
F32 = jnp.float32
BF16 = jnp.bfloat16
NT = (((1,), (1,)), ((), ()))
VMEM_LIMIT = 48 * 1024 * 1024


def exchange(parts, axis, groups=None):
    return lax.all_to_all(parts, axis, 0, 0, tiled=True, axis_index_groups=groups)


def call(kernel, out_shape, *operands):
    return pl.pallas_call(
        kernel,
        out_shape=out_shape,
        compiler_params=pltpu.CompilerParams(vmem_limit_bytes=VMEM_LIMIT),
    )(*operands)


def copies_kernel(block_ref, out_ref):
    for part in range(out_ref.shape[0]):
        out_ref[part] = block_ref[...]


def project_kernel(flip, parity_ref, hidden_ref, gain_ref, main_ref, side_ref, out_ref):
    use = parity_ref[0] if not flip else 1 - parity_ref[0]
    hidden = hidden_ref[...].astype(F32)
    normed = (hidden * gain_ref[...]).astype(BF16)
    squares = (hidden * hidden).astype(BF16)
    ones = jnp.ones((16, hidden.shape[1]), BF16)
    stat = lax.dot_general(ones, squares, NT, preferred_element_type=F32)
    for half in range(G // 2):
        group = 2 * half + use
        main = main_ref[:, pl.ds(pl.multiple_of(group * 256, 256), 256)]
        main = jnp.dot(normed, main, preferred_element_type=F32).astype(BF16)
        side = side_ref[pl.ds(pl.multiple_of(group * 64, 64), 64), :]
        side = lax.dot_general(side, normed, NT, preferred_element_type=F32)
        for request in range(8):
            part = request * (G // 2) + half
            nodes = slice(request * 64, (request + 1) * 64)
            out_ref[part, 0:64, :] = main[nodes, :]
            pieces = [side[0:16, nodes], side[16:32, nodes], side[32:48, nodes], stat[:, nodes]]
            out_ref[part, 64:80, :] = jnp.concatenate(pieces, axis=1).astype(BF16)


def column_of(row, size):
    eye = lax.broadcasted_iota(jnp.int32, (size, size), 0) == lax.broadcasted_iota(
        jnp.int32, (size, size), 1
    )
    wide = jnp.broadcast_to(row, (size, size))
    return jnp.sum(jnp.where(eye, wide, jnp.zeros_like(wide)), axis=1, keepdims=True)


def combine_kernel(parts_ref, bc_ref, local_ref):
    total = parts_ref[0].astype(F32)
    for part in range(1, parts_ref.shape[0]):
        total = total + parts_ref[part].astype(F32)
    scale = lax.rsqrt(total[64:65, 192:256] / D + EPSILON)
    bc = (total[64:80, 0:128] * jnp.concatenate([scale, scale], axis=1)).astype(BF16)
    for col in range(bc_ref.shape[0]):
        bc_ref[col] = bc
    main = total[0:64, :]
    main = jnp.concatenate(
        [main[:, 0:64], main[:, 128:192], main[:, 64:128], main[:, 192:256]], axis=1
    )
    local_ref[0:64, :] = main * column_of(scale, 64)
    step = total[64:72, 128:192] * scale
    local_ref[64:72, :] = jnp.concatenate([step] * 4, axis=1)


BASE, ANC, HOPS, SMALL, PACK = 512, 576, 640, 768, 784


def prepare_kernel(
    request_ref,
    group_ref,
    slot_ref,
    x_hist_ref,
    bc_hist_ref,
    state_ref,
    x_taps_ref,
    bc_taps_ref,
    offset_ref,
    rate_ref,
    skip_ref,
    gain_ref,
    parents_ref,
    anc_ref,
    pack_ref,
    state_out_ref,
):
    request = request_ref[0]
    group = group_ref[0]

    def of_group(ref):
        table = ref[...]
        this = lax.broadcasted_iota(jnp.int32, table.shape, 0) == group
        return jnp.sum(jnp.where(this, table, 0.0), axis=0, keepdims=True)

    x_taps = jnp.zeros((4, 128), F32)
    bc_taps = jnp.zeros((4, 512), F32)
    for index in range(G):
        x_taps = jnp.where(group == index, x_taps_ref[:, index, :].astype(F32), x_taps)
        bc_taps = jnp.where(group == index, bc_taps_ref[:, index, :].astype(F32), bc_taps)

    lane = lax.broadcasted_iota(jnp.int32, (64, 64), 1)
    anc = anc_ref[0]
    anc_float = anc.astype(F32)
    depth_col = jnp.sum(anc, axis=1, keepdims=True) - 1
    depth_row = lax.dot_general(
        jnp.ones((8, 64), BF16), anc_float.astype(BF16), NT, preferred_element_type=F32
    )
    depth_row = depth_row[0:1, :].astype(jnp.int32) - 1
    all_parents = parents_ref[...]
    this = lax.broadcasted_iota(jnp.int32, all_parents.shape, 0) == request
    parent_row = jnp.sum(jnp.where(this, all_parents, 0), axis=0, keepdims=True)
    hop = (column_of(parent_row, 64) == lane).astype(F32)
    hops = [hop]
    for _ in range(2):
        moved = jnp.dot(
            hops[-1].astype(BF16), hop.astype(BF16), preferred_element_type=F32
        )
        hops.append(moved)
    pack_ref[HOPS : HOPS + 64, :] = jnp.concatenate(hops[0:2], axis=1)
    pack_ref[HOPS + 64 : HOPS + 128, :] = jnp.concatenate([hops[2], hops[2]], axis=1)
    pack_ref[ANC : ANC + 64, :] = jnp.concatenate([anc_float, anc_float], axis=1)

    x_hist = x_hist_ref[0, 0].astype(F32)
    x_base = jnp.zeros((64, 128), F32)
    rows = jnp.concatenate([bc_taps, bc_hist_ref[0, 0].astype(F32), jnp.zeros((9, 512), F32)], axis=0)
    square = (512, 512)
    eye = lax.broadcasted_iota(jnp.int32, square, 0) == lax.broadcasted_iota(jnp.int32, square, 1)
    turned = lax.dot_general(
        eye.astype(BF16), rows.astype(BF16), NT, preferred_element_type=F32
    )
    bc_base = jnp.zeros((512, 64), F32)
    for distance in range(1, 4):
        tap = 3 - distance
        for entry in range(3):
            use = (distance > depth_col) & (entry == tap + depth_col)
            x_base = x_base + jnp.where(
                use, x_hist[entry : entry + 1, :] * x_taps[tap : tap + 1, :], 0.0
            )
            use = (distance > depth_row) & (entry == tap + depth_row)
            share = turned[:, 4 + entry : 5 + entry] * turned[:, tap : tap + 1]
            bc_base = bc_base + jnp.where(use, share, 0.0)
    pack_ref[0:512, :] = jnp.concatenate([bc_base, turned, jnp.zeros((512, 48), F32)], axis=1)
    pack_ref[BASE : BASE + 64, :] = x_base

    first = lax.broadcasted_iota(jnp.int32, (1, 128), 1) < P_SIZE
    offset = column_of(of_group(offset_ref), 2)
    rate = column_of(-jnp.exp(of_group(rate_ref)), 2)
    skip = column_of(of_group(skip_ref), 2)
    pack_ref[SMALL : SMALL + 16, :] = jnp.concatenate(
        [
            x_taps,
            of_group(gain_ref),
            jnp.where(first, skip[0:1, :], skip[1:2, :]),
            jnp.zeros((2, 128), F32),
            jnp.broadcast_to(offset, (2, 128)),
            jnp.broadcast_to(rate, (2, 128)),
            jnp.zeros((4, 128), F32),
        ],
        axis=0,
    )
    state_out_ref[...] = state_ref[0, 0].reshape(2 * P_SIZE, N).astype(BF16)


def mixer_kernel(local_ref, bc_new_ref, pack_ref, state_ref, out_ref, bc_ref):
    for col in range(bc_new_ref.shape[0]):
        piece = bc_new_ref[col].astype(F32)
        bc_ref[col * 32 : col * 32 + 16, :] = piece[:, 0:64].astype(BF16)
        bc_ref[col * 32 + 16 : col * 32 + 32, :] = piece[:, 64:128].astype(BF16)
    hops = [
        pack_ref[HOPS : HOPS + 64, 0:64].astype(BF16),
        pack_ref[HOPS : HOPS + 64, 64:128].astype(BF16),
        pack_ref[HOPS + 64 : HOPS + 128, 0:64].astype(BF16),
    ]
    small = pack_ref[SMALL : SMALL + 16, :]

    x_new = local_ref[0:64, 0:128]
    gate = local_ref[0:64, 128:256]
    x_high = x_new.astype(BF16)
    x_low = (x_new - x_high.astype(F32)).astype(BF16)
    x_both = jnp.concatenate([x_high, x_low], axis=1)
    x_run = pack_ref[BASE : BASE + 64, :] + x_new * small[3:4, :]
    bc_run = pack_ref[0:512, 0:64] + bc_ref[...].astype(F32) * pack_ref[0:512, 67:68]
    for distance in range(1, 4):
        tap = 3 - distance
        moved = jnp.dot(hops[distance - 1], x_both, preferred_element_type=F32)
        x_run = x_run + (moved[:, 0:128] + moved[:, 128:256]) * small[tap : tap + 1, :]
        moved = lax.dot_general(bc_ref[...], hops[distance - 1], NT, preferred_element_type=F32)
        bc_run = bc_run + moved * pack_ref[0:512, 64 + tap : 65 + tap]
    x_conv = x_run * jax.nn.sigmoid(x_run)
    bc_conv = (bc_run * jax.nn.sigmoid(bc_run)).astype(BF16)

    raw = local_ref[64:66, 0:64] + small[8:10, 0:64]
    step = jnp.maximum(raw, 0.0) + jnp.log1p(jnp.exp(-jnp.abs(raw)))
    log_decay = small[10:12, 0:64] * step
    anc = pack_ref[ANC : ANC + 64, 0:64]
    cum = lax.dot_general(
        jnp.concatenate([log_decay, jnp.zeros((6, 64), F32)], axis=0),
        anc,
        NT,
        precision=lax.Precision.HIGHEST,
        preferred_element_type=F32,
    )

    square = (64, 64)
    eye = lax.broadcasted_iota(jnp.int32, square, 0) == lax.broadcasted_iota(jnp.int32, square, 1)
    c_node = lax.dot_general(
        eye.astype(BF16), bc_conv[256:512, :], NT, preferred_element_type=F32
    ).astype(BF16)
    scores = jnp.dot(c_node, bc_conv[0:256, :], preferred_element_type=F32)
    carried = lax.dot_general(c_node, state_ref[...], NT, preferred_element_type=F32)
    x_bf = x_conv.astype(BF16)
    is_anc = anc > 0.5
    inner = []
    start = []
    for head in range(2):
        cum_row = cum[head : head + 1, :]
        cum_col = column_of(cum_row, 64)
        gap = jnp.where(is_anc, cum_col - cum_row, 0.0)
        weight = jnp.where(is_anc, jnp.exp(gap), 0.0) * scores * step[head : head + 1, :]
        inner.append(jnp.dot(weight.astype(BF16), x_bf, preferred_element_type=F32))
        start.append(jnp.exp(cum_col))
    first = lax.broadcasted_iota(jnp.int32, (64, 128), 1) < P_SIZE
    mixed = (
        jnp.where(first, inner[0], inner[1])
        + jnp.where(first, start[0], start[1]) * carried
        + small[5:6, :] * x_conv
    )
    gated = mixed * (gate * jax.nn.sigmoid(gate))
    group_sq = jnp.sum(gated * gated, axis=1, keepdims=True)
    both = jnp.concatenate(
        [gated * small[4:5, :], jnp.broadcast_to(group_sq, (64, 128))], axis=1
    )
    for col in range(out_ref.shape[0]):
        out_ref[col] = both[col * 4 : col * 4 + 4, :].astype(BF16)


def scale_heads_kernel(parts_ref, out_ref):
    total = parts_ref[0, :, 128:256].astype(F32)
    for part in range(1, parts_ref.shape[0]):
        total = total + parts_ref[part, :, 128:256].astype(F32)
    scale = lax.rsqrt(total / (H // G * P_SIZE) + EPSILON)
    pieces = [parts_ref[part, :, 0:128].astype(F32) * scale for part in range(parts_ref.shape[0])]
    heads = jnp.concatenate(pieces, axis=0).astype(BF16)
    for row in range(out_ref.shape[0]):
        out_ref[row] = heads


def out_kernel(
    parity_ref, heads_ref, weight_ref, residual_ref, gain_ref, mine_ref, other_ref, left_ref
):
    total = residual_ref[...].astype(F32)
    for group in range(G):
        for request in range(8):
            heads = heads_ref[request * G + group].astype(F32)
            for col in range(16):
                left_ref[request * 4 : request * 4 + 4, col * 128 : (col + 1) * 128] = heads[
                    col * 4 : col * 4 + 4, :
                ]
        left = left_ref[...].astype(BF16)
        weight = weight_ref[:, group].reshape(-1, 256)
        total = total + jnp.dot(left, weight, preferred_element_type=F32)
    after = total.astype(BF16)
    first = parity_ref[0] == 0
    mine_ref[...] = jnp.where(first, after[0:16, :], after[16:32, :])
    other_ref[0:16, :] = jnp.where(first, after[16:32, :], after[0:16, :])
    gain = jnp.broadcast_to(gain_ref[...], (16, 256))
    high = gain.astype(BF16).astype(F32)
    top = lax.broadcasted_iota(jnp.int32, (16, 256), 0) < 8
    other_ref[16:32, :] = jnp.where(top, high, gain - high).astype(BF16)


def pair_copies_kernel(mine_ref, other_ref, out_ref, gain_ref):
    for col in range(out_ref.shape[0]):
        out_ref[col, :, 0:256] = mine_ref[...]
        out_ref[col, :, 256:512] = other_ref[0:16, :]
    terms = other_ref[16:32, :].astype(F32)
    gain_ref[...] = terms[0:1, :] + terms[8:9, :]


def fetch(far_ref, near_ref, done_ref, half):
    copies = []
    for part in range(4):
        rows = pl.ds(half * 1024 + part * 256, 256)
        near = pl.ds(part * 256, 256)
        copies.append(
            pltpu.make_async_copy(far_ref.at[rows], near_ref.at[near], done_ref.at[part])
        )
    for copy in copies:
        copy.start()
    return copies


def up_kernel(
    after_ref,
    gain_ref,
    other_gain_ref,
    weight_ref,
    other_weight_ref,
    far_ref,
    out_ref,
    near_ref,
    done_ref,
    block_ref,
    block_done_ref,
):
    blocks = [
        pltpu.make_async_copy(
            other_weight_ref.at[:, pl.ds(block * 512, 512)],
            block_ref.at[block],
            block_done_ref.at[block],
        )
        for block in range(4)
    ]
    for copy in blocks:
        copy.start()
    copies = fetch(far_ref, near_ref, done_ref, 0)
    after = after_ref[...].reshape(256, 512).astype(F32)
    stat = jnp.broadcast_to(jnp.sum(after * after, axis=1, keepdims=True), (256, 128))
    stat = stat.astype(BF16)
    mine = (after[:, 0:256] * gain_ref[...]).astype(BF16)
    other = (after[:, 256:512] * other_gain_ref[...]).astype(BF16)
    for block in range(4):
        lanes = slice(block * 512, (block + 1) * 512)
        term = jnp.dot(mine, weight_ref[:, lanes], preferred_element_type=F32)
        blocks[block].wait()
        term = term + jnp.dot(other, block_ref[block], preferred_element_type=F32)
        term = term.astype(BF16)
        for part in range(16):
            out_ref[part, :, lanes] = term[part * 16 : (part + 1) * 16, :]
    for part in range(16):
        out_ref[part, :, 2048:2176] = stat[part * 16 : (part + 1) * 16, :]
    for copy in copies:
        copy.wait()


def act_kernel(parts_ref, far_ref, out_ref, near_ref, done_ref):
    copies = fetch(far_ref, near_ref, done_ref, 1)
    stat = parts_ref[0, :, 2048:2176].astype(F32)
    for part in range(1, parts_ref.shape[0]):
        stat = stat + parts_ref[part, :, 2048:2176].astype(F32)
    scale = lax.rsqrt(stat / D + EPSILON)
    for block in range(16):
        lanes = slice(block * 128, (block + 1) * 128)
        up = parts_ref[0, :, lanes].astype(F32)
        for part in range(1, parts_ref.shape[0]):
            up = up + parts_ref[part, :, lanes].astype(F32)
        act = jnp.maximum(up * scale, 0.0)
        act = (act * act).astype(BF16)
        for part in range(out_ref.shape[0]):
            out_ref[part, :, lanes] = act
    for copy in copies:
        copy.wait()


def turn(term, turn_ref):
    for col in range(16):
        for request in range(4):
            start = col * 16 + request * 4
            turn_ref[2 * request + col // 8, col % 8 * 4 : col % 8 * 4 + 4, :] = term[
                start : start + 4, :
            ]
    return turn_ref[...].astype(BF16)


def down_mine_kernel(act_ref, weight_ref, out_ref, turn_ref):
    act = act_ref[...].reshape(256, -1)
    out_ref[...] = turn(jnp.dot(act, weight_ref[...], preferred_element_type=F32), turn_ref)


def down_other_kernel(act_ref, upper_ref, lower_ref, out_ref, turn_ref):
    act = act_ref[...].reshape(256, -1)
    term = jnp.dot(act[:, 0:1024], upper_ref[...], preferred_element_type=F32)
    term = term + jnp.dot(act[:, 1024:2048], lower_ref[...], preferred_element_type=F32)
    out_ref[...] = turn(term, turn_ref)


def join_kernel(parity_ref, mine_ref, other_ref, out_ref):
    parity = parity_ref[0]
    out_ref[pl.ds(parity * 8, 8)] = mine_ref[...]
    out_ref[pl.ds(8 - parity * 8, 8)] = other_ref[...]


def local(
    hidden_in,
    norm_mixer,
    mixer_in,
    bc_proj,
    dt_proj,
    dt_bias,
    a_log,
    skip_d,
    conv_x,
    conv_bc,
    x_cache,
    bc_cache,
    ssm_cache,
    slot_ids,
    parents,
    ancestors,
    norm_gated,
    out_proj,
    norm_ffn,
    ffn_up,
    ffn_down,
):
    rows = lax.axis_size("row")
    cols = lax.axis_size("col")
    row_index = lax.axis_index("row")
    col_index = lax.axis_index("col")
    request = (row_index // G).astype(jnp.int32)[None]
    group = (row_index % G).astype(jnp.int32)[None]
    parity = (row_index % 2).astype(jnp.int32)[None]
    request, group, parity = lax.optimization_barrier((request, group, parity))
    swap = [(row, row ^ 1) for row in range(rows)]
    halves = [[row for row in range(rows) if row % 2 == half] for half in range(2)]
    smem = pl.BlockSpec(memory_space=pltpu.SMEM)
    vmem = pl.BlockSpec(memory_space=pltpu.VMEM)
    hbm = pl.BlockSpec(memory_space=pltpu.HBM)
    params = pltpu.CompilerParams(vmem_limit_bytes=VMEM_LIMIT)

    out_weights = lax.all_gather(out_proj, "col", axis=0, tiled=False)

    copies = call(copies_kernel, jax.ShapeDtypeStruct((cols, 32, 256), BF16), hidden_in)
    hidden = exchange(copies, "col")
    side = jnp.concatenate([bc_proj, dt_proj, jnp.zeros((256, G, 30), BF16)], axis=2)
    side = side.reshape(256, 256).T
    main = mixer_in.reshape(256, -1)

    def pair_sum(half):
        other = lax.ppermute(half(True), "row", swap)
        return (half(False).astype(F32) + other.astype(F32)).astype(BF16)

    def project_half(flip):
        return pl.pallas_call(
            functools.partial(project_kernel, flip),
            out_shape=jax.ShapeDtypeStruct((16, 80, 256), BF16),
            in_specs=[smem, vmem, vmem, vmem, vmem],
            out_specs=vmem,
            compiler_params=params,
        )(parity, hidden.reshape(512, 256), norm_mixer[None, :], main, side)

    parts = pair_sum(project_half)
    parts = exchange(parts, "row", halves)

    bc_own, local_sums = call(
        combine_kernel,
        (jax.ShapeDtypeStruct((cols, 16, 128), BF16), jax.ShapeDtypeStruct((72, 256), F32)),
        parts,
    )
    bc_own, request = lax.optimization_barrier((bc_own, request))

    def whole(array):
        shape = array.shape
        return pl.BlockSpec(shape, lambda step, request, group, slots: (0,) * len(shape))

    def slot_block(*shape):
        zeros = (0,) * (len(shape) - 2)
        return pl.BlockSpec(
            shape, lambda step, request, group, slots: (0, slots[request[0]]) + zeros
        )

    operands = [
        (x_cache, slot_block(1, 1, 3, 128)),
        (bc_cache, slot_block(1, 1, 3, 512)),
        (ssm_cache, slot_block(1, 1, 2, P_SIZE, N)),
        (conv_x, whole(conv_x)),
        (conv_bc, whole(conv_bc)),
        (dt_bias, whole(dt_bias)),
        (a_log, whole(a_log)),
        (skip_d, whole(skip_d)),
        (norm_gated, whole(norm_gated)),
        (parents, whole(parents)),
        (
            ancestors,
            pl.BlockSpec((1, 64, 64), lambda step, request, group, slots: (request[0], 0, 0)),
        ),
    ]
    pack, state = pl.pallas_call(
        prepare_kernel,
        grid_spec=pltpu.PrefetchScalarGridSpec(
            num_scalar_prefetch=3,
            grid=(1,),
            in_specs=[spec for _, spec in operands],
            out_specs=[
                pl.BlockSpec((PACK, 128), lambda step, request, group, slots: (0, 0)),
                pl.BlockSpec((2 * P_SIZE, N), lambda step, request, group, slots: (0, 0)),
            ],
        ),
        out_shape=[
            jax.ShapeDtypeStruct((PACK, 128), F32),
            jax.ShapeDtypeStruct((2 * P_SIZE, N), BF16),
        ],
        compiler_params=params,
    )(request, group, slot_ids, *[operand for operand, _ in operands])

    bc_new = exchange(bc_own, "col")
    bc_new, up_mine, down_mine = lax.optimization_barrier((bc_new, ffn_up, ffn_down))
    up_other, down_other = [
        lax.ppermute(weight, "row", swap) for weight in (up_mine, down_mine)
    ]
    mixed = pl.pallas_call(
        mixer_kernel,
        out_shape=jax.ShapeDtypeStruct((cols, 4, 256), BF16),
        scratch_shapes=[pltpu.VMEM((512, 64), BF16)],
        compiler_params=params,
    )(local_sums, bc_new, pack, state)

    mixed = exchange(mixed, "col")
    heads = call(scale_heads_kernel, jax.ShapeDtypeStruct((rows, cols * 4, 128), BF16), mixed)
    heads = exchange(heads, "row")
    residual = lax.dynamic_slice(
        hidden.reshape(8, 64, 256), (0, 4 * col_index, 0), (8, 4, 256)
    ).reshape(32, 256)
    gain_mine = norm_ffn[None, :]
    after_mine, after_other = pl.pallas_call(
        out_kernel,
        out_shape=(
            jax.ShapeDtypeStruct((16, 256), BF16),
            jax.ShapeDtypeStruct((32, 256), BF16),
        ),
        in_specs=[smem, vmem, vmem, vmem, vmem],
        out_specs=(vmem, vmem),
        scratch_shapes=[pltpu.VMEM((32, 2048), F32)],
        compiler_params=params,
    )(parity, heads, out_weights, residual, gain_mine)

    after_other = lax.ppermute(after_other, "row", swap)
    copies, gain_other = call(
        pair_copies_kernel,
        (
            jax.ShapeDtypeStruct((cols, 16, 512), BF16),
            jax.ShapeDtypeStruct((1, 256), F32),
        ),
        after_mine,
        after_other,
    )
    after = exchange(copies, "col")
    half_shape = jax.ShapeDtypeStruct((1024, 256), BF16)
    fetches = [pltpu.SemaphoreType.DMA((4,))]
    up_parts, upper = pl.pallas_call(
        up_kernel,
        out_shape=(jax.ShapeDtypeStruct((16, 16, 2176), BF16), half_shape),
        in_specs=[vmem, vmem, vmem, vmem, hbm, hbm],
        out_specs=(vmem, vmem),
        scratch_shapes=fetches
        + [pltpu.VMEM((4, 256, 512), BF16), pltpu.SemaphoreType.DMA((4,))],
        compiler_params=params,
    )(after, gain_mine, gain_other, up_mine, up_other, down_other)
    up_parts = exchange(up_parts, "row", halves)
    act, lower = pl.pallas_call(
        act_kernel,
        out_shape=(jax.ShapeDtypeStruct((16, 16, 2048), BF16), half_shape),
        in_specs=[vmem, hbm],
        out_specs=(vmem, vmem),
        scratch_shapes=fetches,
        compiler_params=params,
    )(up_parts, down_other)
    act = exchange(act, "row", halves)

    def down_half(kernel, *weights):
        return pl.pallas_call(
            kernel,
            out_shape=jax.ShapeDtypeStruct((8, 32, 256), BF16),
            scratch_shapes=[pltpu.VMEM((8, 32, 256), F32)],
            compiler_params=params,
        )(act, *weights)

    from_other = lax.ppermute(down_half(down_other_kernel, upper, lower), "row", swap)
    down = pl.pallas_call(
        join_kernel,
        out_shape=jax.ShapeDtypeStruct((cols, 32, 256), BF16),
        in_specs=[smem, vmem, vmem],
        out_specs=vmem,
        compiler_params=params,
    )(parity, down_half(down_mine_kernel, down_mine), from_other)
    ffn_out = jnp.sum(exchange(down, "col").astype(F32), axis=0)
    own = lax.dynamic_slice(
        after, (8 * (col_index % 2), 4 * (col_index // 2 % 4), 0), (8, 4, 512)
    ).reshape(32, 512)
    own_other = lax.ppermute(own[:, 256:], "row", swap)
    own_after = jnp.where(col_index // 8 == row_index % 2, own[:, :256], own_other)
    return (own_after.astype(F32) + ffn_out).astype(BF16)


def solution(mesh):
    return jax.shard_map(
        local,
        mesh=mesh,
        in_specs=(
            P("col", "row"),
            P("row"),
            P("row", None, "col", None),
            P("row", None, "col"),
            P("row", None, "col"),
            P(None, "col"),
            P(None, "col"),
            P(None, "col"),
            P(None, None, "col"),
            P(),
            P("row", None, None, "col"),
            P("row", None, None, None),
            P("row", None, "col", None, None),
            P(),
            P(),
            P(),
            P(None, "col"),
            P(None, "col", "row"),
            P("row"),
            P("row", "col"),
            P("col", "row"),
        ),
        out_specs=P("col", "row"),
        check_vma=False,
    )
```
